512 devices in a mesh: dom: 64 (over z, y), pme: 8 (over x, core).
Axes of the slice: x: 4, y: 4, z: 16, core: 2. Of those that a mesh axis runs over, the one named last changes fastest.
Arguments:
- positions: float32 [1024, 3, 128], P(('dom', 'pme')), may hold values from 0 to 256, as said below
- charges: float32 [1024, 128], P(('dom', 'pme')), may hold values from -1 to 1
- counts: int32 [1024], P(('dom', 'pme')), may hold values from 64 to 128
- mol_ids: int32 [1024, 128], P(('dom', 'pme')), may hold values from 0 to 47
- pair_blocks: int32 [24576, 2], P(('dom', 'pme')), may hold values from 0 to 1, as said below
- pair_count: int32 [512], P(('dom', 'pme')), may hold values from 1 to 48, as said below
Outputs:
- forces: float32 [1024, 3, 128], P(('dom', 'pme'))
The draws below stay inside these ranges and needn't reach their ends.
Inputs may be any that keep to these rules, and one draw needn't show every extreme that they name: `positions`: atom slots of block b lie in the region of their device e = b // 2 = d * 8 + p: first coordinate in [4 d, 4 (d + 1)), second in [32 p, 32 (p + 1)), third in [k * 128, (k + 1) * 128) with k = b mod 2. `pair_blocks`: each row holds a block number of the device (0 to 1, counted within the device) and a block number of the next device along dom, the two at most one apart. Rows past the device's pair_count are not evaluated. `pair_count`: some device has all 48 slots listed in every draw.
All inputs are finite; a program needn't handle non-finite values.
Results may differ from the reference program's by a relative error of at most 0.0003.
Values sent between devices are 32-bit elements; how exact they have to be, the bound alone decides.
A program may use at most 64 MiB of HBM per device.

```python
import math
import jax
import jax.numpy as jnp
from jax import lax

GRID = 256
GZ = 256
BLOCK_ATOMS = 128
BLK_DEV = 2
PAIRS_DEV = 48
N_BLOCKS = 1024
PAIR_ROWS = 24576
SX = 4
SY = 32
N_DOM = 64
N_PME = 8


def draw_positions(key, part):
    key = jax.random.fold_in(key, 5)
    block = jnp.arange(N_BLOCKS)
    device = block // BLK_DEV
    dom_pos = (device // N_PME).astype(jnp.float32)
    pme_pos = (device % N_PME).astype(jnp.float32)
    slot = (block % BLK_DEV).astype(jnp.float32)
    frac = jax.random.uniform(key, (N_BLOCKS, 3, BLOCK_ATOMS), jnp.float32, 0.0, 0.999)
    first = (dom_pos[:, None] + frac[:, 0]) * (GRID / N_DOM)
    second = (pme_pos[:, None] + frac[:, 1]) * (GRID / N_PME)
    third = (slot[:, None] + frac[:, 2]) * (GZ / BLK_DEV)
    return jnp.stack([first, second, third], axis=1).astype(jnp.float32)


def draw_pair_blocks(key, part):
    key = jax.random.fold_in(key, 11)
    first_key, second_key = jax.random.split(key)
    local = jax.random.randint(first_key, (PAIR_ROWS,), 0, BLK_DEV)
    step = jax.random.randint(second_key, (PAIR_ROWS,), -1, 2)
    remote = jnp.clip(local + step, 0, BLK_DEV - 1)
    return jnp.stack([local, remote], axis=1).astype(jnp.int32)


def draw_pair_count(key, part):
    key = jax.random.fold_in(key, 12)
    dense_key, pick_key, low_key = jax.random.split(key, 3)
    total = N_DOM * N_PME
    dense = jax.random.randint(dense_key, (total,), 0, 8) == 0
    chosen = jax.random.randint(pick_key, (), 0, total)
    sparse = jax.random.randint(low_key, (total,), PAIRS_DEV // 6, PAIRS_DEV // 3 + 1)
    full = jnp.logical_or(dense, jnp.arange(total) == chosen)
    return jnp.where(full, PAIRS_DEV, sparse).astype(jnp.int32)


def set_ends(values, own_key, least, top_value):
    shape = values.shape
    spot = [jax.random.randint(jax.random.fold_in(own_key, axis), (), 0, shape[axis]) for axis in range(len(shape))]
    values = values.at[tuple(spot)].set(least)
    longest = shape.index(max(shape))
    spot[longest] = (spot[longest] + 1) % shape[longest]
    return values.at[tuple(spot)].set(top_value)


def block_scale(rng, extent, cuts, low, top_value):
    loudness, own = 1.0, jax.random.fold_in(rng, 6)
    for axis_at, blocks in cuts:
        draws = jnp.exp(jax.random.uniform(jax.random.fold_in(own, axis_at), (blocks,), jnp.float32, low / len(cuts), top_value / len(cuts)))
        loudness = loudness * jnp.repeat(draws, extent[axis_at] // blocks).reshape([-1 if axis == axis_at else 1 for axis in range(len(extent))])
    return loudness


def setup_inputs(seed: int = 0) -> dict:
    splits = jax.random.split(jax.random.key(seed), 7)
    positions = draw_positions(jax.random.fold_in(splits[6], 71), 0)
    charges = jnp.clip(jax.random.uniform(splits[1], (N_BLOCKS, BLOCK_ATOMS), jnp.float32, -1.0, 1.0) * block_scale(splits[1], (N_BLOCKS, BLOCK_ATOMS), ((0, 512),), -0.4, 0.0), -1.0, 1.0)
    counts = set_ends(jax.random.randint(splits[2], (N_BLOCKS,), 64, 129), jax.random.fold_in(splits[2], 1), 64, 128).astype(jnp.int32)
    mol_ids = set_ends(jax.random.randint(splits[3], (N_BLOCKS, BLOCK_ATOMS), 0, 48), jax.random.fold_in(splits[3], 1), 0, 47).astype(jnp.int32)
    pair_blocks = draw_pair_blocks(jax.random.fold_in(splits[6], 71), 0)
    pair_count = draw_pair_count(jax.random.fold_in(splits[6], 71), 0)
    return {"positions": positions, "charges": charges, "counts": counts, "mol_ids": mol_ids, "pair_blocks": pair_blocks, "pair_count": pair_count}


coulomb = 8.0
ewald_beta = 1.0
softening = 1.0
sigma_six = 2.5 ** 6
well_depth = 0.5
core_alpha = 0.5
recip_scale = 6.0

def spline(t, order):
    total = jnp.zeros_like(t)
    for k in range(order + 1):
        total = total + (-1.0) ** k * math.comb(order, k) * jnp.maximum(t - k, 0.0) ** (order - 1)
    return jnp.where(t < order, total / math.factorial(order - 1), 0.0)

def weights(coord, index, length):
    shift = jnp.mod(coord[None, :] - index[:, None].astype(coord.dtype) + 3.0, length)
    return (spline(shift, 6), spline(shift, 5) - spline(shift - 1.0, 5))

def wrapped(index, length):
    return jnp.where(index < length // 2, index, index - length)

def influence(index_x, index_y, index_z, full_x, full_y, full_z):
    fx = wrapped(index_x, full_x).astype(jnp.float32) / full_x
    fy = wrapped(index_y, full_y).astype(jnp.float32) / full_y
    fz = wrapped(index_z, full_z).astype(jnp.float32) / full_z
    wave = fx * fx + fy * fy + fz * fz
    safe = jnp.where(wave > 0, wave, 1.0)
    return jnp.where(wave > 0, recip_scale * jnp.exp(-math.pi ** 2 * safe / ewald_beta ** 2) / safe, 0.0)

def pair_tile(left, right, grid_len, depth_len):
    parts = []
    for comp, length in ((0, grid_len), (1, grid_len), (2, depth_len)):
        delta = left[..., comp, :, None] - right[..., comp, None, :]
        parts.append(jnp.mod(delta + 0.5 * length, length) - 0.5 * length)
    dist_sq = parts[0] * parts[0] + parts[1] * parts[1] + parts[2] * parts[2]
    charge_prod = left[..., 3, :, None] * right[..., 3, None, :]
    present = left[..., 5, :, None] * right[..., 5, None, :]
    same = (left[..., 4, :, None] == right[..., 4, None, :]).astype(dist_sq.dtype)
    soft_sq = dist_sq + softening
    soft = jnp.sqrt(soft_sq)
    gauss = 2.0 * ewald_beta / math.sqrt(math.pi) * jnp.exp(-ewald_beta ** 2 * soft_sq)
    direct = coulomb * charge_prod * (jax.scipy.special.erfc(ewald_beta * soft) / soft + gauss) / soft_sq
    removed = -coulomb * charge_prod * (jax.scipy.special.erf(ewald_beta * soft) / soft - gauss) / soft_sq
    hard = core_alpha * sigma_six + dist_sq ** 3
    ratio = sigma_six / hard
    dispersion = 24.0 * well_depth * dist_sq * dist_sq * (2.0 * ratio * ratio - ratio) / hard
    scalar = present * (same * removed + (1.0 - same) * (direct + dispersion))
    on_left = jnp.stack([lax.optimization_barrier(jnp.sum(scalar * piece, axis=-1)) for piece in parts], axis=-2)
    on_right = jnp.stack([-lax.optimization_barrier(jnp.sum(scalar * piece, axis=-2)) for piece in parts], axis=-2)
    return (on_left, on_right)

def reference(positions, charges, counts, mol_ids, pair_blocks, pair_count):
    ndev = N_DOM * N_PME
    atoms = BLK_DEV * BLOCK_ATOMS
    live = (jnp.arange(BLOCK_ATOMS, dtype=jnp.int32)[None, :] < counts[:, None]).astype(jnp.float32)
    payload = jnp.concatenate([positions, (charges * live)[:, None, :], mol_ids.astype(jnp.float32)[:, None, :], live[:, None, :]], axis=1)
    blocks_idx = jnp.arange(BLK_DEV, dtype=jnp.int32)

    def short_step(total, dev):
        dom_i = dev // N_PME
        pme_i = dev % N_PME
        upper = (dom_i + 1) % N_DOM * N_PME + pme_i
        own = lax.dynamic_slice_in_dim(payload, (dev * BLK_DEV).astype(jnp.int32), BLK_DEV, 0)
        above = lax.dynamic_slice_in_dim(payload, (upper * BLK_DEV).astype(jnp.int32), BLK_DEV, 0)
        pairs = lax.dynamic_slice_in_dim(pair_blocks, (dev * PAIRS_DEV).astype(jnp.int32), PAIRS_DEV, 0)
        valid = (jnp.arange(PAIRS_DEV, dtype=jnp.int32) < pair_count[dev]).astype(jnp.float32)
        on_left, on_right = pair_tile(own[pairs[:, 0]], above[pairs[:, 1]], GRID, GZ)
        pick_left = (pairs[:, 0][:, None] == blocks_idx[None, :]).astype(jnp.float32) * valid[:, None]
        pick_right = (pairs[:, 1][:, None] == blocks_idx[None, :]).astype(jnp.float32) * valid[:, None]
        add_own = jnp.einsum('pb,pcn->bcn', pick_left, on_left, precision=lax.Precision.HIGHEST)
        add_above = jnp.einsum('pb,pcn->bcn', pick_right, on_right, precision=lax.Precision.HIGHEST)
        start_own = (dev * BLK_DEV).astype(jnp.int32)
        start_above = (upper * BLK_DEV).astype(jnp.int32)
        total = lax.dynamic_update_slice_in_dim(total, lax.dynamic_slice_in_dim(total, start_own, BLK_DEV, 0) + add_own, start_own, 0)
        total = lax.dynamic_update_slice_in_dim(total, lax.dynamic_slice_in_dim(total, start_above, BLK_DEV, 0) + add_above, start_above, 0)
        return (total, None)
    devices = jnp.arange(ndev, dtype=jnp.int32)
    short_forces, _ = lax.scan(short_step, jnp.zeros((N_BLOCKS, 3, BLOCK_ATOMS), jnp.float32), devices)

    def local_weights(own, dev):
        x_start = dev // N_PME * SX
        y_start = dev % N_PME * SY
        grid_x = jnp.mod(x_start - 3 + jnp.arange(SX + 6, dtype=jnp.int32), GRID).astype(jnp.int32)
        grid_y = jnp.mod(y_start - 3 + jnp.arange(SY + 6, dtype=jnp.int32), GRID).astype(jnp.int32)
        grid_z = jnp.arange(GZ, dtype=jnp.int32)
        wx, dwx = weights(own[:, 0, :].reshape(-1), grid_x, GRID)
        wy, dwy = weights(own[:, 1, :].reshape(-1), grid_y, GRID)
        wz, dwz = weights(own[:, 2, :].reshape(-1), grid_z, GZ)
        return (wx, dwx, wy, dwy, wz, dwz, x_start, y_start)

    def spread_step(padded, dev):
        own = lax.dynamic_slice_in_dim(payload, (dev * BLK_DEV).astype(jnp.int32), BLK_DEV, 0)
        wx, dwx, wy, dwy, wz, dwz, x_start, y_start = local_weights(own, dev)
        charge = own[:, 3, :].reshape(-1)
        plane = (wx[:, None, :] * wy[None, :, :]).reshape((SX + 6) * (SY + 6), atoms)
        local = jnp.dot(plane, (wz * charge[None, :]).T, precision=lax.Precision.HIGHEST).reshape(SX + 6, SY + 6, GZ)
        corner = (x_start.astype(jnp.int32), y_start.astype(jnp.int32), jnp.int32(0))
        current = lax.dynamic_slice(padded, corner, (SX + 6, SY + 6, GZ))
        return (lax.dynamic_update_slice(padded, current + local, corner), None)
    padded, _ = lax.scan(spread_step, jnp.zeros((GRID + 6, GRID + 6, GZ), jnp.float32), devices)
    folded = padded[3:GRID + 3]
    folded = folded.at[0:3].add(padded[GRID + 3:GRID + 6])
    folded = folded.at[GRID - 3:GRID].add(padded[0:3])
    mesh = folded[:, 3:GRID + 3]
    mesh = mesh.at[:, 0:3].add(folded[:, GRID + 3:GRID + 6])
    mesh = mesh.at[:, GRID - 3:GRID].add(folded[:, 0:3])
    index_x = jnp.arange(GRID, dtype=jnp.int32)[:, None, None]
    index_y = jnp.arange(GRID, dtype=jnp.int32)[None, :, None]
    index_z = jnp.arange(GZ, dtype=jnp.int32)[None, None, :]
    kernel = influence(index_x, index_y, index_z, GRID, GRID, GZ)
    potential = jnp.real(jnp.fft.ifftn(kernel * jnp.fft.fftn(mesh)))
    potential_pad = jnp.pad(potential, ((3, 3), (3, 3), (0, 0)), mode='wrap')

    def interp_step(dev):
        own = lax.dynamic_slice_in_dim(payload, (dev * BLK_DEV).astype(jnp.int32), BLK_DEV, 0)
        wx, dwx, wy, dwy, wz, dwz, x_start, y_start = local_weights(own, dev)
        corner = (x_start.astype(jnp.int32), y_start.astype(jnp.int32), jnp.int32(0))
        local = lax.dynamic_slice(potential_pad, corner, (SX + 6, SY + 6, GZ)).reshape((SX + 6) * (SY + 6), GZ)
        along_z = jnp.dot(local, wz, precision=lax.Precision.HIGHEST)
        slope_z = jnp.dot(local, dwz, precision=lax.Precision.HIGHEST)
        size = (SX + 6) * (SY + 6)
        field_x = lax.optimization_barrier(jnp.sum((dwx[:, None, :] * wy[None, :, :]).reshape(size, atoms) * along_z, axis=0))
        field_y = lax.optimization_barrier(jnp.sum((wx[:, None, :] * dwy[None, :, :]).reshape(size, atoms) * along_z, axis=0))
        field_z = lax.optimization_barrier(jnp.sum((wx[:, None, :] * wy[None, :, :]).reshape(size, atoms) * slope_z, axis=0))
        charge = own[:, 3, :].reshape(-1)
        result = -charge[None, :] * jnp.stack([field_x, field_y, field_z])
        return result.reshape(3, BLK_DEV, BLOCK_ATOMS).transpose(1, 0, 2)
    mesh_forces = lax.map(interp_step, devices).reshape(N_BLOCKS, 3, BLOCK_ATOMS)
    return short_forces + mesh_forces
```

```python
import functools
import math

import jax
import jax.numpy as jnp
import ml_dtypes
import numpy as np
from jax import lax
from jax.experimental import pallas as pl
from jax.experimental.pallas import tpu as pltpu
from jax.sharding import PartitionSpec as P

GRID = 256
N_DOM = 64
N_PME = 8
SX = 4
SY = 32
ROWS_Y = 40
FLAT = SX * ROWS_Y
ATOMS = 768
MESH = pl.DeviceIdType.MESH

coulomb = 8.0
sigma_six = 2.5**6
well_depth = 0.5
core_alpha = 0.5
recip_scale = 6.0
f32 = jnp.float32
bf16 = jnp.bfloat16

NN = (((1,), (0,)), ((), ()))
NT = (((1,), (1,)), ((), ()))


def split(value):
    high = value.astype(bf16)
    return high, (value - high.astype(f32)).astype(bf16)


def product(left, right, dims=NN):
    def one(a, b):
        return lax.dot_general(a, b, dims, preferred_element_type=f32)

    return one(left[0], right[0]) + (one(left[0], right[1]) + one(left[1], right[0]))


def swap_groups(pieces):
    group = lax.broadcasted_iota(jnp.int32, pieces[0].shape, 1) // 32
    out = []
    for j in range(4):
        total = pieces[j]
        for i in range(4):
            if i != j:
                total = jnp.where(group == i, pltpu.roll(pieces[i], 32 * ((i - j) % 4), 1), total)
        out.append(total)
    return out


def bumps(delta):
    away = jnp.abs(delta)
    return [jnp.maximum(top - away, 0.0) for top in (3.0, 2.0, 1.0)]


def weight(delta):
    total = 0.0
    for part, factor in zip(bumps(delta), (1.0, -6.0, 15.0)):
        square = part * part
        total = total + (factor / 120.0) * (square * square * part)
    return total


def slope(delta):
    total = 0.0
    for part, factor in zip(bumps(delta), (1.0, -6.0, 15.0)):
        square = part * part
        total = total + (factor / 24.0) * (square * square)
    return jnp.where(delta > 0.0, -total, total)


def depth_delta(coord):
    cells = lax.broadcasted_iota(jnp.int32, (GRID, 128), 0).astype(f32)
    delta = coord - cells
    delta = jnp.where(delta > 128.0, delta - 256.0, delta)
    return jnp.where(delta < -128.0, delta + 256.0, delta)


def scaled_erfc(z):
    t = 1.0 / (1.0 + 0.5 * z)
    poly = 0.17087277
    for c in (
        -0.82215223,
        1.48851587,
        -1.13520398,
        0.27886807,
        -0.18628806,
        0.09678418,
        0.37409196,
        1.00002368,
        -1.26551223,
    ):
        poly = poly * t + c
    return t * jnp.exp(poly)


def pair_scalar(parts, left, right):
    dist_sq = parts[0] * parts[0] + parts[1] * parts[1] + parts[2] * parts[2]
    soft_sq = dist_sq + 1.0
    inv = lax.rsqrt(soft_sq)
    inv_sq = inv * inv
    gauss = jnp.exp(-soft_sq)
    charge = coulomb * left[3] * right[3]
    whole = (
        charge * gauss * (scaled_erfc(soft_sq * inv) * inv + 2.0 / math.sqrt(math.pi)) * inv_sq
    )
    inv_hard = 1.0 / (core_alpha * sigma_six + dist_sq * dist_sq * dist_sq)
    ratio = sigma_six * inv_hard
    dispersion = 24.0 * well_depth * dist_sq * dist_sq * (2.0 * ratio - 1.0) * ratio * inv_hard
    other = jnp.where(left[4] == right[4], -charge * inv * inv_sq, dispersion)
    return left[5] * right[5] * (whole + other)


def kernel(
    pos,
    charges,
    counts,
    mols,
    pairs,
    listed,
    h_hi,
    h_lo,
    y_hi,
    y_lo,
    yt_hi,
    yt_lo,
    out,
    at,
    wz_hi,
    wz_lo,
    dz_hi,
    dz_lo,
    sp,
    rp,
    sd,
    rd,
    sd2,
    rd2,
    sq,
    rq,
    fs,
    fr,
    lam,
    short,
    halo_s,
    halo_r,
    p1_s,
    p1_r,
    d1_s,
    d1_r,
    d2_s,
    d2_r,
    p2_s,
    p2_r,
    f_s,
    f_r,
):
    me_d = lax.axis_index("dom")
    me_p = lax.axis_index("pme")
    up = lax.rem(me_d + 1, N_DOM)
    down = lax.rem(me_d + N_DOM - 1, N_DOM)

    barrier = pltpu.get_barrier_semaphore()

    def greet_pme(k, carry):
        pl.semaphore_signal(
            barrier, inc=1, device_id=(me_d, lax.rem(me_p + k, N_PME)), device_id_type=MESH
        )
        return carry

    def greet_dom(k, carry):
        pl.semaphore_signal(
            barrier, inc=1, device_id=(lax.rem(me_d + k, N_DOM), me_p), device_id_type=MESH
        )
        return carry

    lax.fori_loop(1, N_PME, greet_pme, 0)
    lax.fori_loop(1, N_DOM, greet_dom, 0)

    lane = lax.broadcasted_iota(jnp.int32, (1, 128), 1)
    for b in range(2):
        live = (lane < counts[b]).astype(f32)
        at[1, b, 0:3, :] = pos[b]
        at[1, b, 3:4, :] = charges[b : b + 1, :] * live
        at[1, b, 4:5, :] = mols[b : b + 1, :].astype(f32)
        at[1, b, 5:6, :] = live
        at[1, b, 6:8, :] = jnp.zeros((2, 128), f32)

    pl.semaphore_wait(barrier, N_PME - 1 + N_DOM - 1)

    to_up = pltpu.make_async_remote_copy(
        src_ref=at.at[1],
        dst_ref=at.at[0],
        send_sem=halo_s.at[0],
        recv_sem=halo_r.at[0],
        device_id=(up, me_p),
        device_id_type=MESH,
    )
    to_down = pltpu.make_async_remote_copy(
        src_ref=at.at[1],
        dst_ref=at.at[2],
        send_sem=halo_s.at[1],
        recv_sem=halo_r.at[1],
        device_id=(down, me_p),
        device_id_type=MESH,
    )
    to_up.start()
    to_down.start()

    def depth_weights(side):
        for b in range(2):
            first = (2 * side + b) * 128
            delta = depth_delta(at[side, b, 2:3, :])
            high, low = split(weight(delta) * at[side, b, 3:4, :])
            wz_hi[:, first : first + 128] = high
            wz_lo[:, first : first + 128] = low

    def depth_slopes(side):
        for b in range(2):
            first = (2 * side + b) * 128
            delta = depth_delta(at[side, b, 2:3, :])
            high, low = split(slope(delta) * at[side, b, 3:4, :])
            dz_hi[:, first : first + 128] = high
            dz_lo[:, first : first + 128] = low

    depth_weights(1)
    to_up.wait_recv()
    to_down.wait_recv()
    depth_weights(0)
    depth_weights(2)

    corner_x = (me_d * SX).astype(f32)
    corner_y = (me_p * SY).astype(f32)
    wrap = (
        jnp.where(me_d == 0, 256.0, 0.0).astype(f32),
        f32(0.0),
        jnp.where(me_d == N_DOM - 1, -256.0, 0.0).astype(f32),
    )
    flat_x = jnp.concatenate(
        [at[s, b, 0:1, :] - (wrap[s] + corner_x) for s in range(3) for b in range(2)], axis=1
    )
    flat_y = jnp.concatenate(
        [at[s, b, 1:2, :] - corner_y for s in range(3) for b in range(2)], axis=1
    )
    cells_x = lax.broadcasted_iota(jnp.int32, (8, ATOMS), 0).astype(f32)
    cells_y = lax.broadcasted_iota(jnp.int32, (ROWS_Y, ATOMS), 0).astype(f32) - 3.0
    wx = weight(flat_x - cells_x)
    wy = weight(flat_y - cells_y)

    plane = jnp.concatenate([wx[x : x + 1] * wy for x in range(SX)], axis=0)
    mesh = product(split(plane), (wz_hi[...], wz_lo[...]), NT)
    depth = product(split(mesh), (h_hi[...], h_lo[...]))
    for half in range(2):
        pieces = [
            depth[ROWS_Y * x : ROWS_Y * (x + 1), 128 * half : 128 * (half + 1)] for x in range(SX)
        ]
        for g, piece in enumerate(swap_groups(pieces)):
            sp[4 * half + g] = piece

    def pme_copy(source, target, k, send, receive):
        other = lax.rem(me_p + k, N_PME)
        return pltpu.make_async_remote_copy(
            src_ref=source.at[other],
            dst_ref=target.at[me_p],
            send_sem=send,
            recv_sem=receive,
            device_id=(me_d, other),
            device_id_type=MESH,
        )

    def pme_all(source, target, send, receive):
        return pltpu.make_async_remote_copy(
            src_ref=source.at[pl.ds(0, N_PME - 1)],
            dst_ref=target.at[pl.ds(0, N_PME - 1)],
            send_sem=send,
            recv_sem=receive,
            device_id=(me_d, lax.rem(me_p + 1, N_PME)),
            device_id_type=MESH,
        )

    def dom_copy(source, target, k, send, receive):
        other = lax.rem(me_d + k, N_DOM)
        return pltpu.make_async_remote_copy(
            src_ref=source.at[other],
            dst_ref=target.at[me_d],
            send_sem=send,
            recv_sem=receive,
            device_id=(other, me_p),
            device_id_type=MESH,
        )

    def dom_all(source, target, send, receive):
        return pltpu.make_async_remote_copy(
            src_ref=source.at[pl.ds(0, N_DOM - 1)],
            dst_ref=target.at[pl.ds(0, N_DOM - 1)],
            send_sem=send,
            recv_sem=receive,
            device_id=(up, me_p),
            device_id_type=MESH,
        )

    def start_pme(source, target, send, receive):
        def body(k, carry):
            pme_copy(source, target, k, send, receive).start()
            return carry

        lax.fori_loop(1, N_PME, body, 0)

    def start_dom(source, target, send, receive):
        def body(k, carry):
            dom_copy(source, target, k, send, receive).start()
            dom_copy(source, target, N_DOM - k, send, receive).start()
            return carry

        lax.fori_loop(1, N_DOM // 2, body, 0)
        dom_copy(source, target, N_DOM // 2, send, receive).start()

    start_pme(sp, rp, p1_s, p1_r)
    rp[me_p] = sp[me_p]

    for side in range(3):
        depth_slopes(side)

    pme_all(sp, rp, p1_s, p1_r).wait_recv()
    lines = product(
        (y_hi[...], y_lo[...]), split(rp[...].reshape(N_PME * ROWS_Y, 128))
    )
    flat_sd = sd.reshape(GRID, 128)
    for x, piece in enumerate(swap_groups([lines[64 * k : 64 * (k + 1)] for k in range(4)])):
        flat_sd[pl.ds(x, 64, stride=4), :] = piece
    start_dom(sd, rd, d1_s, d1_r)
    rd[me_d] = sd[me_d]

    def folded(index):
        return jnp.where(index < GRID // 2, index, index - GRID).astype(f32) * (1.0 / GRID)

    lanes = lax.broadcasted_iota(jnp.int32, (GRID, 128), 1)
    freq_x = folded(lax.broadcasted_iota(jnp.int32, (GRID, 128), 0))
    freq_y = folded(me_d * 4 + lanes // 32)
    freq_z = folded(me_p * 32 + lanes % 32)
    wave = freq_x * freq_x + freq_y * freq_y + freq_z * freq_z
    safe = jnp.where(wave > 0.0, wave, 1.0)
    lam[...] = jnp.where(
        wave > 0.0, (recip_scale / GRID**3) * jnp.exp(-(math.pi**2) * safe) / safe, 0.0
    )

    padded = jnp.concatenate([at[1, 0], at[1, 1], jnp.zeros((112, 128), f32)], axis=0)
    columns = padded.T
    rows = lax.broadcasted_iota(jnp.int32, (48, 1), 0)
    sublane = lax.broadcasted_iota(jnp.int32, (128, 128), 1)
    on_own = jnp.zeros((128, 128), f32)
    on_above = [[0.0] * 3, [0.0] * 3]
    for a in range(2):
        left = [columns[:, 8 * a + r : 8 * a + r + 1] for r in range(6)]
        on_left = [0.0] * 3
        for c in range(2):
            right = [at[2, c, r : r + 1, :] for r in range(6)]
            hit = (rows < listed[0]) & (pairs[:, 0:1] == a) & (pairs[:, 1:2] == c)
            times = jnp.sum(hit.astype(f32), axis=0, keepdims=True)
            dz = left[2] - right[2]
            if a < c:
                dz = jnp.where(dz < -128.0, dz + 256.0, dz)
            if a > c:
                dz = jnp.where(dz >= 128.0, dz - 256.0, dz)
            parts = [left[0] - (right[0] - wrap[2]), left[1] - right[1], dz]
            scalar = pair_scalar(parts, left, right) * times
            for v in range(3):
                force = scalar * parts[v]
                on_left[v] = on_left[v] + force
                on_above[c][v] = on_above[c][v] - jnp.sum(force, axis=0, keepdims=True)
        for v in range(3):
            on_own = jnp.where(
                sublane == 3 * a + v, jnp.sum(on_left[v], axis=1, keepdims=True), on_own
            )
    short[0] = on_own.T[0:8]
    short[1] = jnp.concatenate(on_above[0] + on_above[1] + [jnp.zeros((2, 128), f32)], axis=0)

    dom_all(sd, rd, d1_s, d1_r).wait_recv()
    table = (h_hi[...], h_lo[...])
    spectrum = product(table, split(rd.reshape(GRID, 128)[...])) * lam[...]
    sd2.reshape(GRID, 128)[...] = product(table, split(spectrum))
    start_dom(sd2, rd2, d2_s, d2_r)
    rd2[me_d] = sd2[me_d]

    dom_all(sd2, rd2, d2_s, d2_r).wait_recv()
    flat_rd2 = rd2.reshape(GRID, 128)
    lines = jnp.concatenate(
        swap_groups([flat_rd2[pl.ds(x, 64, stride=4), :] for x in range(4)]), axis=0
    )
    sq[...] = product((yt_hi[...], yt_lo[...]), split(lines)).reshape(N_PME, ROWS_Y, 128)
    start_pme(sq, rq, p2_s, p2_r)
    rq[me_p] = sq[me_p]

    dx = slope(flat_x - cells_x)
    dy = slope(flat_y - cells_y)

    pme_all(sq, rq, p2_s, p2_r).wait_recv()
    halves = [swap_groups([rq[4 * half + g] for g in range(4)]) for half in range(2)]
    depth = jnp.concatenate(
        [jnp.concatenate([halves[0][x], halves[1][x]], axis=1) for x in range(SX)], axis=0
    )
    potential = split(product(split(depth), table))
    along = product(potential, (wz_hi[...], wz_lo[...]))
    along_slope = product(potential, (dz_hi[...], dz_lo[...]))
    field = [0.0] * 3
    for x in range(SX):
        here = along[ROWS_Y * x : ROWS_Y * (x + 1)]
        there = along_slope[ROWS_Y * x : ROWS_Y * (x + 1)]
        field[0] = field[0] - dx[x : x + 1] * jnp.sum(wy * here, axis=0, keepdims=True)
        field[1] = field[1] - wx[x : x + 1] * jnp.sum(dy * here, axis=0, keepdims=True)
        field[2] = field[2] - wx[x : x + 1] * jnp.sum(wy * there, axis=0, keepdims=True)

    def force_rows(side):
        return jnp.concatenate(
            [
                field[v][:, 128 * (2 * side + b) : 128 * (2 * side + b + 1)]
                for b in range(2)
                for v in range(3)
            ]
            + [jnp.zeros((2, 128), f32)],
            axis=0,
        )

    fs[0] = force_rows(0)
    fs[1] = force_rows(2) + short[1]
    send_down = pltpu.make_async_remote_copy(
        src_ref=fs.at[0],
        dst_ref=fr.at[0],
        send_sem=f_s.at[0],
        recv_sem=f_r.at[0],
        device_id=(down, me_p),
        device_id_type=MESH,
    )
    send_up = pltpu.make_async_remote_copy(
        src_ref=fs.at[1],
        dst_ref=fr.at[1],
        send_sem=f_s.at[1],
        recv_sem=f_r.at[1],
        device_id=(up, me_p),
        device_id_type=MESH,
    )
    send_down.start()
    send_up.start()
    total = force_rows(1) + short[0]

    to_up.wait_send()
    to_down.wait_send()
    pme_all(sp, rp, p1_s, p1_r).wait_send()
    dom_all(sd, rd, d1_s, d1_r).wait_send()
    dom_all(sd2, rd2, d2_s, d2_r).wait_send()
    pme_all(sq, rq, p2_s, p2_r).wait_send()
    send_down.wait_recv()
    send_up.wait_recv()
    total = total + fr[0] + fr[1]
    out[0] = total[0:3]
    out[1] = total[3:6]
    send_down.wait_send()
    send_up.wait_send()


def two_parts(table):
    high = table.astype(ml_dtypes.bfloat16)
    low = (table - high.astype(np.float64)).astype(ml_dtypes.bfloat16)
    return high, low


def cas(first, second):
    angle = 2.0 * np.pi / GRID * (np.outer(first, second) % GRID)
    return np.cos(angle) + np.sin(angle)


def tables():
    index = np.arange(GRID)
    square = cas(index, index)
    freq = (4 * np.arange(64)[None, :] + np.arange(4)[:, None]).reshape(-1)
    cell = np.arange(ROWS_Y) - 3
    cells = (SY * np.arange(N_PME)[:, None] + cell[None, :]).reshape(-1)
    real = np.tile(np.arange(ROWS_Y) < SY + 6, N_PME)
    lines = cas(freq, cells % GRID) * real[None, :]
    return [*two_parts(square), *two_parts(lines), *two_parts(lines.T)]


def per_device(positions, charges, counts, mol_ids, pair_blocks, pair_count):
    vmem = pl.BlockSpec(memory_space=pltpu.VMEM)
    smem = pl.BlockSpec(memory_space=pltpu.SMEM)
    one = pltpu.SemaphoreType.DMA
    two = pltpu.SemaphoreType.DMA((2,))
    constants = [jnp.asarray(t) for t in tables()]
    return pl.pallas_call(
        kernel,
        out_shape=jax.ShapeDtypeStruct(positions.shape, f32),
        in_specs=[vmem, vmem, smem, vmem, vmem, smem] + [vmem] * 6,
        out_specs=vmem,
        scratch_shapes=[
            pltpu.VMEM((3, 2, 8, 128), f32),
            pltpu.VMEM((GRID, ATOMS), bf16),
            pltpu.VMEM((GRID, ATOMS), bf16),
            pltpu.VMEM((GRID, ATOMS), bf16),
            pltpu.VMEM((GRID, ATOMS), bf16),
            pltpu.VMEM((N_PME, ROWS_Y, 128), f32),
            pltpu.VMEM((N_PME, ROWS_Y, 128), f32),
            pltpu.VMEM((N_DOM, 4, 128), f32),
            pltpu.VMEM((N_DOM, 4, 128), f32),
            pltpu.VMEM((N_DOM, 4, 128), f32),
            pltpu.VMEM((N_DOM, 4, 128), f32),
            pltpu.VMEM((N_PME, ROWS_Y, 128), f32),
            pltpu.VMEM((N_PME, ROWS_Y, 128), f32),
            pltpu.VMEM((2, 8, 128), f32),
            pltpu.VMEM((2, 8, 128), f32),
            pltpu.VMEM((GRID, 128), f32),
            pltpu.VMEM((2, 8, 128), f32),
            two,
            two,
            one,
            one,
            one,
            one,
            one,
            one,
            one,
            one,
            two,
            two,
        ],
        compiler_params=pltpu.CompilerParams(
            collective_id=0, has_side_effects=True, vmem_limit_bytes=40 * 1024 * 1024
        ),
    )(positions, charges, counts, mol_ids, pair_blocks, pair_count, *constants)


def solution(mesh):
    in_specs = (
        P(("dom", "pme"), None, None),
        P(("dom", "pme"), None),
        P(("dom", "pme")),
        P(("dom", "pme"), None),
        P(("dom", "pme"), None),
        P(("dom", "pme")),
    )
    out_specs = P(("dom", "pme"), None, None)
    return jax.shard_map(
        per_device, mesh=mesh, in_specs=in_specs, out_specs=out_specs, check_vma=False
    )
```

```python
import functools
import math

import jax
import jax.numpy as jnp
import ml_dtypes
import numpy as np
from jax import lax
from jax.experimental import pallas as pl
from jax.experimental.pallas import tpu as pltpu
from jax.sharding import PartitionSpec as P

GRID = 256
N_DOM = 64
N_PME = 8
SX = 4
SY = 32
ROWS_Y = 40
FLAT = SX * ROWS_Y
ATOMS = 768
MESH = pl.DeviceIdType.MESH

coulomb = 8.0
sigma_six = 2.5**6
well_depth = 0.5
core_alpha = 0.5
recip_scale = 6.0
f32 = jnp.float32
bf16 = jnp.bfloat16

SPANS = (((0, 144, 0), (240, 256, -256)), ((112, 256, 0), (0, 16, 256)))

NN = (((1,), (0,)), ((), ()))
NT = (((1,), (1,)), ((), ()))


def split(value):
    high = value.astype(bf16)
    return high, (value - high.astype(f32)).astype(bf16)


def product(left, right, dims=NN):
    def one(a, b):
        return lax.dot_general(a, b, dims, preferred_element_type=f32)

    return one(left[0], right[0]) + (one(left[0], right[1]) + one(left[1], right[0]))


def swap_groups(pieces):
    group = lax.broadcasted_iota(jnp.int32, pieces[0].shape, 1) // 32
    out = []
    for j in range(4):
        total = pieces[j]
        for i in range(4):
            if i != j:
                total = jnp.where(group == i, pltpu.roll(pieces[i], 32 * ((i - j) % 4), 1), total)
        out.append(total)
    return out


def bumps(delta):
    away = jnp.abs(delta)
    return [jnp.maximum(top - away, 0.0) for top in (3.0, 2.0, 1.0)]


def weight(delta):
    total = 0.0
    for part, factor in zip(bumps(delta), (1.0, -6.0, 15.0)):
        square = part * part
        total = total + (factor / 120.0) * (square * square * part)
    return total


def slope(delta):
    total = 0.0
    for part, factor in zip(bumps(delta), (1.0, -6.0, 15.0)):
        square = part * part
        total = total + (factor / 24.0) * (square * square)
    return jnp.where(delta > 0.0, -total, total)


def scaled_erfc(z):
    t = 1.0 / (1.0 + 0.5 * z)
    poly = 0.17087277
    for c in (
        -0.82215223,
        1.48851587,
        -1.13520398,
        0.27886807,
        -0.18628806,
        0.09678418,
        0.37409196,
        1.00002368,
        -1.26551223,
    ):
        poly = poly * t + c
    return t * jnp.exp(poly)


def pair_scalar(parts, left, right):
    dist_sq = parts[0] * parts[0] + parts[1] * parts[1] + parts[2] * parts[2]
    soft_sq = dist_sq + 1.0
    inv = lax.rsqrt(soft_sq)
    inv_sq = inv * inv
    gauss = jnp.exp(-soft_sq)
    charge = coulomb * left[3] * right[3]
    whole = (
        charge * gauss * (scaled_erfc(soft_sq * inv) * inv + 2.0 / math.sqrt(math.pi)) * inv_sq
    )
    inv_hard = 1.0 / (core_alpha * sigma_six + dist_sq * dist_sq * dist_sq)
    ratio = sigma_six * inv_hard
    dispersion = 24.0 * well_depth * dist_sq * dist_sq * (2.0 * ratio - 1.0) * ratio * inv_hard
    other = jnp.where(left[4] == right[4], -charge * inv * inv_sq, dispersion)
    return left[5] * right[5] * (whole + other)


def kernel(
    pos_in,
    charges_in,
    counts_in,
    mols_in,
    pairs_in,
    listed_in,
    h_in,
    y_in,
    yt_in,
    out,
    pos,
    charges,
    counts,
    mols,
    pairs,
    listed,
    h,
    y,
    yt,
    in_s,
    at,
    wz_hi,
    wz_lo,
    dz_hi,
    dz_lo,
    sp,
    rp,
    sd,
    rd,
    sd2,
    rd2,
    sq,
    rq,
    fs,
    fr,
    lam,
    short,
    halo_s,
    halo_r,
    p1_s,
    p1_r,
    d1_s,
    d1_r,
    d2_s,
    d2_r,
    p2_s,
    p2_r,
    f_s,
    f_r,
):
    me_d = lax.axis_index("dom")
    me_p = lax.axis_index("pme")
    up = lax.rem(me_d + 1, N_DOM)
    down = lax.rem(me_d + N_DOM - 1, N_DOM)

    inputs = [
        pltpu.make_async_copy(source, target, in_s.at[i])
        for i, (source, target) in enumerate(
            (
                (pos_in, pos),
                (charges_in, charges),
                (counts_in, counts),
                (mols_in, mols),
                (pairs_in, pairs),
                (listed_in, listed),
                (h_in, h),
                (y_in, y),
                (yt_in, yt),
            )
        )
    ]
    for copy in inputs:
        copy.start()

    barrier = pltpu.get_barrier_semaphore()
    for other in (up, down):
        pl.semaphore_signal(barrier, inc=1, device_id=(other, me_p), device_id_type=MESH)

    def greet_pme(k, carry):
        pl.semaphore_signal(
            barrier, inc=1, device_id=(me_d, lax.rem(me_p + k, N_PME)), device_id_type=MESH
        )
        return carry

    def greet_dom(k, carry):
        pl.semaphore_signal(
            barrier, inc=1, device_id=(lax.rem(me_d + k, N_DOM), me_p), device_id_type=MESH
        )
        return carry

    lax.fori_loop(1, N_PME, greet_pme, 0)
    lax.fori_loop(2, N_DOM - 1, greet_dom, 0)

    for copy in inputs[:4]:
        copy.wait()
    lane = lax.broadcasted_iota(jnp.int32, (1, 128), 1)
    for b in range(2):
        live = (lane < counts[b]).astype(f32)
        for v in range(3):
            at[1, b, v : v + 1, :] = pos[v, b : b + 1, :]
        at[1, b, 3:4, :] = charges[b : b + 1, :] * live
        at[1, b, 4:5, :] = mols[b : b + 1, :].astype(f32)
        at[1, b, 5:6, :] = live
        at[1, b, 6:8, :] = jnp.zeros((2, 128), f32)

    pl.semaphore_wait(barrier, N_PME - 1 + N_DOM - 1)

    to_up = pltpu.make_async_remote_copy(
        src_ref=at.at[1],
        dst_ref=at.at[0],
        send_sem=halo_s.at[0],
        recv_sem=halo_r.at[0],
        device_id=(up, me_p),
        device_id_type=MESH,
    )
    to_down = pltpu.make_async_remote_copy(
        src_ref=at.at[1],
        dst_ref=at.at[2],
        send_sem=halo_s.at[1],
        recv_sem=halo_r.at[1],
        device_id=(down, me_p),
        device_id_type=MESH,
    )
    to_up.start()
    to_down.start()

    def fill(side, function, high_ref, low_ref):
        for b in range(2):
            first = (2 * side + b) * 128
            coord = at[side, b, 2:3, :]
            charge = at[side, b, 3:4, :]
            for start, stop, wrap_z in SPANS[b]:
                cells = lax.broadcasted_iota(jnp.int32, (stop - start, 128), 0)
                delta = coord - (cells + (start + wrap_z)).astype(f32)
                high, low = split(function(delta) * charge)
                high_ref[start:stop, first : first + 128] = high
                low_ref[start:stop, first : first + 128] = low

    for refs in (wz_hi, wz_lo, dz_hi, dz_lo):
        for side in range(3):
            for b in range(2):
                first = (2 * side + b) * 128
                refs[128 - 112 * b : 240 - 112 * b, first : first + 128] = jnp.zeros((112, 128), bf16)
    fill(1, weight, wz_hi, wz_lo)
    corner_x = (me_d * SX).astype(f32)
    corner_y = (me_p * SY).astype(f32)
    wrap = (
        jnp.where(me_d == 0, 256.0, 0.0).astype(f32),
        f32(0.0),
        jnp.where(me_d == N_DOM - 1, -256.0, 0.0).astype(f32),
    )
    cells_x = lax.broadcasted_iota(jnp.int32, (8, 256), 0).astype(f32)
    cells_y = lax.broadcasted_iota(jnp.int32, (ROWS_Y, 256), 0).astype(f32) - 3.0

    def deltas(side):
        flat_x = jnp.concatenate(
            [at[side, b, 0:1, :] - (wrap[side] + corner_x) for b in range(2)], axis=1
        )
        flat_y = jnp.concatenate([at[side, b, 1:2, :] - corner_y for b in range(2)], axis=1)
        return flat_x - cells_x, flat_y - cells_y

    def spread(side):
        delta_x, delta_y = deltas(side)
        wx, wy = weight(delta_x), weight(delta_y)
        plane = jnp.concatenate([wx[x : x + 1] * wy for x in range(SX)], axis=0)
        first = 256 * side
        loaded = (wz_hi[:, first : first + 256], wz_lo[:, first : first + 256])
        return product(split(plane), loaded, NT)

    mesh = spread(1)
    to_up.wait_recv()
    to_down.wait_recv()
    for side in (0, 2):
        fill(side, weight, wz_hi, wz_lo)
        mesh = mesh + spread(side)
    inputs[6].wait()
    table = (h[0], h[1])
    depth = product(split(mesh), table)
    for half in range(2):
        pieces = [
            depth[ROWS_Y * x : ROWS_Y * (x + 1), 128 * half : 128 * (half + 1)] for x in range(SX)
        ]
        for g, piece in enumerate(swap_groups(pieces)):
            sp[4 * half + g] = piece

    def pme_copy(source, target, k, send, receive):
        other = lax.rem(me_p + k, N_PME)
        return pltpu.make_async_remote_copy(
            src_ref=source.at[other],
            dst_ref=target.at[me_p],
            send_sem=send,
            recv_sem=receive,
            device_id=(me_d, other),
            device_id_type=MESH,
        )

    def pme_all(source, target, send, receive):
        return pltpu.make_async_remote_copy(
            src_ref=source.at[pl.ds(0, N_PME - 1)],
            dst_ref=target.at[pl.ds(0, N_PME - 1)],
            send_sem=send,
            recv_sem=receive,
            device_id=(me_d, lax.rem(me_p + 1, N_PME)),
            device_id_type=MESH,
        )

    def dom_copy(source, target, k, send, receive):
        other = lax.rem(me_d + k, N_DOM)
        return pltpu.make_async_remote_copy(
            src_ref=source.at[other],
            dst_ref=target.at[me_d],
            send_sem=send,
            recv_sem=receive,
            device_id=(other, me_p),
            device_id_type=MESH,
        )

    def dom_all(source, target, send, receive):
        return pltpu.make_async_remote_copy(
            src_ref=source.at[pl.ds(0, N_DOM - 1)],
            dst_ref=target.at[pl.ds(0, N_DOM - 1)],
            send_sem=send,
            recv_sem=receive,
            device_id=(up, me_p),
            device_id_type=MESH,
        )

    def start_pme(source, target, send, receive):
        def body(k, carry):
            pme_copy(source, target, k, send, receive).start()
            return carry

        lax.fori_loop(1, N_PME, body, 0)

    def start_dom(source, target, send, receive):
        def body(k, carry):
            dom_copy(source, target, N_DOM // 2 - k, send, receive).start()
            dom_copy(source, target, N_DOM // 2 + k, send, receive).start()
            return carry

        dom_copy(source, target, N_DOM // 2, send, receive).start()
        lax.fori_loop(1, N_DOM // 2, body, 0)

    start_pme(sp, rp, p1_s, p1_r)
    rp[me_p] = sp[me_p]

    for side in range(3):
        fill(side, slope, dz_hi, dz_lo)

    inputs[7].wait()
    pme_all(sp, rp, p1_s, p1_r).wait_recv()
    lines = product(
        (y[0], y[1]), split(rp[...].reshape(N_PME * ROWS_Y, 128))
    )
    flat_sd = sd.reshape(GRID, 128)
    for x, piece in enumerate(swap_groups([lines[64 * k : 64 * (k + 1)] for k in range(4)])):
        flat_sd[pl.ds(x, 64, stride=4), :] = piece
    start_dom(sd, rd, d1_s, d1_r)
    rd[me_d] = sd[me_d]

    def folded(index):
        return jnp.where(index < GRID // 2, index, index - GRID).astype(f32) * (1.0 / GRID)

    lanes = lax.broadcasted_iota(jnp.int32, (GRID, 128), 1)
    freq_x = folded(lax.broadcasted_iota(jnp.int32, (GRID, 128), 0))
    freq_y = folded(me_d * 4 + lanes // 32)
    freq_z = folded(me_p * 32 + lanes % 32)
    wave = freq_x * freq_x + freq_y * freq_y + freq_z * freq_z
    safe = jnp.where(wave > 0.0, wave, 1.0)
    lam[...] = jnp.where(
        wave > 0.0, (recip_scale / GRID**3) * jnp.exp(-(math.pi**2) * safe) / safe, 0.0
    )

    dom_all(sd, rd, d1_s, d1_r).wait_recv()
    spectrum = product(table, split(rd.reshape(GRID, 128)[...])) * lam[...]
    sd2.reshape(GRID, 128)[...] = product(table, split(spectrum))
    start_dom(sd2, rd2, d2_s, d2_r)
    rd2[me_d] = sd2[me_d]

    padded = jnp.concatenate([at[1, 0], at[1, 1], jnp.zeros((112, 128), f32)], axis=0)
    columns = padded.T
    inputs[4].wait()
    inputs[5].wait()
    rows = lax.broadcasted_iota(jnp.int32, (1, 48), 1)
    sublane = lax.broadcasted_iota(jnp.int32, (128, 128), 1)
    on_own = jnp.zeros((128, 128), f32)
    on_above = [[0.0] * 3, [0.0] * 3]
    for a in range(2):
        left = [columns[:, 8 * a + r : 8 * a + r + 1] for r in range(6)]
        on_left = [0.0] * 3
        for c in range(2):
            right = [at[2, c, r : r + 1, :] for r in range(6)]
            hit = (rows < listed[0]) & (pairs[0:1, :] == a) & (pairs[1:2, :] == c)
            times = jnp.sum(hit.astype(f32), axis=1, keepdims=True)
            dz = left[2] - right[2]
            if a < c:
                dz = jnp.where(dz < -128.0, dz + 256.0, dz)
            if a > c:
                dz = jnp.where(dz >= 128.0, dz - 256.0, dz)
            parts = [left[0] - (right[0] - wrap[2]), left[1] - right[1], dz]
            scalar = pair_scalar(parts, left, right) * times
            for v in range(3):
                force = scalar * parts[v]
                on_left[v] = on_left[v] + force
                on_above[c][v] = on_above[c][v] - jnp.sum(force, axis=0, keepdims=True)
        for v in range(3):
            on_own = jnp.where(
                sublane == 3 * a + v, jnp.sum(on_left[v], axis=1, keepdims=True), on_own
            )
    short[0] = on_own.T[0:8]
    short[1] = jnp.concatenate(on_above[0] + on_above[1] + [jnp.zeros((2, 128), f32)], axis=0)

    weights_x, slopes_x, weights_y, slopes_y = [], [], [], []
    for side in range(3):
        delta_x, delta_y = deltas(side)
        weights_x.append(weight(delta_x))
        slopes_x.append(slope(delta_x))
        weights_y.append(weight(delta_y))
        slopes_y.append(slope(delta_y))
    wx, dx, wy, dy = (
        jnp.concatenate(parts, axis=1) for parts in (weights_x, slopes_x, weights_y, slopes_y)
    )
    inputs[8].wait()

    dom_all(sd2, rd2, d2_s, d2_r).wait_recv()
    flat_rd2 = rd2.reshape(GRID, 128)
    lines = jnp.concatenate(
        swap_groups([flat_rd2[pl.ds(x, 64, stride=4), :] for x in range(4)]), axis=0
    )
    sq[...] = product((yt[0], yt[1]), split(lines)).reshape(N_PME, ROWS_Y, 128)
    start_pme(sq, rq, p2_s, p2_r)
    rq[me_p] = sq[me_p]

    pme_all(sq, rq, p2_s, p2_r).wait_recv()
    halves = [swap_groups([rq[4 * half + g] for g in range(4)]) for half in range(2)]
    depth = jnp.concatenate(
        [jnp.concatenate([halves[0][x], halves[1][x]], axis=1) for x in range(SX)], axis=0
    )
    potential = split(product(split(depth), table))
    along = product(potential, (wz_hi[...], wz_lo[...]))
    along_slope = product(potential, (dz_hi[...], dz_lo[...]))
    field = [0.0] * 3
    for x in range(SX):
        here = along[ROWS_Y * x : ROWS_Y * (x + 1)]
        there = along_slope[ROWS_Y * x : ROWS_Y * (x + 1)]
        field[0] = field[0] - dx[x : x + 1] * jnp.sum(wy * here, axis=0, keepdims=True)
        field[1] = field[1] - wx[x : x + 1] * jnp.sum(dy * here, axis=0, keepdims=True)
        field[2] = field[2] - wx[x : x + 1] * jnp.sum(wy * there, axis=0, keepdims=True)

    def force_rows(side):
        return jnp.concatenate(
            [
                field[v][:, 128 * (2 * side + b) : 128 * (2 * side + b + 1)]
                for b in range(2)
                for v in range(3)
            ]
            + [jnp.zeros((2, 128), f32)],
            axis=0,
        )

    fs[0] = force_rows(0)
    fs[1] = force_rows(2) + short[1]
    send_down = pltpu.make_async_remote_copy(
        src_ref=fs.at[0],
        dst_ref=fr.at[0],
        send_sem=f_s.at[0],
        recv_sem=f_r.at[0],
        device_id=(down, me_p),
        device_id_type=MESH,
    )
    send_up = pltpu.make_async_remote_copy(
        src_ref=fs.at[1],
        dst_ref=fr.at[1],
        send_sem=f_s.at[1],
        recv_sem=f_r.at[1],
        device_id=(up, me_p),
        device_id_type=MESH,
    )
    send_down.start()
    send_up.start()
    total = force_rows(1) + short[0]

    to_up.wait_send()
    to_down.wait_send()
    pme_all(sp, rp, p1_s, p1_r).wait_send()
    dom_all(sd, rd, d1_s, d1_r).wait_send()
    dom_all(sd2, rd2, d2_s, d2_r).wait_send()
    pme_all(sq, rq, p2_s, p2_r).wait_send()
    send_down.wait_recv()
    send_up.wait_recv()
    total = total + fr[0] + fr[1]
    for v in range(3):
        for b in range(2):
            out[v, b : b + 1, :] = total[3 * b + v : 3 * b + v + 1]
    send_down.wait_send()
    send_up.wait_send()


def two_parts(table):
    high = table.astype(ml_dtypes.bfloat16)
    low = (table - high.astype(np.float64)).astype(ml_dtypes.bfloat16)
    return np.stack([high, low])


def cas(first, second):
    angle = 2.0 * np.pi / GRID * (np.outer(first, second) % GRID)
    return np.cos(angle) + np.sin(angle)


def tables():
    index = np.arange(GRID)
    square = cas(index, index)
    freq = (4 * np.arange(64)[None, :] + np.arange(4)[:, None]).reshape(-1)
    cell = np.arange(ROWS_Y) - 3
    cells = (SY * np.arange(N_PME)[:, None] + cell[None, :]).reshape(-1)
    real = np.tile(np.arange(ROWS_Y) < SY + 6, N_PME)
    lines = cas(freq, cells % GRID) * real[None, :]
    return [two_parts(square), two_parts(lines), two_parts(lines.T)]


def per_device(positions, charges, counts, mol_ids, pair_blocks, pair_count):
    one = pltpu.SemaphoreType.DMA
    two = pltpu.SemaphoreType.DMA((2,))
    constants = [jnp.asarray(t) for t in tables()]
    forces = pl.pallas_call(
        kernel,
        out_shape=pltpu.VMEM((3, 2, 128), f32),
        in_specs=[pl.BlockSpec(memory_space=pltpu.HBM)] * 9,
        out_specs=pl.BlockSpec(memory_space=pltpu.VMEM),
        scratch_shapes=[
            pltpu.VMEM((3, 2, 128), f32),
            pltpu.VMEM((2, 128), f32),
            pltpu.SMEM((2,), jnp.int32),
            pltpu.VMEM((2, 128), jnp.int32),
            pltpu.VMEM((2, 48), jnp.int32),
            pltpu.SMEM((1,), jnp.int32),
            pltpu.VMEM((2, GRID, GRID), bf16),
            pltpu.VMEM((2, GRID, N_PME * ROWS_Y), bf16),
            pltpu.VMEM((2, N_PME * ROWS_Y, GRID), bf16),
            pltpu.SemaphoreType.DMA((9,)),
            pltpu.VMEM((3, 2, 8, 128), f32),
            pltpu.VMEM((GRID, ATOMS), bf16),
            pltpu.VMEM((GRID, ATOMS), bf16),
            pltpu.VMEM((GRID, ATOMS), bf16),
            pltpu.VMEM((GRID, ATOMS), bf16),
            pltpu.VMEM((N_PME, ROWS_Y, 128), f32),
            pltpu.VMEM((N_PME, ROWS_Y, 128), f32),
            pltpu.VMEM((N_DOM, 4, 128), f32),
            pltpu.VMEM((N_DOM, 4, 128), f32),
            pltpu.VMEM((N_DOM, 4, 128), f32),
            pltpu.VMEM((N_DOM, 4, 128), f32),
            pltpu.VMEM((N_PME, ROWS_Y, 128), f32),
            pltpu.VMEM((N_PME, ROWS_Y, 128), f32),
            pltpu.VMEM((2, 8, 128), f32),
            pltpu.VMEM((2, 8, 128), f32),
            pltpu.VMEM((GRID, 128), f32),
            pltpu.VMEM((2, 8, 128), f32),
            two,
            two,
            one,
            one,
            one,
            one,
            one,
            one,
            one,
            one,
            two,
            two,
        ],
        compiler_params=pltpu.CompilerParams(
            collective_id=0, has_side_effects=True, vmem_limit_bytes=48 * 1024 * 1024
        ),
    )(
        *(
            value if value is pair_count else pltpu.with_memory_space_constraint(value, pltpu.HBM)
            for value in (
                positions.transpose(1, 0, 2),
                charges,
                counts,
                mol_ids,
                pair_blocks.T,
                pair_count,
                *constants,
            )
        )
    )
    return forces.transpose(1, 0, 2)


def solution(mesh):
    in_specs = (
        P(("dom", "pme"), None, None),
        P(("dom", "pme"), None),
        P(("dom", "pme")),
        P(("dom", "pme"), None),
        P(("dom", "pme"), None),
        P(("dom", "pme")),
    )
    out_specs = P(("dom", "pme"), None, None)
    return jax.shard_map(
        per_device, mesh=mesh, in_specs=in_specs, out_specs=out_specs, check_vma=False
    )
```

```python
import functools
import math

import jax
import jax.numpy as jnp
import ml_dtypes
import numpy as np
from jax import lax
from jax.experimental import pallas as pl
from jax.experimental.pallas import tpu as pltpu
from jax.sharding import PartitionSpec as P

GRID = 256
N_DOM = 64
RING_Y = 4
RING_Z = 16
N_PME = 8
SX = 4
SY = 32
ROWS_Y = 40
FLAT = SX * ROWS_Y
ATOMS = 768
MESH = pl.DeviceIdType.MESH

coulomb = 8.0
sigma_six = 2.5**6
well_depth = 0.5
core_alpha = 0.5
recip_scale = 6.0
f32 = jnp.float32
bf16 = jnp.bfloat16

SPANS = (((0, 144, 0), (240, 256, -256)), ((112, 256, 0), (0, 16, 256)))

NN = (((1,), (0,)), ((), ()))
NT = (((1,), (1,)), ((), ()))


def split(value):
    high = value.astype(bf16)
    return high, (value - high.astype(f32)).astype(bf16)


def product(left, right, dims=NN):
    def one(a, b):
        return lax.dot_general(a, b, dims, preferred_element_type=f32)

    return one(left[0], right[0]) + (one(left[0], right[1]) + one(left[1], right[0]))


def swap_groups(pieces):
    group = lax.broadcasted_iota(jnp.int32, pieces[0].shape, 1) // 32
    out = []
    for j in range(4):
        total = pieces[j]
        for i in range(4):
            if i != j:
                total = jnp.where(group == i, pltpu.roll(pieces[i], 32 * ((i - j) % 4), 1), total)
        out.append(total)
    return out


def bumps(delta):
    away = jnp.abs(delta)
    return [jnp.maximum(top - away, 0.0) for top in (3.0, 2.0, 1.0)]


def weight(delta):
    total = 0.0
    for part, factor in zip(bumps(delta), (1.0, -6.0, 15.0)):
        square = part * part
        total = total + (factor / 120.0) * (square * square * part)
    return total


def slope(delta):
    total = 0.0
    for part, factor in zip(bumps(delta), (1.0, -6.0, 15.0)):
        square = part * part
        total = total + (factor / 24.0) * (square * square)
    return jnp.where(delta > 0.0, -total, total)


def scaled_erfc(z):
    t = 1.0 / (1.0 + 0.5 * z)
    poly = 0.17087277
    for c in (
        -0.82215223,
        1.48851587,
        -1.13520398,
        0.27886807,
        -0.18628806,
        0.09678418,
        0.37409196,
        1.00002368,
        -1.26551223,
    ):
        poly = poly * t + c
    return t * jnp.exp(poly)


def pair_scalar(parts, left, right):
    dist_sq = parts[0] * parts[0] + parts[1] * parts[1] + parts[2] * parts[2]
    soft_sq = dist_sq + 1.0
    inv = lax.rsqrt(soft_sq)
    inv_sq = inv * inv
    gauss = jnp.exp(-soft_sq)
    charge = coulomb * left[3] * right[3]
    whole = (
        charge * gauss * (scaled_erfc(soft_sq * inv) * inv + 2.0 / math.sqrt(math.pi)) * inv_sq
    )
    inv_hard = 1.0 / (core_alpha * sigma_six + dist_sq * dist_sq * dist_sq)
    ratio = sigma_six * inv_hard
    dispersion = 24.0 * well_depth * dist_sq * dist_sq * (2.0 * ratio - 1.0) * ratio * inv_hard
    other = jnp.where(left[4] == right[4], -charge * inv * inv_sq, dispersion)
    return left[5] * right[5] * (whole + other)


def kernel(
    pos_in,
    charges_in,
    counts_in,
    mols_in,
    pairs_in,
    listed_in,
    h_in,
    y_in,
    yt_in,
    out,
    pos,
    charges,
    counts,
    mols,
    pairs,
    listed,
    h,
    y,
    yt,
    in_s,
    at,
    wz_hi,
    wz_lo,
    dz_hi,
    dz_lo,
    sp,
    rp,
    sd,
    ta,
    rd,
    sd2,
    tb,
    rd2,
    sq,
    rq,
    fs,
    fr,
    lam,
    short,
    halo_s,
    halo_r,
    p1_s,
    p1_r,
    y1_s,
    y1_r,
    z1_s,
    z1_r,
    z2_s,
    z2_r,
    y2_s,
    y2_r,
    p2_s,
    p2_r,
    f_s,
    f_r,
):
    me_d = lax.axis_index("dom")
    me_p = lax.axis_index("pme")
    up = lax.rem(me_d + 1, N_DOM)
    down = lax.rem(me_d + N_DOM - 1, N_DOM)

    inputs = [
        pltpu.make_async_copy(source, target, in_s.at[i])
        for i, (source, target) in enumerate(
            (
                (pos_in, pos),
                (charges_in, charges),
                (counts_in, counts),
                (mols_in, mols),
                (pairs_in, pairs),
                (listed_in, listed),
                (h_in, h),
                (y_in, y),
                (yt_in, yt),
            )
        )
    ]
    for copy in inputs:
        copy.start()

    barrier = pltpu.get_barrier_semaphore()
    for other in (up, down):
        pl.semaphore_signal(barrier, inc=1, device_id=(other, me_p), device_id_type=MESH)

    def pme_at(k):
        there = me_p + k
        return jnp.where(there >= N_PME, there - N_PME, there)

    me_z, me_y = me_d // RING_Y, me_d % RING_Y

    def y_at(k):
        there = me_y + k
        return jnp.where(there >= RING_Y, there - RING_Y, there)

    def z_at(k):
        there = me_z + k
        return jnp.where(there >= RING_Z, there - RING_Z, there)

    for k in range(1, N_PME):
        pl.semaphore_signal(barrier, inc=1, device_id=(me_d, pme_at(k)), device_id_type=MESH)

    for k in range(1, RING_Y):
        other = me_z * RING_Y + y_at(k)
        pl.semaphore_signal(barrier, inc=1, device_id=(other, me_p), device_id_type=MESH)
    for k in range(1, RING_Z):
        other = z_at(k) * RING_Y + me_y
        pl.semaphore_signal(barrier, inc=1, device_id=(other, me_p), device_id_type=MESH)

    for copy in inputs[:4]:
        copy.wait()
    lane = lax.broadcasted_iota(jnp.int32, (1, 128), 1)
    for b in range(2):
        live = (lane < counts[b]).astype(f32)
        for v in range(3):
            at[1, b, v : v + 1, :] = pos[v, b : b + 1, :]
        at[1, b, 3:4, :] = charges[b : b + 1, :] * live
        at[1, b, 4:5, :] = mols[b : b + 1, :].astype(f32)
        at[1, b, 5:6, :] = live
        at[1, b, 6:8, :] = jnp.zeros((2, 128), f32)

    pl.semaphore_wait(barrier, 2 + N_PME - 1 + RING_Y - 1 + RING_Z - 1)

    to_up = pltpu.make_async_remote_copy(
        src_ref=at.at[1],
        dst_ref=at.at[0],
        send_sem=halo_s.at[0],
        recv_sem=halo_r.at[0],
        device_id=(up, me_p),
        device_id_type=MESH,
    )
    to_down = pltpu.make_async_remote_copy(
        src_ref=at.at[1],
        dst_ref=at.at[2],
        send_sem=halo_s.at[1],
        recv_sem=halo_r.at[1],
        device_id=(down, me_p),
        device_id_type=MESH,
    )
    to_up.start()
    to_down.start()

    def fill(side, function, high_ref, low_ref):
        for b in range(2):
            first = (2 * side + b) * 128
            coord = at[side, b, 2:3, :]
            charge = at[side, b, 3:4, :]
            for start, stop, wrap_z in SPANS[b]:
                cells = lax.broadcasted_iota(jnp.int32, (stop - start, 128), 0)
                delta = coord - (cells + (start + wrap_z)).astype(f32)
                high, low = split(function(delta) * charge)
                high_ref[start:stop, first : first + 128] = high
                low_ref[start:stop, first : first + 128] = low

    for refs in (wz_hi, wz_lo, dz_hi, dz_lo):
        for side in range(3):
            for b in range(2):
                first = (2 * side + b) * 128
                refs[128 - 112 * b : 240 - 112 * b, first : first + 128] = jnp.zeros((112, 128), bf16)
    fill(1, weight, wz_hi, wz_lo)
    corner_x = (me_d * SX).astype(f32)
    corner_y = (me_p * SY).astype(f32)
    wrap = (
        jnp.where(me_d == 0, 256.0, 0.0).astype(f32),
        f32(0.0),
        jnp.where(me_d == N_DOM - 1, -256.0, 0.0).astype(f32),
    )
    cells_x = lax.broadcasted_iota(jnp.int32, (8, 256), 0).astype(f32)
    cells_y = lax.broadcasted_iota(jnp.int32, (ROWS_Y, 256), 0).astype(f32) - 3.0

    def deltas(side):
        flat_x = jnp.concatenate(
            [at[side, b, 0:1, :] - (wrap[side] + corner_x) for b in range(2)], axis=1
        )
        flat_y = jnp.concatenate([at[side, b, 1:2, :] - corner_y for b in range(2)], axis=1)
        return flat_x - cells_x, flat_y - cells_y

    def spread(side):
        delta_x, delta_y = deltas(side)
        wx, wy = weight(delta_x), weight(delta_y)
        plane = jnp.concatenate([wx[x : x + 1] * wy for x in range(SX)], axis=0)
        first = 256 * side
        loaded = (wz_hi[:, first : first + 256], wz_lo[:, first : first + 256])
        return product(split(plane), loaded, NT)

    mesh = spread(1)
    to_up.wait_recv()
    to_down.wait_recv()
    for side in (0, 2):
        fill(side, weight, wz_hi, wz_lo)
        mesh = mesh + spread(side)
    inputs[6].wait()
    table = (h[0], h[1])
    depth = product(split(mesh), table)
    for half in range(2):
        pieces = [
            depth[ROWS_Y * x : ROWS_Y * (x + 1), 128 * half : 128 * (half + 1)] for x in range(SX)
        ]
        for g, piece in enumerate(swap_groups(pieces)):
            sp[4 * half + g] = piece

    def pme_copy(source, target, k, send, receive):
        other = pme_at(k)
        return pltpu.make_async_remote_copy(
            src_ref=source.at[other],
            dst_ref=target.at[me_p],
            send_sem=send,
            recv_sem=receive,
            device_id=(me_d, other),
            device_id_type=MESH,
        )

    def pme_all(source, target, send, receive):
        return pltpu.make_async_remote_copy(
            src_ref=source.at[pl.ds(0, N_PME - 1)],
            dst_ref=target.at[pl.ds(0, N_PME - 1)],
            send_sem=send,
            recv_sem=receive,
            device_id=(me_d, pme_at(1)),
            device_id_type=MESH,
        )

    def start_y(source, target, send, receive):
        for k in (2, 1, 3):
            other = y_at(k)
            pltpu.make_async_remote_copy(
                src_ref=source(other),
                dst_ref=target(me_y),
                send_sem=send,
                recv_sem=receive,
                device_id=(me_z * RING_Y + other, me_p),
                device_id_type=MESH,
            ).start()

    def start_z(source, target, send, receive):
        for k in (8, 7, 9, 6, 10, 5, 11, 4, 12, 3, 13, 2, 14, 1, 15):
            other = z_at(k)
            pltpu.make_async_remote_copy(
                src_ref=source(other),
                dst_ref=target(me_z),
                send_sem=send,
                recv_sem=receive,
                device_id=(other * RING_Y + me_y, me_p),
                device_id_type=MESH,
            ).start()

    def all_of(view, send, receive):
        return pltpu.make_async_remote_copy(
            src_ref=view,
            dst_ref=view,
            send_sem=send,
            recv_sem=receive,
            device_id=(up, me_p),
            device_id_type=MESH,
        )

    def start_pme(source, target, send, receive):
        for k in (4, 3, 5, 2, 6, 7, 1):
            pme_copy(source, target, k, send, receive).start()

    all_y1 = all_of(ta.at[pl.ds(0, RING_Y - 1)], y1_s, y1_r)
    all_z1 = all_of(rd.at[pl.ds(0, RING_Z - 1)], z1_s, z1_r)
    all_z2 = all_of(tb.at[pl.ds(0, RING_Z - 1)], z2_s, z2_r)
    all_y2 = all_of(rd2.at[:, pl.ds(0, RING_Y - 1)], y2_s, y2_r)
    start_pme(sp, rp, p1_s, p1_r)
    rp[me_p] = sp[me_p]

    for side in range(3):
        fill(side, slope, dz_hi, dz_lo)

    inputs[7].wait()
    pme_all(sp, rp, p1_s, p1_r).wait_recv()
    lines = product(
        (y[0], y[1]), split(rp[...].reshape(N_PME * ROWS_Y, 128))
    )
    flat_sd = sd.reshape(GRID, 128)
    for x, piece in enumerate(swap_groups([lines[64 * k : 64 * (k + 1)] for k in range(4)])):
        flat_sd[pl.ds(x, 64, stride=4), :] = piece
    start_y(lambda i: sd.at[:, i], lambda i: ta.at[i], y1_s, y1_r)
    ta[me_y] = sd[:, me_y]

    def folded(index):
        return jnp.where(index < GRID // 2, index, index - GRID).astype(f32) * (1.0 / GRID)

    lanes = lax.broadcasted_iota(jnp.int32, (GRID, 128), 1)
    freq_x = folded(lax.broadcasted_iota(jnp.int32, (GRID, 128), 0))
    freq_y = folded(me_d * 4 + lanes // 32)
    freq_z = folded(me_p * 32 + lanes % 32)
    wave = freq_x * freq_x + freq_y * freq_y + freq_z * freq_z
    safe = jnp.where(wave > 0.0, wave, 1.0)
    lam[...] = jnp.where(
        wave > 0.0, (recip_scale / GRID**3) * jnp.exp(-(math.pi**2) * safe) / safe, 0.0
    )

    all_y1.wait_recv()
    start_z(lambda i: ta.at[:, i], lambda i: rd.at[i], z1_s, z1_r)
    rd[me_z] = ta[:, me_z]
    all_z1.wait_recv()
    spectrum = product(table, split(rd.reshape(GRID, 128)[...])) * lam[...]
    sd2.reshape(GRID, 128)[...] = product(table, split(spectrum))
    start_z(lambda i: sd2.at[i], lambda i: tb.at[i], z2_s, z2_r)
    tb[me_z] = sd2[me_z]

    padded = jnp.concatenate([at[1, 0], at[1, 1], jnp.zeros((112, 128), f32)], axis=0)
    columns = padded.T
    inputs[4].wait()
    inputs[5].wait()
    rows = lax.broadcasted_iota(jnp.int32, (1, 48), 1)
    sublane = lax.broadcasted_iota(jnp.int32, (128, 128), 1)
    on_own = jnp.zeros((128, 128), f32)
    on_above = [[0.0] * 3, [0.0] * 3]
    for a in range(2):
        left = [columns[:, 8 * a + r : 8 * a + r + 1] for r in range(6)]
        on_left = [0.0] * 3
        for c in range(2):
            right = [at[2, c, r : r + 1, :] for r in range(6)]
            hit = (rows < listed[0]) & (pairs[0:1, :] == a) & (pairs[1:2, :] == c)
            times = jnp.sum(hit.astype(f32), axis=1, keepdims=True)
            dz = left[2] - right[2]
            if a < c:
                dz = jnp.where(dz < -128.0, dz + 256.0, dz)
            if a > c:
                dz = jnp.where(dz >= 128.0, dz - 256.0, dz)
            parts = [left[0] - (right[0] - wrap[2]), left[1] - right[1], dz]
            scalar = pair_scalar(parts, left, right) * times
            for v in range(3):
                force = scalar * parts[v]
                on_left[v] = on_left[v] + force
                on_above[c][v] = on_above[c][v] - jnp.sum(force, axis=0, keepdims=True)
        for v in range(3):
            on_own = jnp.where(
                sublane == 3 * a + v, jnp.sum(on_left[v], axis=1, keepdims=True), on_own
            )
    short[0] = on_own.T[0:8]
    short[1] = jnp.concatenate(on_above[0] + on_above[1] + [jnp.zeros((2, 128), f32)], axis=0)

    weights_x, slopes_x, weights_y, slopes_y = [], [], [], []
    for side in range(3):
        delta_x, delta_y = deltas(side)
        weights_x.append(weight(delta_x))
        slopes_x.append(slope(delta_x))
        weights_y.append(weight(delta_y))
        slopes_y.append(slope(delta_y))
    wx, dx, wy, dy = (
        jnp.concatenate(parts, axis=1) for parts in (weights_x, slopes_x, weights_y, slopes_y)
    )
    inputs[8].wait()

    all_z2.wait_recv()
    start_y(lambda i: tb.at[:, i], lambda i: rd2.at[:, i], y2_s, y2_r)
    rd2[:, me_y] = tb[:, me_y]
    all_y2.wait_recv()
    flat_rd2 = rd2.reshape(GRID, 128)
    lines = jnp.concatenate(
        swap_groups([flat_rd2[pl.ds(x, 64, stride=4), :] for x in range(4)]), axis=0
    )
    sq[...] = product((yt[0], yt[1]), split(lines)).reshape(N_PME, ROWS_Y, 128)
    start_pme(sq, rq, p2_s, p2_r)
    rq[me_p] = sq[me_p]

    pme_all(sq, rq, p2_s, p2_r).wait_recv()
    halves = [swap_groups([rq[4 * half + g] for g in range(4)]) for half in range(2)]
    depth = jnp.concatenate(
        [jnp.concatenate([halves[0][x], halves[1][x]], axis=1) for x in range(SX)], axis=0
    )
    potential = split(product(split(depth), table))
    along = product(potential, (wz_hi[...], wz_lo[...]))
    along_slope = product(potential, (dz_hi[...], dz_lo[...]))
    field = [0.0] * 3
    for x in range(SX):
        here = along[ROWS_Y * x : ROWS_Y * (x + 1)]
        there = along_slope[ROWS_Y * x : ROWS_Y * (x + 1)]
        field[0] = field[0] - dx[x : x + 1] * jnp.sum(wy * here, axis=0, keepdims=True)
        field[1] = field[1] - wx[x : x + 1] * jnp.sum(dy * here, axis=0, keepdims=True)
        field[2] = field[2] - wx[x : x + 1] * jnp.sum(wy * there, axis=0, keepdims=True)

    def force_rows(side):
        return jnp.concatenate(
            [
                field[v][:, 128 * (2 * side + b) : 128 * (2 * side + b + 1)]
                for b in range(2)
                for v in range(3)
            ]
            + [jnp.zeros((2, 128), f32)],
            axis=0,
        )

    fs[0] = force_rows(0)
    fs[1] = force_rows(2) + short[1]
    send_down = pltpu.make_async_remote_copy(
        src_ref=fs.at[0],
        dst_ref=fr.at[0],
        send_sem=f_s.at[0],
        recv_sem=f_r.at[0],
        device_id=(down, me_p),
        device_id_type=MESH,
    )
    send_up = pltpu.make_async_remote_copy(
        src_ref=fs.at[1],
        dst_ref=fr.at[1],
        send_sem=f_s.at[1],
        recv_sem=f_r.at[1],
        device_id=(up, me_p),
        device_id_type=MESH,
    )
    send_down.start()
    send_up.start()
    total = force_rows(1) + short[0]

    to_up.wait_send()
    to_down.wait_send()
    pme_all(sp, rp, p1_s, p1_r).wait_send()
    for copies in (all_y1, all_z1, all_z2, all_y2):
        copies.wait_send()
    pme_all(sq, rq, p2_s, p2_r).wait_send()
    send_down.wait_recv()
    send_up.wait_recv()
    total = total + fr[0] + fr[1]
    for v in range(3):
        for b in range(2):
            out[v, b : b + 1, :] = total[3 * b + v : 3 * b + v + 1]
    send_down.wait_send()
    send_up.wait_send()


def two_parts(table):
    high = table.astype(ml_dtypes.bfloat16)
    low = (table - high.astype(np.float64)).astype(ml_dtypes.bfloat16)
    return np.stack([high, low])


def cas(first, second):
    angle = 2.0 * np.pi / GRID * (np.outer(first, second) % GRID)
    return np.cos(angle) + np.sin(angle)


def tables():
    index = np.arange(GRID)
    square = cas(index, index)
    freq = (4 * np.arange(64)[None, :] + np.arange(4)[:, None]).reshape(-1)
    cell = np.arange(ROWS_Y) - 3
    cells = (SY * np.arange(N_PME)[:, None] + cell[None, :]).reshape(-1)
    real = np.tile(np.arange(ROWS_Y) < SY + 6, N_PME)
    lines = cas(freq, cells % GRID) * real[None, :]
    return [two_parts(square), two_parts(lines), two_parts(lines.T)]


def per_device(positions, charges, counts, mol_ids, pair_blocks, pair_count):
    one = pltpu.SemaphoreType.DMA
    two = pltpu.SemaphoreType.DMA((2,))
    constants = [jnp.asarray(t) for t in tables()]
    forces = pl.pallas_call(
        kernel,
        out_shape=pltpu.VMEM((3, 2, 128), f32),
        in_specs=[pl.BlockSpec(memory_space=pltpu.HBM)] * 9,
        out_specs=pl.BlockSpec(memory_space=pltpu.VMEM),
        scratch_shapes=[
            pltpu.VMEM((3, 2, 128), f32),
            pltpu.VMEM((2, 128), f32),
            pltpu.SMEM((2,), jnp.int32),
            pltpu.VMEM((2, 128), jnp.int32),
            pltpu.VMEM((2, 48), jnp.int32),
            pltpu.SMEM((1,), jnp.int32),
            pltpu.VMEM((2, GRID, GRID), bf16),
            pltpu.VMEM((2, GRID, N_PME * ROWS_Y), bf16),
            pltpu.VMEM((2, N_PME * ROWS_Y, GRID), bf16),
            pltpu.SemaphoreType.DMA((9,)),
            pltpu.VMEM((3, 2, 8, 128), f32),
            pltpu.VMEM((GRID, ATOMS), bf16),
            pltpu.VMEM((GRID, ATOMS), bf16),
            pltpu.VMEM((GRID, ATOMS), bf16),
            pltpu.VMEM((GRID, ATOMS), bf16),
            pltpu.VMEM((N_PME, ROWS_Y, 128), f32),
            pltpu.VMEM((N_PME, ROWS_Y, 128), f32),
            pltpu.VMEM((RING_Z, RING_Y, 4, 128), f32),
            pltpu.VMEM((RING_Y, RING_Z, 4, 128), f32),
            pltpu.VMEM((RING_Z, RING_Y, 4, 128), f32),
            pltpu.VMEM((RING_Z, RING_Y, 4, 128), f32),
            pltpu.VMEM((RING_Z, RING_Y, 4, 128), f32),
            pltpu.VMEM((RING_Z, RING_Y, 4, 128), f32),
            pltpu.VMEM((N_PME, ROWS_Y, 128), f32),
            pltpu.VMEM((N_PME, ROWS_Y, 128), f32),
            pltpu.VMEM((2, 8, 128), f32),
            pltpu.VMEM((2, 8, 128), f32),
            pltpu.VMEM((GRID, 128), f32),
            pltpu.VMEM((2, 8, 128), f32),
            two,
            two,
            one,
            one,
            one,
            one,
            one,
            one,
            one,
            one,
            one,
            one,
            one,
            one,
            two,
            two,
        ],
        compiler_params=pltpu.CompilerParams(
            collective_id=0, has_side_effects=True, vmem_limit_bytes=48 * 1024 * 1024
        ),
    )(
        *(
            value if value is pair_count else pltpu.with_memory_space_constraint(value, pltpu.HBM)
            for value in (
                positions.transpose(1, 0, 2),
                charges,
                counts,
                mol_ids,
                pair_blocks.T,
                pair_count,
                *constants,
            )
        )
    )
    return forces.transpose(1, 0, 2)


def solution(mesh):
    in_specs = (
        P(("dom", "pme"), None, None),
        P(("dom", "pme"), None),
        P(("dom", "pme")),
        P(("dom", "pme"), None),
        P(("dom", "pme"), None),
        P(("dom", "pme")),
    )
    out_specs = P(("dom", "pme"), None, None)
    return jax.shard_map(
        per_device, mesh=mesh, in_specs=in_specs, out_specs=out_specs, check_vma=False
    )
```

```python
import functools
import math

import jax
import jax.numpy as jnp
import ml_dtypes
import numpy as np
from jax import lax
from jax.experimental import pallas as pl
from jax.experimental.pallas import tpu as pltpu
from jax.sharding import PartitionSpec as P

GRID = 256
N_DOM = 64
RING_Y = 4
RING_Z = 16
N_PME = 8
SX = 4
SY = 32
ROWS_Y = 40
FLAT = SX * ROWS_Y
ATOMS = 768
MESH = pl.DeviceIdType.MESH

coulomb = 8.0
sigma_six = 2.5**6
well_depth = 0.5
core_alpha = 0.5
recip_scale = 6.0
f32 = jnp.float32
bf16 = jnp.bfloat16

SPANS = (((0, 144, 0), (240, 256, -256)), ((112, 256, 0), (0, 16, 256)))

LANES = (256, 0, 512)

NN = (((1,), (0,)), ((), ()))
NT = (((1,), (1,)), ((), ()))


def split(value):
    high = value.astype(bf16)
    return high, (value - high.astype(f32)).astype(bf16)


def product(left, right, dims=NN):
    def one(a, b):
        return lax.dot_general(a, b, dims, preferred_element_type=f32)

    return one(left[0], right[0]) + (one(left[0], right[1]) + one(left[1], right[0]))


def lane_group(shape):
    return lax.shift_right_logical(lax.broadcasted_iota(jnp.int32, shape, 1), 5)


def swap_groups(pieces):
    group = lane_group((1, 128))
    out = []
    for j in range(4):
        total = pieces[j]
        for i in range(4):
            if i != j:
                total = jnp.where(group == i, pltpu.roll(pieces[i], 32 * ((i - j) % 4), 1), total)
        out.append(total)
    return out


def bumps(delta):
    away = jnp.abs(delta)
    return [jnp.maximum(top - away, 0.0) for top in (3.0, 2.0, 1.0)]


def weight(delta):
    total = 0.0
    for part, factor in zip(bumps(delta), (1.0, -6.0, 15.0)):
        square = part * part
        total = total + (factor / 120.0) * (square * square * part)
    return total


def slope(delta):
    total = 0.0
    for part, factor in zip(bumps(delta), (1.0, -6.0, 15.0)):
        square = part * part
        total = total + (factor / 24.0) * (square * square)
    return jnp.where(delta > 0.0, -total, total)


def scaled_erfc(z):
    t = 1.0 / (1.0 + 0.5 * z)
    poly = 0.17087277
    for c in (
        -0.82215223,
        1.48851587,
        -1.13520398,
        0.27886807,
        -0.18628806,
        0.09678418,
        0.37409196,
        1.00002368,
        -1.26551223,
    ):
        poly = poly * t + c
    return t * jnp.exp(poly)


def pair_scalar(parts, left, right):
    dist_sq = parts[0] * parts[0] + parts[1] * parts[1] + parts[2] * parts[2]
    soft_sq = dist_sq + 1.0
    inv = lax.rsqrt(soft_sq)
    inv_sq = inv * inv
    gauss = jnp.exp(-soft_sq)
    charge = coulomb * left[3] * right[3]
    whole = (
        charge * gauss * (scaled_erfc(soft_sq * inv) * inv + 2.0 / math.sqrt(math.pi)) * inv_sq
    )
    inv_hard = 1.0 / (core_alpha * sigma_six + dist_sq * dist_sq * dist_sq)
    ratio = sigma_six * inv_hard
    dispersion = 24.0 * well_depth * dist_sq * dist_sq * (2.0 * ratio - 1.0) * ratio * inv_hard
    other = jnp.where(left[4] == right[4], -charge * inv * inv_sq, dispersion)
    return left[5] * right[5] * (whole + other)


def kernel(
    pos_in,
    charges_in,
    counts_in,
    mols_in,
    pairs_in,
    listed_in,
    h_in,
    y_in,
    yt_in,
    out,
    pos,
    charges,
    counts,
    mols,
    pairs,
    listed,
    h,
    y,
    yt,
    in_s,
    at,
    wz_hi,
    wz_lo,
    dz_hi,
    dz_lo,
    sp,
    rp,
    sd,
    rd,
    sd2,
    rd2,
    sq,
    rq,
    fs,
    fr,
    lam,
    short,
    column_s,
    halo_s,
    halo_r,
    p1_s,
    p1_r,
    d1_s,
    d1_r,
    d2_s,
    d2_r,
    p2_s,
    p2_r,
    f_s,
    f_r,
):
    me_d = lax.axis_index("dom")
    me_p = lax.axis_index("pme")
    up = lax.rem(me_d + 1, N_DOM)
    down = lax.rem(me_d + N_DOM - 1, N_DOM)

    inputs = [
        pltpu.make_async_copy(source, target, in_s.at[i])
        for i, (source, target) in enumerate(
            (
                (pos_in, pos),
                (charges_in, charges),
                (counts_in, counts),
                (mols_in, mols),
                (pairs_in, pairs),
                (listed_in, listed),
                (h_in, h),
                (y_in, y),
                (yt_in, yt),
            )
        )
    ]
    for copy in inputs[:4]:
        copy.start()

    barrier = pltpu.get_barrier_semaphore()
    for other in (up, down):
        pl.semaphore_signal(barrier, inc=1, device_id=(other, me_p), device_id_type=MESH)

    def pme_at(k):
        there = me_p + k
        return jnp.where(there >= N_PME, there - N_PME, there)

    def dom_at(k):
        there = me_d + k
        return jnp.where(there >= N_DOM, there - N_DOM, there)

    def y_mate(k):
        own_y = lax.rem(me_d, RING_Y)
        return me_d - own_y + lax.rem(own_y + k, RING_Y)

    for k in range(1, N_PME):
        pl.semaphore_signal(barrier, inc=1, device_id=(me_d, pme_at(k)), device_id_type=MESH)

    for k in range(1, RING_Y):
        pl.semaphore_signal(barrier, inc=1, device_id=(y_mate(k), me_p), device_id_type=MESH)
    for k in range(1, RING_Z):
        pl.semaphore_signal(
            barrier, inc=1, device_id=(dom_at(RING_Y * k), me_p), device_id_type=MESH
        )

    def far_first(visit, nearest):
        visit(N_DOM // 2)
        for j in range(1, 8):
            visit(N_DOM // 2 - j)
            visit(N_DOM // 2 + j)

        def body(step, carry):
            for j in range(8):
                visit(N_DOM // 2 - 8 * step - j)
                visit(N_DOM // 2 + 8 * step + j)
            return carry

        lax.fori_loop(1, 3, body, 0)
        for j in range(24, N_DOM // 2 + 1 - nearest):
            visit(N_DOM // 2 - j)
            visit(N_DOM // 2 + j)


    for copy in inputs[4:]:
        copy.start()
    for copy in inputs[:4]:
        copy.wait()
    lane = lax.broadcasted_iota(jnp.int32, (1, 128), 1)
    for b in range(2):
        live = (lane < counts[b]).astype(f32)
        for v in range(3):
            at[1, b, v : v + 1, :] = pos[v, b : b + 1, :]
        at[1, b, 3:4, :] = charges[b : b + 1, :] * live
        at[1, b, 4:5, :] = mols[b : b + 1, :].astype(f32)
        at[1, b, 5:6, :] = live
        at[1, b, 6:8, :] = jnp.zeros((2, 128), f32)

    pl.semaphore_wait(barrier, 2 + N_PME - 1 + RING_Y - 1 + RING_Z - 1)

    to_up = pltpu.make_async_remote_copy(
        src_ref=at.at[1],
        dst_ref=at.at[0],
        send_sem=halo_s.at[0],
        recv_sem=halo_r.at[0],
        device_id=(up, me_p),
        device_id_type=MESH,
    )
    to_down = pltpu.make_async_remote_copy(
        src_ref=at.at[1],
        dst_ref=at.at[2],
        send_sem=halo_s.at[1],
        recv_sem=halo_r.at[1],
        device_id=(down, me_p),
        device_id_type=MESH,
    )
    to_up.start()
    to_down.start()
    for k in range(1, RING_Y):
        pl.semaphore_signal(column_s, inc=1, device_id=(y_mate(k), me_p), device_id_type=MESH)

    def fill(side, function, high_ref, low_ref):
        for b in range(2):
            first = LANES[side] + 128 * b
            coord = at[side, b, 2:3, :]
            charge = at[side, b, 3:4, :]
            for start, stop, wrap_z in SPANS[b]:
                cells = lax.broadcasted_iota(jnp.int32, (stop - start, 128), 0)
                delta = coord - (cells + (start + wrap_z)).astype(f32)
                high, low = split(function(delta) * charge)
                high_ref[start:stop, first : first + 128] = high
                low_ref[start:stop, first : first + 128] = low

    for refs in (wz_hi, wz_lo, dz_hi, dz_lo):
        for side in range(3):
            for b in range(2):
                first = LANES[side] + 128 * b
                refs[128 - 112 * b : 240 - 112 * b, first : first + 128] = jnp.zeros((112, 128), bf16)
    fill(1, weight, wz_hi, wz_lo)
    corner_x = (me_d * SX).astype(f32)
    corner_y = (me_p * SY).astype(f32)
    wrap = (
        jnp.where(me_d == 0, 256.0, 0.0).astype(f32),
        f32(0.0),
        jnp.where(me_d == N_DOM - 1, -256.0, 0.0).astype(f32),
    )
    cells_x = lax.broadcasted_iota(jnp.int32, (8, 256), 0).astype(f32)
    cells_y = lax.broadcasted_iota(jnp.int32, (ROWS_Y, 256), 0).astype(f32) - 3.0

    def deltas(side):
        flat_x = jnp.concatenate(
            [at[side, b, 0:1, :] - (wrap[side] + corner_x) for b in range(2)], axis=1
        )
        flat_y = jnp.concatenate([at[side, b, 1:2, :] - corner_y for b in range(2)], axis=1)
        return flat_x - cells_x, flat_y - cells_y

    def spread(sides):
        planes = []
        for side in sides:
            delta_x, delta_y = deltas(side)
            wx, wy = weight(delta_x), weight(delta_y)
            planes.append(jnp.concatenate([wx[x : x + 1] * wy for x in range(SX)], axis=0))
        span = slice(LANES[sides[0]], LANES[sides[-1]] + 256)
        loaded = (wz_hi[:, span], wz_lo[:, span])
        return product(split(jnp.concatenate(planes, axis=1)), loaded, NT)

    mesh = spread((1,))
    to_up.wait_recv()
    to_down.wait_recv()
    fill(0, weight, wz_hi, wz_lo)
    fill(2, weight, wz_hi, wz_lo)
    mesh = mesh + spread((0, 2))
    inputs[6].wait()
    table = (h[0], h[1])
    depth = product(split(mesh), table)
    for half in range(2):
        pieces = [
            depth[ROWS_Y * x : ROWS_Y * (x + 1), 128 * half : 128 * (half + 1)] for x in range(SX)
        ]
        for g, piece in enumerate(swap_groups(pieces)):
            sp[4 * half + g] = piece

    def pme_copy(source, target, k, send, receive):
        other = pme_at(k)
        return pltpu.make_async_remote_copy(
            src_ref=source.at[other],
            dst_ref=target.at[me_p],
            send_sem=send,
            recv_sem=receive,
            device_id=(me_d, other),
            device_id_type=MESH,
        )

    def pme_all(source, target, send, receive):
        return pltpu.make_async_remote_copy(
            src_ref=source.at[pl.ds(0, N_PME - 1)],
            dst_ref=target.at[pl.ds(0, N_PME - 1)],
            send_sem=send,
            recv_sem=receive,
            device_id=(me_d, pme_at(1)),
            device_id_type=MESH,
        )

    def dom_copy(source, target, k, send, receive):
        other = dom_at(k)
        return pltpu.make_async_remote_copy(
            src_ref=source.at[other],
            dst_ref=target.at[me_d],
            send_sem=send,
            recv_sem=receive,
            device_id=(other, me_p),
            device_id_type=MESH,
        )

    def dom_all(source, target, send, receive):
        return pltpu.make_async_remote_copy(
            src_ref=source.at[pl.ds(0, N_DOM - 1)],
            dst_ref=target.at[pl.ds(0, N_DOM - 1)],
            send_sem=send,
            recv_sem=receive,
            device_id=(up, me_p),
            device_id_type=MESH,
        )

    def start_pme(source, target, send, receive):
        for k in (4, 3, 5, 2, 6, 7, 1):
            pme_copy(source, target, k, send, receive).start()

    def start_dom(source, target, send, receive):
        far_first(lambda k: dom_copy(source, target, k, send, receive).start(), 1)

    start_pme(sp, rp, p1_s, p1_r)
    rp[me_p] = sp[me_p]

    for side in range(3):
        fill(side, slope, dz_hi, dz_lo)

    inputs[7].wait()
    pme_all(sp, rp, p1_s, p1_r).wait_recv()
    lines = product(
        (y[0], y[1]), split(rp[...].reshape(N_PME * ROWS_Y, 128))
    )
    flat_sd = sd.reshape(GRID, 128)
    for x, piece in enumerate(swap_groups([lines[64 * k : 64 * (k + 1)] for k in range(4)])):
        flat_sd[pl.ds(x, 64, stride=4), :] = piece
    pl.semaphore_wait(column_s, RING_Y - 1)
    start_dom(sd, rd, d1_s, d1_r)
    rd[me_d] = sd[me_d]

    def folded(index):
        return jnp.where(index < GRID // 2, index, index - GRID).astype(f32) * (1.0 / GRID)

    freq_x = folded(lax.broadcasted_iota(jnp.int32, (GRID, 128), 0))
    freq_y = folded(me_d * 4 + lane_group((1, 128)))
    freq_z = folded(me_p * 32 + lane - 32 * lane_group((1, 128)))
    wave = freq_x * freq_x + (freq_y * freq_y + freq_z * freq_z)
    safe = jnp.where(wave > 0.0, wave, 1.0)
    lam[...] = jnp.where(
        wave > 0.0, (recip_scale / GRID**3) * jnp.exp(-(math.pi**2) * safe) / safe, 0.0
    )

    dom_all(sd, rd, d1_s, d1_r).wait_recv()
    spectrum = product(table, split(rd.reshape(GRID, 128)[...])) * lam[...]
    sd2.reshape(GRID, 128)[...] = product(table, split(spectrum))
    start_dom(sd2, rd2, d2_s, d2_r)
    rd2[me_d] = sd2[me_d]

    padded = jnp.concatenate([at[1, 0], at[1, 1], jnp.zeros((112, 128), f32)], axis=0)
    columns = padded.T
    inputs[4].wait()
    inputs[5].wait()
    rows = lax.broadcasted_iota(jnp.int32, (1, 48), 1)
    sublane = lax.broadcasted_iota(jnp.int32, (128, 128), 1)
    on_own = jnp.zeros((128, 128), f32)
    on_above = [[0.0] * 3, [0.0] * 3]
    for a in range(2):
        left = [columns[:, 8 * a + r : 8 * a + r + 1] for r in range(6)]
        on_left = [0.0] * 3
        for c in range(2):
            right = [at[2, c, r : r + 1, :] for r in range(6)]
            hit = (rows < listed[0]) & (pairs[0:1, :] == a) & (pairs[1:2, :] == c)
            times = jnp.sum(hit.astype(f32), axis=1, keepdims=True)
            dz = left[2] - right[2]
            if a < c:
                dz = jnp.where(dz < -128.0, dz + 256.0, dz)
            if a > c:
                dz = jnp.where(dz >= 128.0, dz - 256.0, dz)
            parts = [left[0] - (right[0] - wrap[2]), left[1] - right[1], dz]
            scalar = pair_scalar(parts, left, right) * times
            for v in range(3):
                force = scalar * parts[v]
                on_left[v] = on_left[v] + force
                on_above[c][v] = on_above[c][v] - jnp.sum(force, axis=0, keepdims=True)
        for v in range(3):
            on_own = jnp.where(
                sublane == 3 * a + v, jnp.sum(on_left[v], axis=1, keepdims=True), on_own
            )
    short[0] = on_own.T[0:8]
    short[1] = jnp.concatenate(on_above[0] + on_above[1] + [jnp.zeros((2, 128), f32)], axis=0)

    weights_x, slopes_x, weights_y, slopes_y = [], [], [], []
    for side in range(3):
        delta_x, delta_y = deltas(side)
        weights_x.append(weight(delta_x))
        slopes_x.append(slope(delta_x))
        weights_y.append(weight(delta_y))
        slopes_y.append(slope(delta_y))
    for high_ref, low_ref in ((wz_hi, wz_lo), (dz_hi, dz_lo)):
        high, low = split(product(table, (high_ref[...], low_ref[...])))
        high_ref[...] = high
        low_ref[...] = low

    inputs[8].wait()

    dom_all(sd2, rd2, d2_s, d2_r).wait_recv()
    flat_rd2 = rd2.reshape(GRID, 128)
    lines = jnp.concatenate(
        swap_groups([flat_rd2[pl.ds(x, 64, stride=4), :] for x in range(4)]), axis=0
    )
    sq[...] = product((yt[0], yt[1]), split(lines)).reshape(N_PME, ROWS_Y, 128)
    start_pme(sq, rq, p2_s, p2_r)
    rq[me_p] = sq[me_p]

    pme_all(sq, rq, p2_s, p2_r).wait_recv()
    halves = [swap_groups([rq[4 * half + g] for g in range(4)]) for half in range(2)]
    depth = jnp.concatenate(
        [jnp.concatenate([halves[0][x], halves[1][x]], axis=1) for x in range(SX)], axis=0
    )
    lines = split(depth)

    def force_rows(side):
        span = slice(LANES[side], LANES[side] + 256)
        base = 32 if side == 2 else 0
        spectrum = [part[base : base + (FLAT if side == 1 else 128)] for part in lines]
        along = product(spectrum, (wz_hi[:, span], wz_lo[:, span]))
        along_slope = product(spectrum, (dz_hi[:, span], dz_lo[:, span]))
        wx, dx, wy, dy = weights_x[side], slopes_x[side], weights_y[side], slopes_y[side]
        field = [0.0] * 3
        for x in ((0, 1, 2), (0, 1, 2, 3), (1, 2, 3))[side]:
            here = along[ROWS_Y * x - base : ROWS_Y * (x + 1) - base]
            there = along_slope[ROWS_Y * x - base : ROWS_Y * (x + 1) - base]
            field[0] = field[0] - dx[x : x + 1] * jnp.sum(wy * here, axis=0, keepdims=True)
            field[1] = field[1] - wx[x : x + 1] * jnp.sum(dy * here, axis=0, keepdims=True)
            field[2] = field[2] - wx[x : x + 1] * jnp.sum(wy * there, axis=0, keepdims=True)
        return jnp.concatenate(
            [field[v][:, 128 * b : 128 * (b + 1)] for b in range(2) for v in range(3)]
            + [jnp.zeros((2, 128), f32)],
            axis=0,
        )

    send_down = pltpu.make_async_remote_copy(
        src_ref=fs.at[0],
        dst_ref=fr.at[0],
        send_sem=f_s.at[0],
        recv_sem=f_r.at[0],
        device_id=(down, me_p),
        device_id_type=MESH,
    )
    send_up = pltpu.make_async_remote_copy(
        src_ref=fs.at[1],
        dst_ref=fr.at[1],
        send_sem=f_s.at[1],
        recv_sem=f_r.at[1],
        device_id=(up, me_p),
        device_id_type=MESH,
    )
    fs[0] = force_rows(0)
    send_down.start()
    fs[1] = force_rows(2) + short[1]
    send_up.start()
    total = force_rows(1) + short[0]

    to_up.wait_send()
    to_down.wait_send()
    pme_all(sp, rp, p1_s, p1_r).wait_send()
    dom_all(sd, rd, d1_s, d1_r).wait_send()
    dom_all(sd2, rd2, d2_s, d2_r).wait_send()
    pme_all(sq, rq, p2_s, p2_r).wait_send()
    send_down.wait_recv()
    send_up.wait_recv()
    total = total + fr[0] + fr[1]
    for v in range(3):
        for b in range(2):
            out[v, b : b + 1, :] = total[3 * b + v : 3 * b + v + 1]
    send_down.wait_send()
    send_up.wait_send()


def two_parts(table):
    high = table.astype(ml_dtypes.bfloat16)
    low = (table - high.astype(np.float64)).astype(ml_dtypes.bfloat16)
    return np.stack([high, low])


def cas(first, second):
    angle = 2.0 * np.pi / GRID * (np.outer(first, second) % GRID)
    return np.cos(angle) + np.sin(angle)


def tables():
    index = np.arange(GRID)
    square = cas(index, index)
    freq = (4 * np.arange(64)[None, :] + np.arange(4)[:, None]).reshape(-1)
    cell = np.arange(ROWS_Y) - 3
    cells = (SY * np.arange(N_PME)[:, None] + cell[None, :]).reshape(-1)
    real = np.tile(np.arange(ROWS_Y) < SY + 6, N_PME)
    lines = cas(freq, cells % GRID) * real[None, :]
    return [two_parts(square), two_parts(lines), two_parts(lines.T)]


def per_device(positions, charges, counts, mol_ids, pair_blocks, pair_count):
    one = pltpu.SemaphoreType.DMA
    two = pltpu.SemaphoreType.DMA((2,))
    constants = [jnp.asarray(t) for t in tables()]
    forces = pl.pallas_call(
        kernel,
        out_shape=pltpu.VMEM((3, 2, 128), f32),
        in_specs=[pl.BlockSpec(memory_space=pltpu.HBM)] * 9,
        out_specs=pl.BlockSpec(memory_space=pltpu.VMEM),
        scratch_shapes=[
            pltpu.VMEM((3, 2, 128), f32),
            pltpu.VMEM((2, 128), f32),
            pltpu.SMEM((2,), jnp.int32),
            pltpu.VMEM((2, 128), jnp.int32),
            pltpu.VMEM((2, 48), jnp.int32),
            pltpu.SMEM((1,), jnp.int32),
            pltpu.VMEM((2, GRID, GRID), bf16),
            pltpu.VMEM((2, GRID, N_PME * ROWS_Y), bf16),
            pltpu.VMEM((2, N_PME * ROWS_Y, GRID), bf16),
            pltpu.SemaphoreType.DMA((9,)),
            pltpu.VMEM((3, 2, 8, 128), f32),
            pltpu.VMEM((GRID, ATOMS), bf16),
            pltpu.VMEM((GRID, ATOMS), bf16),
            pltpu.VMEM((GRID, ATOMS), bf16),
            pltpu.VMEM((GRID, ATOMS), bf16),
            pltpu.VMEM((N_PME, ROWS_Y, 128), f32),
            pltpu.VMEM((N_PME, ROWS_Y, 128), f32),
            pltpu.VMEM((N_DOM, 4, 128), f32),
            pltpu.VMEM((N_DOM, 4, 128), f32),
            pltpu.VMEM((N_DOM, 4, 128), f32),
            pltpu.VMEM((N_DOM, 4, 128), f32),
            pltpu.VMEM((N_PME, ROWS_Y, 128), f32),
            pltpu.VMEM((N_PME, ROWS_Y, 128), f32),
            pltpu.VMEM((2, 8, 128), f32),
            pltpu.VMEM((2, 8, 128), f32),
            pltpu.VMEM((GRID, 128), f32),
            pltpu.VMEM((2, 8, 128), f32),
            pltpu.SemaphoreType.REGULAR,
            two,
            two,
            one,
            one,
            one,
            one,
            one,
            one,
            one,
            one,
            two,
            two,
        ],
        compiler_params=pltpu.CompilerParams(
            collective_id=0, has_side_effects=True, vmem_limit_bytes=48 * 1024 * 1024
        ),
    )(
        *(
            value if value is pair_count else pltpu.with_memory_space_constraint(value, pltpu.HBM)
            for value in (
                positions.transpose(1, 0, 2),
                charges,
                counts,
                mol_ids,
                pair_blocks.T,
                pair_count,
                *constants,
            )
        )
    )
    return forces.transpose(1, 0, 2)


def solution(mesh):
    in_specs = (
        P(("dom", "pme"), None, None),
        P(("dom", "pme"), None),
        P(("dom", "pme")),
        P(("dom", "pme"), None),
        P(("dom", "pme"), None),
        P(("dom", "pme")),
    )
    out_specs = P(("dom", "pme"), None, None)
    return jax.shard_map(
        per_device, mesh=mesh, in_specs=in_specs, out_specs=out_specs, check_vma=False
    )
```

```python
import functools
import math

import jax
import jax.numpy as jnp
import ml_dtypes
import numpy as np
from jax import lax
from jax.experimental import pallas as pl
from jax.experimental.pallas import tpu as pltpu
from jax.sharding import PartitionSpec as P

GRID = 256
N_DOM = 64
RING_Y = 4
RING_Z = 16
N_PME = 8
SX = 4
SY = 32
ROWS_Y = 40
FLAT = SX * ROWS_Y
ATOMS = 768
MESH = pl.DeviceIdType.MESH

coulomb = 8.0
sigma_six = 2.5**6
well_depth = 0.5
core_alpha = 0.5
recip_scale = 6.0
f32 = jnp.float32
bf16 = jnp.bfloat16

SPANS = (((0, 144, 0), (240, 256, -256)), ((112, 256, 0), (0, 16, 256)))

LANES = (256, 0, 512)

NN = (((1,), (0,)), ((), ()))
NT = (((1,), (1,)), ((), ()))


def split(value):
    high = value.astype(bf16)
    return high, (value - high.astype(f32)).astype(bf16)


def product(left, right, dims=NN):
    def one(a, b):
        return lax.dot_general(a, b, dims, preferred_element_type=f32)

    return one(left[0], right[0]) + (one(left[0], right[1]) + one(left[1], right[0]))


def lane_group(shape):
    return lax.shift_right_logical(lax.broadcasted_iota(jnp.int32, shape, 1), 5)


def swap_groups(pieces):
    group = lane_group((1, 128))
    out = []
    for j in range(4):
        total = pieces[j]
        for i in range(4):
            if i != j:
                total = jnp.where(group == i, pltpu.roll(pieces[i], 32 * ((i - j) % 4), 1), total)
        out.append(total)
    return out


def bumps(delta):
    away = jnp.abs(delta)
    return [jnp.maximum(top - away, 0.0) for top in (3.0, 2.0, 1.0)]


def weight(delta):
    total = 0.0
    for part, factor in zip(bumps(delta), (1.0, -6.0, 15.0)):
        square = part * part
        total = total + (factor / 120.0) * (square * square * part)
    return total


def slope(delta):
    total = 0.0
    for part, factor in zip(bumps(delta), (1.0, -6.0, 15.0)):
        square = part * part
        total = total + (factor / 24.0) * (square * square)
    return jnp.where(delta > 0.0, -total, total)


def scaled_erfc(z):
    t = 1.0 / (1.0 + 0.5 * z)
    poly = 0.17087277
    for c in (
        -0.82215223,
        1.48851587,
        -1.13520398,
        0.27886807,
        -0.18628806,
        0.09678418,
        0.37409196,
        1.00002368,
        -1.26551223,
    ):
        poly = poly * t + c
    return t * jnp.exp(poly)


def pair_scalar(parts, left, right):
    dist_sq = parts[0] * parts[0] + parts[1] * parts[1] + parts[2] * parts[2]
    soft_sq = dist_sq + 1.0
    inv = lax.rsqrt(soft_sq)
    inv_sq = inv * inv
    gauss = jnp.exp(-soft_sq)
    charge = coulomb * left[3] * right[3]
    whole = (
        charge * gauss * (scaled_erfc(soft_sq * inv) * inv + 2.0 / math.sqrt(math.pi)) * inv_sq
    )
    inv_hard = 1.0 / (core_alpha * sigma_six + dist_sq * dist_sq * dist_sq)
    ratio = sigma_six * inv_hard
    dispersion = 24.0 * well_depth * dist_sq * dist_sq * (2.0 * ratio - 1.0) * ratio * inv_hard
    other = jnp.where(left[4] == right[4], -charge * inv * inv_sq, dispersion)
    return left[5] * right[5] * (whole + other)


def kernel(
    pos_in,
    charges_in,
    counts_in,
    mols_in,
    pairs_in,
    listed_in,
    h_in,
    y_in,
    yt_in,
    out,
    pos,
    charges,
    counts,
    mols,
    pairs,
    listed,
    h,
    y,
    yt,
    in_s,
    at,
    wz_hi,
    wz_lo,
    dz_hi,
    dz_lo,
    sp,
    rp,
    sd,
    rd,
    sd2,
    rd2,
    sq,
    rq,
    fs,
    fr,
    lam,
    short,
    column_s,
    halo_s,
    halo_r,
    p1_s,
    p1_near,
    p1_far,
    d1_s,
    d1_r,
    d2_s,
    d2_r,
    p2_s,
    p2_near,
    p2_far,
    f_s,
    f_r,
):
    me_d = lax.axis_index("dom")
    me_p = lax.axis_index("pme")
    up = lax.rem(me_d + 1, N_DOM)
    down = lax.rem(me_d + N_DOM - 1, N_DOM)

    inputs = [
        pltpu.make_async_copy(source, target, in_s.at[i])
        for i, (source, target) in enumerate(
            (
                (pos_in, pos),
                (charges_in, charges),
                (counts_in, counts),
                (mols_in, mols),
                (pairs_in, pairs),
                (listed_in, listed),
                (h_in, h),
                (y_in, y),
                (yt_in, yt),
            )
        )
    ]
    for copy in inputs[:4]:
        copy.start()

    barrier = pltpu.get_barrier_semaphore()
    for other in (up, down):
        pl.semaphore_signal(barrier, inc=1, device_id=(other, me_p), device_id_type=MESH)

    def pme_at(k):
        there = me_p + k
        return jnp.where(there >= N_PME, there - N_PME, there)

    def dom_at(k):
        there = me_d + k
        return jnp.where(there >= N_DOM, there - N_DOM, there)

    def y_mate(k):
        own_y = lax.rem(me_d, RING_Y)
        return me_d - own_y + lax.rem(own_y + k, RING_Y)

    for k in range(1, N_PME):
        pl.semaphore_signal(barrier, inc=1, device_id=(me_d, pme_at(k)), device_id_type=MESH)

    for k in range(1, RING_Y):
        pl.semaphore_signal(barrier, inc=1, device_id=(y_mate(k), me_p), device_id_type=MESH)
    for k in range(1, RING_Z):
        pl.semaphore_signal(
            barrier, inc=1, device_id=(dom_at(RING_Y * k), me_p), device_id_type=MESH
        )

    for copy in inputs[4:]:
        copy.start()
    for copy in inputs[:4]:
        copy.wait()
    lane = lax.broadcasted_iota(jnp.int32, (1, 128), 1)
    for b in range(2):
        live = (lane < counts[b]).astype(f32)
        for v in range(3):
            at[1, b, v : v + 1, :] = pos[v, b : b + 1, :]
        at[1, b, 3:4, :] = charges[b : b + 1, :] * live
        at[1, b, 4:5, :] = mols[b : b + 1, :].astype(f32)
        at[1, b, 5:6, :] = live
        at[1, b, 6:8, :] = jnp.zeros((2, 128), f32)

    pl.semaphore_wait(barrier, 2 + N_PME - 1 + RING_Y - 1 + RING_Z - 1)

    to_up = pltpu.make_async_remote_copy(
        src_ref=at.at[1],
        dst_ref=at.at[0],
        send_sem=halo_s.at[0],
        recv_sem=halo_r.at[0],
        device_id=(up, me_p),
        device_id_type=MESH,
    )
    to_down = pltpu.make_async_remote_copy(
        src_ref=at.at[1],
        dst_ref=at.at[2],
        send_sem=halo_s.at[1],
        recv_sem=halo_r.at[1],
        device_id=(down, me_p),
        device_id_type=MESH,
    )
    to_up.start()
    to_down.start()
    for k in range(1, RING_Y):
        pl.semaphore_signal(column_s, inc=1, device_id=(y_mate(k), me_p), device_id_type=MESH)

    def fill(side, function, high_ref, low_ref):
        for b in range(2):
            first = LANES[side] + 128 * b
            coord = at[side, b, 2:3, :]
            charge = at[side, b, 3:4, :]
            for start, stop, wrap_z in SPANS[b]:
                cells = lax.broadcasted_iota(jnp.int32, (stop - start, 128), 0)
                delta = coord - (cells + (start + wrap_z)).astype(f32)
                high, low = split(function(delta) * charge)
                high_ref[start:stop, first : first + 128] = high
                low_ref[start:stop, first : first + 128] = low

    for refs in (wz_hi, wz_lo, dz_hi, dz_lo):
        for side in range(3):
            for b in range(2):
                first = LANES[side] + 128 * b
                refs[128 - 112 * b : 240 - 112 * b, first : first + 128] = jnp.zeros((112, 128), bf16)
    fill(1, weight, wz_hi, wz_lo)
    corner_x = (me_d * SX).astype(f32)
    corner_y = (me_p * SY).astype(f32)
    wrap = (
        jnp.where(me_d == 0, 256.0, 0.0).astype(f32),
        f32(0.0),
        jnp.where(me_d == N_DOM - 1, -256.0, 0.0).astype(f32),
    )
    cells_x = lax.broadcasted_iota(jnp.int32, (8, 256), 0).astype(f32)
    cells_y = lax.broadcasted_iota(jnp.int32, (ROWS_Y, 256), 0).astype(f32) - 3.0

    def deltas(side):
        flat_x = jnp.concatenate(
            [at[side, b, 0:1, :] - (wrap[side] + corner_x) for b in range(2)], axis=1
        )
        flat_y = jnp.concatenate([at[side, b, 1:2, :] - corner_y for b in range(2)], axis=1)
        return flat_x - cells_x, flat_y - cells_y

    def spread(sides):
        planes = []
        for side in sides:
            delta_x, delta_y = deltas(side)
            wx, wy = weight(delta_x), weight(delta_y)
            planes.append(jnp.concatenate([wx[x : x + 1] * wy for x in range(SX)], axis=0))
        span = slice(LANES[sides[0]], LANES[sides[-1]] + 256)
        loaded = (wz_hi[:, span], wz_lo[:, span])
        return product(split(jnp.concatenate(planes, axis=1)), loaded, NT)

    mesh = spread((1,))
    to_up.wait_recv()
    to_down.wait_recv()
    fill(0, weight, wz_hi, wz_lo)
    fill(2, weight, wz_hi, wz_lo)
    mesh = mesh + spread((0, 2))
    mesh = split(mesh)
    own_half = me_p // 4
    halves = (1 - own_half, own_half)

    def send_half(source, target, half, first, send, receive):
        for k in range(first, 4):
            other = 4 * half + lax.rem(me_p + k, 4)
            pltpu.make_async_remote_copy(
                src_ref=source.at[other],
                dst_ref=target.at[me_p],
                send_sem=send,
                recv_sem=receive,
                device_id=(me_d, other),
                device_id_type=MESH,
            ).start()

    def all_of(view, send, receive):
        return pltpu.make_async_remote_copy(
            src_ref=view,
            dst_ref=view,
            send_sem=send,
            recv_sem=receive,
            device_id=(up, me_p),
            device_id_type=MESH,
        )

    own_group, in_group = me_d // 16, lax.rem(me_d, 16)
    far_groups = [lax.rem(own_group + k, 4) for k in (2, 1)]
    near_groups = [lax.rem(own_group + k, 4) for k in (3, 0)]

    def send_groups(source, target, groups, send, receive):
        def one(other):
            pltpu.make_async_remote_copy(
                src_ref=source.at[other],
                dst_ref=target.at[me_d],
                send_sem=send,
                recv_sem=receive,
                device_id=(other, me_p),
                device_id_type=MESH,
            ).start()

        def body(step, carry):
            for j in range(4):
                one(16 * groups[0] + 4 * step + j)
            return carry

        lax.fori_loop(0, 4, body, 0)
        if groups is near_groups:
            for k in range(1, 16):
                one(16 * own_group + lax.rem(in_group + k, 16))
        else:
            def last(step, carry):
                for j in range(4):
                    one(16 * groups[1] + 4 * step + j)
                return carry

            lax.fori_loop(0, 4, last, 0)

    inputs[6].wait()
    for half in halves:
        columns_z = pl.ds(pl.multiple_of(128 * half, 128), 128)
        part = product(mesh, [h[i, :, :, columns_z].reshape(GRID, 128) for i in range(2)])
        pieces = [part[ROWS_Y * x : ROWS_Y * (x + 1)] for x in range(SX)]
        for g, piece in enumerate(swap_groups(pieces)):
            sp[4 * half + g] = piece
        if half is own_half:
            send_half(sp, rp, half, 1, p1_s, p1_near)
        else:
            send_half(sp, rp, half, 0, p1_s, p1_far)
    rp[me_p] = sp[me_p]

    for side in range(3):
        fill(side, slope, dz_hi, dz_lo)

    inputs[7].wait()
    all_of(rp.at[pl.ds(0, 3)], p1_s, p1_near).wait_recv()
    all_of(rp.at[pl.ds(0, 4)], p1_s, p1_far).wait_recv()
    received = split(rp[...].reshape(N_PME * ROWS_Y, 128))
    pl.semaphore_wait(column_s, RING_Y - 1)
    flat_sd = sd.reshape(GRID, 128)
    for groups in (far_groups, near_groups):
        rows_y = [jnp.concatenate([y[i, g] for g in groups], axis=0) for i in range(2)]
        lines = product(rows_y, received)
        pieces = [
            jnp.concatenate([lines[16 * k : 16 * k + 16], lines[64 + 16 * k : 80 + 16 * k]], axis=0)
            for k in range(4)
        ]
        for x, piece in enumerate(swap_groups(pieces)):
            for i, g in enumerate(groups):
                flat_sd[pl.ds(64 * g + x, 16, stride=4), :] = piece[16 * i : 16 * (i + 1)]
        send_groups(sd, rd, groups, d1_s, d1_r)
    rd[me_d] = sd[me_d]

    def folded(index):
        return jnp.where(index < GRID // 2, index, index - GRID).astype(f32) * (1.0 / GRID)

    freq_x = folded(lax.broadcasted_iota(jnp.int32, (GRID, 128), 0))
    freq_y = folded(me_d * 4 + lane_group((1, 128)))
    freq_z = folded(me_p * 32 + lane - 32 * lane_group((1, 128)))
    wave = freq_x * freq_x + (freq_y * freq_y + freq_z * freq_z)
    safe = jnp.where(wave > 0.0, wave, 1.0)
    lam[...] = jnp.where(
        wave > 0.0, (recip_scale / GRID**3) * jnp.exp(-(math.pi**2) * safe) / safe, 0.0
    )

    table = (h[0].reshape(GRID, GRID), h[1].reshape(GRID, GRID))
    for high_ref, low_ref in ((wz_hi, wz_lo), (dz_hi, dz_lo)):
        high, low = split(product(table, (high_ref[...], low_ref[...])))
        high_ref[...] = high
        low_ref[...] = low

    all_of(rd.at[pl.ds(0, N_DOM - 1)], d1_s, d1_r).wait_recv()
    spectrum = split(product(table, split(rd.reshape(GRID, 128)[...])) * lam[...])
    flat_sd2 = sd2.reshape(GRID, 128)
    for groups in (far_groups, near_groups):
        rows_x = [jnp.concatenate([h[i, g] for g in groups], axis=0) for i in range(2)]
        lines = product(rows_x, spectrum)
        for i, g in enumerate(groups):
            flat_sd2[pl.ds(pl.multiple_of(64 * g, 64), 64), :] = lines[64 * i : 64 * (i + 1)]
        send_groups(sd2, rd2, groups, d2_s, d2_r)
    rd2[me_d] = sd2[me_d]

    padded = jnp.concatenate([at[1, 0], at[1, 1], jnp.zeros((112, 128), f32)], axis=0)
    columns = padded.T
    inputs[4].wait()
    inputs[5].wait()
    rows = lax.broadcasted_iota(jnp.int32, (1, 48), 1)
    sublane = lax.broadcasted_iota(jnp.int32, (128, 128), 1)
    on_own = jnp.zeros((128, 128), f32)
    on_above = [[0.0] * 3, [0.0] * 3]
    for a in range(2):
        left = [columns[:, 8 * a + r : 8 * a + r + 1] for r in range(6)]
        on_left = [0.0] * 3
        for c in range(2):
            right = [at[2, c, r : r + 1, :] for r in range(6)]
            hit = (rows < listed[0]) & (pairs[0:1, :] == a) & (pairs[1:2, :] == c)
            times = jnp.sum(hit.astype(f32), axis=1, keepdims=True)
            dz = left[2] - right[2]
            if a < c:
                dz = jnp.where(dz < -128.0, dz + 256.0, dz)
            if a > c:
                dz = jnp.where(dz >= 128.0, dz - 256.0, dz)
            parts = [left[0] - (right[0] - wrap[2]), left[1] - right[1], dz]
            scalar = pair_scalar(parts, left, right) * times
            for v in range(3):
                force = scalar * parts[v]
                on_left[v] = on_left[v] + force
                on_above[c][v] = on_above[c][v] - jnp.sum(force, axis=0, keepdims=True)
        for v in range(3):
            on_own = jnp.where(
                sublane == 3 * a + v, jnp.sum(on_left[v], axis=1, keepdims=True), on_own
            )
    short[0] = on_own.T[0:8]
    short[1] = jnp.concatenate(on_above[0] + on_above[1] + [jnp.zeros((2, 128), f32)], axis=0)

    inputs[8].wait()

    all_of(rd2.at[pl.ds(0, N_DOM - 1)], d2_s, d2_r).wait_recv()
    flat_rd2 = rd2.reshape(GRID, 128)
    lines = jnp.concatenate(
        swap_groups([flat_rd2[pl.ds(x, 64, stride=4), :] for x in range(4)]), axis=0
    )
    lines = split(lines)
    for half in halves:
        part = product((yt[0, half], yt[1, half]), lines)
        for g in range(4):
            sq[4 * half + g] = part[ROWS_Y * g : ROWS_Y * (g + 1)]
        if half is own_half:
            send_half(sq, rq, half, 1, p2_s, p2_near)
        else:
            send_half(sq, rq, half, 0, p2_s, p2_far)
    rq[me_p] = sq[me_p]

    weights_x, slopes_x, weights_y, slopes_y = [], [], [], []
    for side in range(3):
        delta_x, delta_y = deltas(side)
        weights_x.append(weight(delta_x))
        slopes_x.append(slope(delta_x))
        weights_y.append(weight(delta_y))
        slopes_y.append(slope(delta_y))
    all_of(rq.at[pl.ds(0, 3)], p2_s, p2_near).wait_recv()
    near = swap_groups([rq[4 * own_half + g] for g in range(4)])
    all_of(rq.at[pl.ds(0, 4)], p2_s, p2_far).wait_recv()
    far = swap_groups([rq[4 * (1 - own_half) + g] for g in range(4)])
    lines = split(
        jnp.concatenate(
            [jnp.concatenate([near[x], far[x]], axis=1) for x in range(SX)], axis=0
        )
    )

    def arrived(ref, span):
        return jnp.concatenate(
            [ref[pl.ds(pl.multiple_of(128 * half, 128), 128), span] for half in halves[::-1]], axis=0
        )

    def force_rows(side):
        span = slice(LANES[side], LANES[side] + 256)
        base = 32 if side == 2 else 0
        spectrum = [part[base : base + (FLAT if side == 1 else 128)] for part in lines]
        along = product(spectrum, (arrived(wz_hi, span), arrived(wz_lo, span)))
        along_slope = product(spectrum, (arrived(dz_hi, span), arrived(dz_lo, span)))
        wx, dx, wy, dy = weights_x[side], slopes_x[side], weights_y[side], slopes_y[side]
        field = [0.0] * 3
        for x in ((0, 1, 2), (0, 1, 2, 3), (1, 2, 3))[side]:
            here = along[ROWS_Y * x - base : ROWS_Y * (x + 1) - base]
            there = along_slope[ROWS_Y * x - base : ROWS_Y * (x + 1) - base]
            field[0] = field[0] - dx[x : x + 1] * jnp.sum(wy * here, axis=0, keepdims=True)
            field[1] = field[1] - wx[x : x + 1] * jnp.sum(dy * here, axis=0, keepdims=True)
            field[2] = field[2] - wx[x : x + 1] * jnp.sum(wy * there, axis=0, keepdims=True)
        return jnp.concatenate(
            [field[v][:, 128 * b : 128 * (b + 1)] for b in range(2) for v in range(3)]
            + [jnp.zeros((2, 128), f32)],
            axis=0,
        )

    send_down = pltpu.make_async_remote_copy(
        src_ref=fs.at[0],
        dst_ref=fr.at[0],
        send_sem=f_s.at[0],
        recv_sem=f_r.at[0],
        device_id=(down, me_p),
        device_id_type=MESH,
    )
    send_up = pltpu.make_async_remote_copy(
        src_ref=fs.at[1],
        dst_ref=fr.at[1],
        send_sem=f_s.at[1],
        recv_sem=f_r.at[1],
        device_id=(up, me_p),
        device_id_type=MESH,
    )
    fs[0] = force_rows(0)
    send_down.start()
    fs[1] = force_rows(2) + short[1]
    send_up.start()
    total = force_rows(1) + short[0]

    to_up.wait_send()
    to_down.wait_send()
    all_of(sp.at[pl.ds(0, N_PME - 1)], p1_s, p1_near).wait_send()
    all_of(sd.at[pl.ds(0, N_DOM - 1)], d1_s, d1_r).wait_send()
    all_of(sd2.at[pl.ds(0, N_DOM - 1)], d2_s, d2_r).wait_send()
    all_of(sq.at[pl.ds(0, N_PME - 1)], p2_s, p2_near).wait_send()
    send_down.wait_recv()
    send_up.wait_recv()
    total = total + fr[0] + fr[1]
    for v in range(3):
        for b in range(2):
            out[v, b : b + 1, :] = total[3 * b + v : 3 * b + v + 1]
    send_down.wait_send()
    send_up.wait_send()


def two_parts(table):
    high = table.astype(ml_dtypes.bfloat16)
    low = (table - high.astype(np.float64)).astype(ml_dtypes.bfloat16)
    return np.stack([high, low])


def cas(first, second):
    angle = 2.0 * np.pi / GRID * (np.outer(first, second) % GRID)
    return np.cos(angle) + np.sin(angle)


def tables():
    index = np.arange(GRID)
    square = cas(index, index)
    freq = (64 * np.arange(4)[:, None, None] + np.arange(4)[:, None] + 4 * np.arange(16)).reshape(-1)
    cell = np.arange(ROWS_Y) - 3
    cells = (SY * np.arange(N_PME)[:, None] + cell[None, :]).reshape(-1)
    real = np.tile(np.arange(ROWS_Y) < SY + 6, N_PME)
    lines = cas(freq, cells % GRID) * real[None, :]
    turned = lines.reshape(4, 4, 16, -1).transpose(1, 0, 2, 3).reshape(GRID, -1).T
    return [
        two_parts(square).reshape(2, 4, 64, GRID),
        two_parts(lines).reshape(2, 4, 64, -1),
        two_parts(turned).reshape(2, 2, 4 * ROWS_Y, GRID),
    ]


def per_device(positions, charges, counts, mol_ids, pair_blocks, pair_count):
    one = pltpu.SemaphoreType.DMA
    two = pltpu.SemaphoreType.DMA((2,))
    constants = [jnp.asarray(t) for t in tables()]
    forces = pl.pallas_call(
        kernel,
        out_shape=pltpu.VMEM((3, 2, 128), f32),
        in_specs=[pl.BlockSpec(memory_space=pltpu.HBM)] * 9,
        out_specs=pl.BlockSpec(memory_space=pltpu.VMEM),
        scratch_shapes=[
            pltpu.VMEM((3, 2, 128), f32),
            pltpu.VMEM((2, 128), f32),
            pltpu.SMEM((2,), jnp.int32),
            pltpu.VMEM((2, 128), jnp.int32),
            pltpu.VMEM((2, 48), jnp.int32),
            pltpu.SMEM((1,), jnp.int32),
            pltpu.VMEM((2, 4, 64, GRID), bf16),
            pltpu.VMEM((2, 4, 64, N_PME * ROWS_Y), bf16),
            pltpu.VMEM((2, 2, 4 * ROWS_Y, GRID), bf16),
            pltpu.SemaphoreType.DMA((9,)),
            pltpu.VMEM((3, 2, 8, 128), f32),
            pltpu.VMEM((GRID, ATOMS), bf16),
            pltpu.VMEM((GRID, ATOMS), bf16),
            pltpu.VMEM((GRID, ATOMS), bf16),
            pltpu.VMEM((GRID, ATOMS), bf16),
            pltpu.VMEM((N_PME, ROWS_Y, 128), f32),
            pltpu.VMEM((N_PME, ROWS_Y, 128), f32),
            pltpu.VMEM((N_DOM, 4, 128), f32),
            pltpu.VMEM((N_DOM, 4, 128), f32),
            pltpu.VMEM((N_DOM, 4, 128), f32),
            pltpu.VMEM((N_DOM, 4, 128), f32),
            pltpu.VMEM((N_PME, ROWS_Y, 128), f32),
            pltpu.VMEM((N_PME, ROWS_Y, 128), f32),
            pltpu.VMEM((2, 8, 128), f32),
            pltpu.VMEM((2, 8, 128), f32),
            pltpu.VMEM((GRID, 128), f32),
            pltpu.VMEM((2, 8, 128), f32),
            pltpu.SemaphoreType.REGULAR,
            two,
            two,
            one,
            one,
            one,
            one,
            one,
            one,
            one,
            one,
            one,
            one,
            two,
            two,
        ],
        compiler_params=pltpu.CompilerParams(
            collective_id=0, has_side_effects=True, vmem_limit_bytes=48 * 1024 * 1024
        ),
    )(
        *(
            value if value is pair_count else pltpu.with_memory_space_constraint(value, pltpu.HBM)
            for value in (
                positions.transpose(1, 0, 2),
                charges,
                counts,
                mol_ids,
                pair_blocks.T,
                pair_count,
                *constants,
            )
        )
    )
    return forces.transpose(1, 0, 2)


def solution(mesh):
    in_specs = (
        P(("dom", "pme"), None, None),
        P(("dom", "pme"), None),
        P(("dom", "pme")),
        P(("dom", "pme"), None),
        P(("dom", "pme"), None),
        P(("dom", "pme")),
    )
    out_specs = P(("dom", "pme"), None, None)
    return jax.shard_map(
        per_device, mesh=mesh, in_specs=in_specs, out_specs=out_specs, check_vma=False
    )
```

```python
import functools
import math

import jax
import jax.numpy as jnp
import ml_dtypes
import numpy as np
from jax import lax
from jax.experimental import pallas as pl
from jax.experimental.pallas import tpu as pltpu
from jax.sharding import PartitionSpec as P

GRID = 256
N_DOM = 64
RING_Y = 4
RING_Z = 16
N_PME = 8
SX = 4
SY = 32
ROWS_Y = 40
FLAT = SX * ROWS_Y
ATOMS = 768
MESH = pl.DeviceIdType.MESH

coulomb = 8.0
sigma_six = 2.5**6
well_depth = 0.5
core_alpha = 0.5
recip_scale = 6.0
f32 = jnp.float32
bf16 = jnp.bfloat16

SPANS = (((0, 144, 0), (240, 256, -256)), ((112, 256, 0), (0, 16, 256)))

LANES = (256, 0, 512)

NN = (((1,), (0,)), ((), ()))
NT = (((1,), (1,)), ((), ()))


def split(value):
    high = value.astype(bf16)
    return high, (value - high.astype(f32)).astype(bf16)


def product(left, right, dims=NN):
    def one(a, b):
        return lax.dot_general(a, b, dims, preferred_element_type=f32)

    return one(left[0], right[0]) + (one(left[0], right[1]) + one(left[1], right[0]))


def lane_group(shape):
    return lax.shift_right_logical(lax.broadcasted_iota(jnp.int32, shape, 1), 5)


def swap_groups(pieces):
    group = lane_group((1, 128))
    out = []
    for j in range(4):
        total = pieces[j]
        for i in range(4):
            if i != j:
                total = jnp.where(group == i, pltpu.roll(pieces[i], 32 * ((i - j) % 4), 1), total)
        out.append(total)
    return out


def bumps(delta):
    away = jnp.abs(delta)
    return [jnp.maximum(top - away, 0.0) for top in (3.0, 2.0, 1.0)]


def weight(delta):
    total = 0.0
    for part, factor in zip(bumps(delta), (1.0, -6.0, 15.0)):
        square = part * part
        total = total + (factor / 120.0) * (square * square * part)
    return total


def slope(delta):
    total = 0.0
    for part, factor in zip(bumps(delta), (1.0, -6.0, 15.0)):
        square = part * part
        total = total + (factor / 24.0) * (square * square)
    return jnp.where(delta > 0.0, -total, total)


def scaled_erfc(z):
    t = 1.0 / (1.0 + 0.5 * z)
    poly = 0.17087277
    for c in (
        -0.82215223,
        1.48851587,
        -1.13520398,
        0.27886807,
        -0.18628806,
        0.09678418,
        0.37409196,
        1.00002368,
        -1.26551223,
    ):
        poly = poly * t + c
    return t * jnp.exp(poly)


def pair_scalar(parts, left, right):
    dist_sq = parts[0] * parts[0] + parts[1] * parts[1] + parts[2] * parts[2]
    soft_sq = dist_sq + 1.0
    inv = lax.rsqrt(soft_sq)
    inv_sq = inv * inv
    gauss = jnp.exp(-soft_sq)
    charge = coulomb * left[3] * right[3]
    whole = (
        charge * gauss * (scaled_erfc(soft_sq * inv) * inv + 2.0 / math.sqrt(math.pi)) * inv_sq
    )
    inv_hard = 1.0 / (core_alpha * sigma_six + dist_sq * dist_sq * dist_sq)
    ratio = sigma_six * inv_hard
    dispersion = 24.0 * well_depth * dist_sq * dist_sq * (2.0 * ratio - 1.0) * ratio * inv_hard
    other = jnp.where(left[4] == right[4], -charge * inv * inv_sq, dispersion)
    return left[5] * right[5] * (whole + other)


def kernel(
    pos_in,
    charges_in,
    counts_in,
    mols_in,
    pairs_in,
    listed_in,
    h_in,
    y_in,
    yt_in,
    out,
    pos,
    charges,
    counts,
    mols,
    pairs,
    listed,
    h,
    y,
    yt,
    in_s,
    at,
    wz_hi,
    wz_lo,
    dz_hi,
    dz_lo,
    sp,
    rp,
    sd,
    rd,
    sd2,
    rd2,
    sq,
    rq,
    fs,
    fr,
    lam,
    short,
    column_s,
    halo_s,
    halo_r,
    p1_s,
    p1_near,
    p1_far,
    d1_s,
    d1_r,
    d2_s,
    d2_r,
    p2_s,
    p2_near,
    p2_far,
    f_s,
    f_r,
):
    me_d = lax.axis_index("dom")
    me_p = lax.axis_index("pme")
    up = lax.rem(me_d + 1, N_DOM)
    down = lax.rem(me_d + N_DOM - 1, N_DOM)

    inputs = [
        pltpu.make_async_copy(source, target, in_s.at[i])
        for i, (source, target) in enumerate(
            (
                (pos_in, pos),
                (charges_in, charges),
                (counts_in, counts),
                (mols_in, mols),
                (pairs_in, pairs),
                (listed_in, listed),
                (h_in, h),
                (y_in, y),
                (yt_in, yt),
            )
        )
    ]
    for copy in inputs[:4]:
        copy.start()

    barrier = pltpu.get_barrier_semaphore()
    for other in (up, down):
        pl.semaphore_signal(barrier, inc=1, device_id=(other, me_p), device_id_type=MESH)

    def pme_at(k):
        there = me_p + k
        return jnp.where(there >= N_PME, there - N_PME, there)

    def dom_at(k):
        there = me_d + k
        return jnp.where(there >= N_DOM, there - N_DOM, there)

    def y_mate(k):
        own_y = lax.rem(me_d, RING_Y)
        return me_d - own_y + lax.rem(own_y + k, RING_Y)

    for k in range(1, N_PME):
        pl.semaphore_signal(barrier, inc=1, device_id=(me_d, pme_at(k)), device_id_type=MESH)

    for k in range(1, RING_Y):
        pl.semaphore_signal(barrier, inc=1, device_id=(y_mate(k), me_p), device_id_type=MESH)
    for k in range(1, RING_Z):
        pl.semaphore_signal(
            barrier, inc=1, device_id=(dom_at(RING_Y * k), me_p), device_id_type=MESH
        )

    for copy in inputs[4:]:
        copy.start()
    for copy in inputs[:4]:
        copy.wait()
    lane = lax.broadcasted_iota(jnp.int32, (1, 128), 1)
    for b in range(2):
        live = (lane < counts[b]).astype(f32)
        for v in range(3):
            at[1, b, v : v + 1, :] = pos[v, b : b + 1, :]
        at[1, b, 3:4, :] = charges[b : b + 1, :] * live
        at[1, b, 4:5, :] = mols[b : b + 1, :].astype(f32)
        at[1, b, 5:6, :] = live
        at[1, b, 6:8, :] = jnp.zeros((2, 128), f32)

    pl.semaphore_wait(barrier, 2 + N_PME - 1 + RING_Y - 1 + RING_Z - 1)

    to_up = pltpu.make_async_remote_copy(
        src_ref=at.at[1],
        dst_ref=at.at[0],
        send_sem=halo_s.at[0],
        recv_sem=halo_r.at[0],
        device_id=(up, me_p),
        device_id_type=MESH,
    )
    to_down = pltpu.make_async_remote_copy(
        src_ref=at.at[1],
        dst_ref=at.at[2],
        send_sem=halo_s.at[1],
        recv_sem=halo_r.at[1],
        device_id=(down, me_p),
        device_id_type=MESH,
    )
    to_up.start()
    to_down.start()
    for k in range(1, RING_Y):
        pl.semaphore_signal(column_s, inc=1, device_id=(y_mate(k), me_p), device_id_type=MESH)

    def fill(side, function, high_ref, low_ref):
        for b in range(2):
            first = LANES[side] + 128 * b
            coord = at[side, b, 2:3, :]
            charge = at[side, b, 3:4, :]
            for start, stop, wrap_z in SPANS[b]:
                cells = lax.broadcasted_iota(jnp.int32, (stop - start, 128), 0)
                delta = coord - (cells + (start + wrap_z)).astype(f32)
                high, low = split(function(delta) * charge)
                high_ref[start:stop, first : first + 128] = high
                low_ref[start:stop, first : first + 128] = low

    for refs in (wz_hi, wz_lo, dz_hi, dz_lo):
        for side in range(3):
            for b in range(2):
                first = LANES[side] + 128 * b
                refs[128 - 112 * b : 240 - 112 * b, first : first + 128] = jnp.zeros((112, 128), bf16)
    fill(1, weight, wz_hi, wz_lo)
    corner_x = (me_d * SX).astype(f32)
    corner_y = (me_p * SY).astype(f32)
    wrap = (
        jnp.where(me_d == 0, 256.0, 0.0).astype(f32),
        f32(0.0),
        jnp.where(me_d == N_DOM - 1, -256.0, 0.0).astype(f32),
    )
    cells_x = lax.broadcasted_iota(jnp.int32, (8, 256), 0).astype(f32)
    cells_y = lax.broadcasted_iota(jnp.int32, (ROWS_Y, 256), 0).astype(f32) - 3.0

    def deltas(side):
        flat_x = jnp.concatenate(
            [at[side, b, 0:1, :] - (wrap[side] + corner_x) for b in range(2)], axis=1
        )
        flat_y = jnp.concatenate([at[side, b, 1:2, :] - corner_y for b in range(2)], axis=1)
        return flat_x - cells_x, flat_y - cells_y

    def spread(sides):
        planes = []
        for side in sides:
            delta_x, delta_y = deltas(side)
            wx, wy = weight(delta_x), weight(delta_y)
            planes.append(jnp.concatenate([wx[x : x + 1] * wy for x in range(SX)], axis=0))
        span = slice(LANES[sides[0]], LANES[sides[-1]] + 256)
        loaded = (wz_hi[:, span], wz_lo[:, span])
        return product(split(jnp.concatenate(planes, axis=1)), loaded, NT)

    mesh = spread((1,))
    to_up.wait_recv()
    to_down.wait_recv()
    fill(0, weight, wz_hi, wz_lo)
    fill(2, weight, wz_hi, wz_lo)
    mesh = mesh + spread((0, 2))
    mesh = split(mesh)
    own_half = me_p // 4
    halves = (1 - own_half, own_half)

    def send_half(source, target, half, first, send, receive):
        for k in range(first, 4):
            other = 4 * half + lax.rem(me_p + k, 4)
            pltpu.make_async_remote_copy(
                src_ref=source.at[other],
                dst_ref=target.at[me_p],
                send_sem=send,
                recv_sem=receive,
                device_id=(me_d, other),
                device_id_type=MESH,
            ).start()

    def all_of(view, send, receive):
        return pltpu.make_async_remote_copy(
            src_ref=view,
            dst_ref=view,
            send_sem=send,
            recv_sem=receive,
            device_id=(up, me_p),
            device_id_type=MESH,
        )

    own_group, in_group = me_d // 16, lax.rem(me_d, 16)
    far_groups = [lax.rem(own_group + k, 4) for k in (2, 1)]
    near_groups = [lax.rem(own_group + k, 4) for k in (3, 0)]

    def send_groups(source, target, groups, send, receive):
        def one(other):
            pltpu.make_async_remote_copy(
                src_ref=source.at[other],
                dst_ref=target.at[me_d],
                send_sem=send,
                recv_sem=receive,
                device_id=(other, me_p),
                device_id_type=MESH,
            ).start()

        def body(step, carry):
            for j in range(4):
                one(16 * groups[0] + lax.rem(in_group + 4 * step + j, 16))
            return carry

        lax.fori_loop(0, 4, body, 0)
        if groups is near_groups:
            for k in range(1, 16):
                one(16 * own_group + lax.rem(in_group + k, 16))
        else:
            def last(step, carry):
                for j in range(4):
                    one(16 * groups[1] + lax.rem(in_group + 4 * step + j, 16))
                return carry

            lax.fori_loop(0, 4, last, 0)

    inputs[6].wait()
    for half in halves:
        columns_z = pl.ds(pl.multiple_of(128 * half, 128), 128)
        part = product(mesh, [h[i, :, :, columns_z].reshape(GRID, 128) for i in range(2)])
        pieces = [part[ROWS_Y * x : ROWS_Y * (x + 1)] for x in range(SX)]
        for g, piece in enumerate(swap_groups(pieces)):
            sp[4 * half + g] = piece
        if half is own_half:
            send_half(sp, rp, half, 1, p1_s, p1_near)
        else:
            send_half(sp, rp, half, 0, p1_s, p1_far)
    rp[me_p] = sp[me_p]

    for side in range(3):
        fill(side, slope, dz_hi, dz_lo)

    inputs[7].wait()
    all_of(rp.at[pl.ds(0, 3)], p1_s, p1_near).wait_recv()
    all_of(rp.at[pl.ds(0, 4)], p1_s, p1_far).wait_recv()
    received = split(rp[...].reshape(N_PME * ROWS_Y, 128))
    pl.semaphore_wait(column_s, RING_Y - 1)
    flat_sd = sd.reshape(GRID, 128)
    for groups in (far_groups, near_groups):
        rows_y = [jnp.concatenate([y[i, g] for g in groups], axis=0) for i in range(2)]
        lines = product(rows_y, received)
        pieces = [
            jnp.concatenate([lines[16 * k : 16 * k + 16], lines[64 + 16 * k : 80 + 16 * k]], axis=0)
            for k in range(4)
        ]
        for x, piece in enumerate(swap_groups(pieces)):
            for i, g in enumerate(groups):
                flat_sd[pl.ds(64 * g + x, 16, stride=4), :] = piece[16 * i : 16 * (i + 1)]
        send_groups(sd, rd, groups, d1_s, d1_r)
    rd[me_d] = sd[me_d]

    def folded(index):
        return jnp.where(index < GRID // 2, index, index - GRID).astype(f32) * (1.0 / GRID)

    freq_x = folded(lax.broadcasted_iota(jnp.int32, (GRID, 128), 0))
    freq_y = folded(me_d * 4 + lane_group((1, 128)))
    freq_z = folded(me_p * 32 + lane - 32 * lane_group((1, 128)))
    wave = freq_x * freq_x + (freq_y * freq_y + freq_z * freq_z)
    safe = jnp.where(wave > 0.0, wave, 1.0)
    lam[...] = jnp.where(
        wave > 0.0, (recip_scale / GRID**3) * jnp.exp(-(math.pi**2) * safe) / safe, 0.0
    )

    table = (h[0].reshape(GRID, GRID), h[1].reshape(GRID, GRID))
    for high_ref, low_ref in ((wz_hi, wz_lo), (dz_hi, dz_lo)):
        high, low = split(product(table, (high_ref[...], low_ref[...])))
        high_ref[...] = high
        low_ref[...] = low

    all_of(rd.at[pl.ds(0, N_DOM - 1)], d1_s, d1_r).wait_recv()
    spectrum = split(product(table, split(rd.reshape(GRID, 128)[...])) * lam[...])
    flat_sd2 = sd2.reshape(GRID, 128)
    for groups in (far_groups, near_groups):
        rows_x = [jnp.concatenate([h[i, g] for g in groups], axis=0) for i in range(2)]
        lines = product(rows_x, spectrum)
        for i, g in enumerate(groups):
            flat_sd2[pl.ds(pl.multiple_of(64 * g, 64), 64), :] = lines[64 * i : 64 * (i + 1)]
        send_groups(sd2, rd2, groups, d2_s, d2_r)
    rd2[me_d] = sd2[me_d]

    padded = jnp.concatenate([at[1, 0], at[1, 1], jnp.zeros((112, 128), f32)], axis=0)
    columns = padded.T
    inputs[4].wait()
    inputs[5].wait()
    rows = lax.broadcasted_iota(jnp.int32, (1, 48), 1)
    sublane = lax.broadcasted_iota(jnp.int32, (128, 128), 1)
    on_own = jnp.zeros((128, 128), f32)
    on_above = [[0.0] * 3, [0.0] * 3]
    for a in range(2):
        left = [columns[:, 8 * a + r : 8 * a + r + 1] for r in range(6)]
        on_left = [0.0] * 3
        for c in range(2):
            right = [at[2, c, r : r + 1, :] for r in range(6)]
            hit = (rows < listed[0]) & (pairs[0:1, :] == a) & (pairs[1:2, :] == c)
            times = jnp.sum(hit.astype(f32), axis=1, keepdims=True)
            dz = left[2] - right[2]
            if a < c:
                dz = jnp.where(dz < -128.0, dz + 256.0, dz)
            if a > c:
                dz = jnp.where(dz >= 128.0, dz - 256.0, dz)
            parts = [left[0] - (right[0] - wrap[2]), left[1] - right[1], dz]
            scalar = pair_scalar(parts, left, right) * times
            for v in range(3):
                force = scalar * parts[v]
                on_left[v] = on_left[v] + force
                on_above[c][v] = on_above[c][v] - jnp.sum(force, axis=0, keepdims=True)
        for v in range(3):
            on_own = jnp.where(
                sublane == 3 * a + v, jnp.sum(on_left[v], axis=1, keepdims=True), on_own
            )
    short[0] = on_own.T[0:8]
    short[1] = jnp.concatenate(on_above[0] + on_above[1] + [jnp.zeros((2, 128), f32)], axis=0)

    inputs[8].wait()

    all_of(rd2.at[pl.ds(0, N_DOM - 1)], d2_s, d2_r).wait_recv()
    flat_rd2 = rd2.reshape(GRID, 128)
    lines = jnp.concatenate(
        swap_groups([flat_rd2[pl.ds(x, 64, stride=4), :] for x in range(4)]), axis=0
    )
    lines = split(lines)
    for half in halves:
        part = product((yt[0, half], yt[1, half]), lines)
        for g in range(4):
            sq[4 * half + g] = part[ROWS_Y * g : ROWS_Y * (g + 1)]
        if half is own_half:
            send_half(sq, rq, half, 1, p2_s, p2_near)
        else:
            send_half(sq, rq, half, 0, p2_s, p2_far)
    rq[me_p] = sq[me_p]

    weights_x, slopes_x, weights_y, slopes_y = [], [], [], []
    for side in range(3):
        delta_x, delta_y = deltas(side)
        weights_x.append(weight(delta_x))
        slopes_x.append(slope(delta_x))
        weights_y.append(weight(delta_y))
        slopes_y.append(slope(delta_y))
    all_of(rq.at[pl.ds(0, 3)], p2_s, p2_near).wait_recv()
    near = swap_groups([rq[4 * own_half + g] for g in range(4)])
    all_of(rq.at[pl.ds(0, 4)], p2_s, p2_far).wait_recv()
    far = swap_groups([rq[4 * (1 - own_half) + g] for g in range(4)])
    lines = split(
        jnp.concatenate(
            [jnp.concatenate([near[x], far[x]], axis=1) for x in range(SX)], axis=0
        )
    )

    def arrived(ref, span):
        return jnp.concatenate(
            [ref[pl.ds(pl.multiple_of(128 * half, 128), 128), span] for half in halves[::-1]], axis=0
        )

    def force_rows(side):
        span = slice(LANES[side], LANES[side] + 256)
        base = 32 if side == 2 else 0
        spectrum = [part[base : base + (FLAT if side == 1 else 128)] for part in lines]
        along = product(spectrum, (arrived(wz_hi, span), arrived(wz_lo, span)))
        along_slope = product(spectrum, (arrived(dz_hi, span), arrived(dz_lo, span)))
        wx, dx, wy, dy = weights_x[side], slopes_x[side], weights_y[side], slopes_y[side]
        field = [0.0] * 3
        for x in ((0, 1, 2), (0, 1, 2, 3), (1, 2, 3))[side]:
            here = along[ROWS_Y * x - base : ROWS_Y * (x + 1) - base]
            there = along_slope[ROWS_Y * x - base : ROWS_Y * (x + 1) - base]
            field[0] = field[0] - dx[x : x + 1] * jnp.sum(wy * here, axis=0, keepdims=True)
            field[1] = field[1] - wx[x : x + 1] * jnp.sum(dy * here, axis=0, keepdims=True)
            field[2] = field[2] - wx[x : x + 1] * jnp.sum(wy * there, axis=0, keepdims=True)
        return jnp.concatenate(
            [field[v][:, 128 * b : 128 * (b + 1)] for b in range(2) for v in range(3)]
            + [jnp.zeros((2, 128), f32)],
            axis=0,
        )

    send_down = pltpu.make_async_remote_copy(
        src_ref=fs.at[0],
        dst_ref=fr.at[0],
        send_sem=f_s.at[0],
        recv_sem=f_r.at[0],
        device_id=(down, me_p),
        device_id_type=MESH,
    )
    send_up = pltpu.make_async_remote_copy(
        src_ref=fs.at[1],
        dst_ref=fr.at[1],
        send_sem=f_s.at[1],
        recv_sem=f_r.at[1],
        device_id=(up, me_p),
        device_id_type=MESH,
    )
    fs[0] = force_rows(0)
    send_down.start()
    fs[1] = force_rows(2) + short[1]
    send_up.start()
    total = force_rows(1) + short[0]

    to_up.wait_send()
    to_down.wait_send()
    all_of(sp.at[pl.ds(0, N_PME - 1)], p1_s, p1_near).wait_send()
    all_of(sd.at[pl.ds(0, N_DOM - 1)], d1_s, d1_r).wait_send()
    all_of(sd2.at[pl.ds(0, N_DOM - 1)], d2_s, d2_r).wait_send()
    all_of(sq.at[pl.ds(0, N_PME - 1)], p2_s, p2_near).wait_send()
    send_down.wait_recv()
    send_up.wait_recv()
    total = total + fr[0] + fr[1]
    for v in range(3):
        for b in range(2):
            out[v, b : b + 1, :] = total[3 * b + v : 3 * b + v + 1]
    send_down.wait_send()
    send_up.wait_send()


def two_parts(table):
    high = table.astype(ml_dtypes.bfloat16)
    low = (table - high.astype(np.float64)).astype(ml_dtypes.bfloat16)
    return np.stack([high, low])


def cas(first, second):
    angle = 2.0 * np.pi / GRID * (np.outer(first, second) % GRID)
    return np.cos(angle) + np.sin(angle)


def tables():
    index = np.arange(GRID)
    square = cas(index, index)
    freq = (64 * np.arange(4)[:, None, None] + np.arange(4)[:, None] + 4 * np.arange(16)).reshape(-1)
    cell = np.arange(ROWS_Y) - 3
    cells = (SY * np.arange(N_PME)[:, None] + cell[None, :]).reshape(-1)
    real = np.tile(np.arange(ROWS_Y) < SY + 6, N_PME)
    lines = cas(freq, cells % GRID) * real[None, :]
    turned = lines.reshape(4, 4, 16, -1).transpose(1, 0, 2, 3).reshape(GRID, -1).T
    return [
        two_parts(square).reshape(2, 4, 64, GRID),
        two_parts(lines).reshape(2, 4, 64, -1),
        two_parts(turned).reshape(2, 2, 4 * ROWS_Y, GRID),
    ]


def per_device(positions, charges, counts, mol_ids, pair_blocks, pair_count):
    one = pltpu.SemaphoreType.DMA
    two = pltpu.SemaphoreType.DMA((2,))
    constants = [jnp.asarray(t) for t in tables()]
    forces = pl.pallas_call(
        kernel,
        out_shape=pltpu.VMEM((3, 2, 128), f32),
        in_specs=[pl.BlockSpec(memory_space=pltpu.HBM)] * 9,
        out_specs=pl.BlockSpec(memory_space=pltpu.VMEM),
        scratch_shapes=[
            pltpu.VMEM((3, 2, 128), f32),
            pltpu.VMEM((2, 128), f32),
            pltpu.SMEM((2,), jnp.int32),
            pltpu.VMEM((2, 128), jnp.int32),
            pltpu.VMEM((2, 48), jnp.int32),
            pltpu.SMEM((1,), jnp.int32),
            pltpu.VMEM((2, 4, 64, GRID), bf16),
            pltpu.VMEM((2, 4, 64, N_PME * ROWS_Y), bf16),
            pltpu.VMEM((2, 2, 4 * ROWS_Y, GRID), bf16),
            pltpu.SemaphoreType.DMA((9,)),
            pltpu.VMEM((3, 2, 8, 128), f32),
            pltpu.VMEM((GRID, ATOMS), bf16),
            pltpu.VMEM((GRID, ATOMS), bf16),
            pltpu.VMEM((GRID, ATOMS), bf16),
            pltpu.VMEM((GRID, ATOMS), bf16),
            pltpu.VMEM((N_PME, ROWS_Y, 128), f32),
            pltpu.VMEM((N_PME, ROWS_Y, 128), f32),
            pltpu.VMEM((N_DOM, 4, 128), f32),
            pltpu.VMEM((N_DOM, 4, 128), f32),
            pltpu.VMEM((N_DOM, 4, 128), f32),
            pltpu.VMEM((N_DOM, 4, 128), f32),
            pltpu.VMEM((N_PME, ROWS_Y, 128), f32),
            pltpu.VMEM((N_PME, ROWS_Y, 128), f32),
            pltpu.VMEM((2, 8, 128), f32),
            pltpu.VMEM((2, 8, 128), f32),
            pltpu.VMEM((GRID, 128), f32),
            pltpu.VMEM((2, 8, 128), f32),
            pltpu.SemaphoreType.REGULAR,
            two,
            two,
            one,
            one,
            one,
            one,
            one,
            one,
            one,
            one,
            one,
            one,
            two,
            two,
        ],
        compiler_params=pltpu.CompilerParams(
            collective_id=0, has_side_effects=True, vmem_limit_bytes=48 * 1024 * 1024
        ),
    )(
        *(
            value if value is pair_count else pltpu.with_memory_space_constraint(value, pltpu.HBM)
            for value in (
                positions.transpose(1, 0, 2),
                charges,
                counts,
                mol_ids,
                pair_blocks.T,
                pair_count,
                *constants,
            )
        )
    )
    return forces.transpose(1, 0, 2)


def solution(mesh):
    in_specs = (
        P(("dom", "pme"), None, None),
        P(("dom", "pme"), None),
        P(("dom", "pme")),
        P(("dom", "pme"), None),
        P(("dom", "pme"), None),
        P(("dom", "pme")),
    )
    out_specs = P(("dom", "pme"), None, None)
    return jax.shard_map(
        per_device, mesh=mesh, in_specs=in_specs, out_specs=out_specs, check_vma=False
    )
```

```python
import functools
import math

import jax
import jax.numpy as jnp
import ml_dtypes
import numpy as np
from jax import lax
from jax.experimental import pallas as pl
from jax.experimental.pallas import tpu as pltpu
from jax.sharding import PartitionSpec as P

GRID = 256
N_DOM = 64
RING_Y = 4
RING_Z = 16
N_PME = 8
SX = 4
SY = 32
ROWS_Y = 40
FLAT = SX * ROWS_Y
ATOMS = 768
MESH = pl.DeviceIdType.MESH

coulomb = 8.0
sigma_six = 2.5**6
well_depth = 0.5
core_alpha = 0.5
recip_scale = 6.0
f32 = jnp.float32
bf16 = jnp.bfloat16

SPANS = (((0, 144, 0), (240, 256, -256)), ((112, 256, 0), (0, 16, 256)))

LANES = (256, 0, 512)

NN = (((1,), (0,)), ((), ()))
NT = (((1,), (1,)), ((), ()))


def split(value):
    high = value.astype(bf16)
    return high, (value - high.astype(f32)).astype(bf16)


def product(left, right, dims=NN):
    def one(a, b):
        return lax.dot_general(a, b, dims, preferred_element_type=f32)

    return one(left[0], right[0]) + (one(left[0], right[1]) + one(left[1], right[0]))


def lane_group(shape):
    return lax.shift_right_logical(lax.broadcasted_iota(jnp.int32, shape, 1), 5)


def swap_groups(pieces):
    group = lane_group((1, 128))
    out = []
    for j in range(4):
        total = pieces[j]
        for i in range(4):
            if i != j:
                total = jnp.where(group == i, pltpu.roll(pieces[i], 32 * ((i - j) % 4), 1), total)
        out.append(total)
    return out


def bumps(delta):
    away = jnp.abs(delta)
    return [jnp.maximum(top - away, 0.0) for top in (3.0, 2.0, 1.0)]


def weight(delta):
    total = 0.0
    for part, factor in zip(bumps(delta), (1.0, -6.0, 15.0)):
        square = part * part
        total = total + (factor / 120.0) * (square * square * part)
    return total


def slope(delta):
    total = 0.0
    for part, factor in zip(bumps(delta), (1.0, -6.0, 15.0)):
        square = part * part
        total = total + (factor / 24.0) * (square * square)
    return jnp.where(delta > 0.0, -total, total)


def scaled_erfc(z):
    t = 1.0 / (1.0 + 0.5 * z)
    poly = 0.17087277
    for c in (
        -0.82215223,
        1.48851587,
        -1.13520398,
        0.27886807,
        -0.18628806,
        0.09678418,
        0.37409196,
        1.00002368,
        -1.26551223,
    ):
        poly = poly * t + c
    return t * jnp.exp(poly)


def pair_scalar(parts, left, right):
    dist_sq = parts[0] * parts[0] + parts[1] * parts[1] + parts[2] * parts[2]
    soft_sq = dist_sq + 1.0
    inv = lax.rsqrt(soft_sq)
    inv_sq = inv * inv
    gauss = jnp.exp(-soft_sq)
    charge = coulomb * left[3] * right[3]
    whole = (
        charge * gauss * (scaled_erfc(soft_sq * inv) * inv + 2.0 / math.sqrt(math.pi)) * inv_sq
    )
    inv_hard = 1.0 / (core_alpha * sigma_six + dist_sq * dist_sq * dist_sq)
    ratio = sigma_six * inv_hard
    dispersion = 24.0 * well_depth * dist_sq * dist_sq * (2.0 * ratio - 1.0) * ratio * inv_hard
    other = jnp.where(left[4] == right[4], -charge * inv * inv_sq, dispersion)
    return left[5] * right[5] * (whole + other)


def kernel(
    pos_in,
    charges_in,
    counts_in,
    mols_in,
    pairs_in,
    listed_in,
    h_in,
    y_in,
    yt_in,
    out,
    pos,
    charges,
    counts,
    mols,
    pairs,
    listed,
    h,
    y,
    yt,
    in_s,
    at,
    wz_hi,
    wz_lo,
    dz_hi,
    dz_lo,
    sp,
    rp,
    sd,
    rd,
    sd2,
    rd2,
    sq,
    rq,
    fs,
    fr,
    lam,
    short,
    column_s,
    halo_s,
    halo_r,
    p1_s,
    p1_near,
    p1_far,
    d1_s,
    d1_r,
    d2_s,
    d2_r,
    p2_s,
    p2_near,
    p2_far,
    f_s,
    f_r,
):
    me_d = lax.axis_index("dom")
    me_p = lax.axis_index("pme")
    up = lax.rem(me_d + 1, N_DOM)
    down = lax.rem(me_d + N_DOM - 1, N_DOM)

    inputs = [
        pltpu.make_async_copy(source, target, in_s.at[i])
        for i, (source, target) in enumerate(
            (
                (pos_in, pos),
                (charges_in, charges),
                (counts_in, counts),
                (mols_in, mols),
                (pairs_in, pairs),
                (listed_in, listed),
                (h_in, h),
                (y_in, y),
                (yt_in, yt),
            )
        )
    ]
    for copy in inputs[:4]:
        copy.start()

    barrier = pltpu.get_barrier_semaphore()
    for other in (up, down):
        pl.semaphore_signal(barrier, inc=1, device_id=(other, me_p), device_id_type=MESH)

    def pme_at(k):
        there = me_p + k
        return jnp.where(there >= N_PME, there - N_PME, there)

    def dom_at(k):
        there = me_d + k
        return jnp.where(there >= N_DOM, there - N_DOM, there)

    def y_mate(k):
        own_y = lax.rem(me_d, RING_Y)
        return me_d - own_y + lax.rem(own_y + k, RING_Y)

    for k in range(1, N_PME):
        pl.semaphore_signal(barrier, inc=1, device_id=(me_d, pme_at(k)), device_id_type=MESH)

    for k in range(1, RING_Y):
        pl.semaphore_signal(barrier, inc=1, device_id=(y_mate(k), me_p), device_id_type=MESH)
    for k in range(1, RING_Z):
        pl.semaphore_signal(
            barrier, inc=1, device_id=(dom_at(RING_Y * k), me_p), device_id_type=MESH
        )

    for copy in inputs[4:]:
        copy.start()
    for copy in inputs[:4]:
        copy.wait()
    lane = lax.broadcasted_iota(jnp.int32, (1, 128), 1)
    for b in range(2):
        live = (lane < counts[b]).astype(f32)
        for v in range(3):
            at[1, b, v : v + 1, :] = pos[v, b : b + 1, :]
        at[1, b, 3:4, :] = charges[b : b + 1, :] * live
        at[1, b, 4:5, :] = mols[b : b + 1, :].astype(f32)
        at[1, b, 5:6, :] = live
        at[1, b, 6:8, :] = jnp.zeros((2, 128), f32)

    pl.semaphore_wait(barrier, 2 + N_PME - 1 + RING_Y - 1 + RING_Z - 1)

    to_up = pltpu.make_async_remote_copy(
        src_ref=at.at[1],
        dst_ref=at.at[0],
        send_sem=halo_s.at[0],
        recv_sem=halo_r.at[0],
        device_id=(up, me_p),
        device_id_type=MESH,
    )
    to_down = pltpu.make_async_remote_copy(
        src_ref=at.at[1],
        dst_ref=at.at[2],
        send_sem=halo_s.at[1],
        recv_sem=halo_r.at[1],
        device_id=(down, me_p),
        device_id_type=MESH,
    )
    to_up.start()
    to_down.start()
    for k in range(1, RING_Y):
        pl.semaphore_signal(column_s, inc=1, device_id=(y_mate(k), me_p), device_id_type=MESH)

    def fill(side, function, high_ref, low_ref):
        for b in range(2):
            first = LANES[side] + 128 * b
            coord = at[side, b, 2:3, :]
            charge = at[side, b, 3:4, :]
            for start, stop, wrap_z in SPANS[b]:
                cells = lax.broadcasted_iota(jnp.int32, (stop - start, 128), 0)
                delta = coord - (cells + (start + wrap_z)).astype(f32)
                high, low = split(function(delta) * charge)
                high_ref[start:stop, first : first + 128] = high
                low_ref[start:stop, first : first + 128] = low

    for refs in (wz_hi, wz_lo, dz_hi, dz_lo):
        for side in range(3):
            for b in range(2):
                first = LANES[side] + 128 * b
                refs[128 - 112 * b : 240 - 112 * b, first : first + 128] = jnp.zeros((112, 128), bf16)
    fill(1, weight, wz_hi, wz_lo)
    corner_x = (me_d * SX).astype(f32)
    corner_y = (me_p * SY).astype(f32)
    wrap = (
        jnp.where(me_d == 0, 256.0, 0.0).astype(f32),
        f32(0.0),
        jnp.where(me_d == N_DOM - 1, -256.0, 0.0).astype(f32),
    )
    cells_x = lax.broadcasted_iota(jnp.int32, (8, 256), 0).astype(f32)
    cells_y = lax.broadcasted_iota(jnp.int32, (ROWS_Y, 256), 0).astype(f32) - 3.0

    def deltas(side):
        flat_x = jnp.concatenate(
            [at[side, b, 0:1, :] - (wrap[side] + corner_x) for b in range(2)], axis=1
        )
        flat_y = jnp.concatenate([at[side, b, 1:2, :] - corner_y for b in range(2)], axis=1)
        return flat_x - cells_x, flat_y - cells_y

    def spread(sides):
        planes = []
        for side in sides:
            delta_x, delta_y = deltas(side)
            wx, wy = weight(delta_x), weight(delta_y)
            planes.append(jnp.concatenate([wx[x : x + 1] * wy for x in range(SX)], axis=0))
        span = slice(LANES[sides[0]], LANES[sides[-1]] + 256)
        loaded = (wz_hi[:, span], wz_lo[:, span])
        return product(split(jnp.concatenate(planes, axis=1)), loaded, NT)

    mesh = spread((1,))
    to_up.wait_recv()
    to_down.wait_recv()
    fill(0, weight, wz_hi, wz_lo)
    fill(2, weight, wz_hi, wz_lo)
    mesh = mesh + spread((0, 2))
    mesh = split(mesh)
    own_half = me_p // 4
    halves = (1 - own_half, own_half)

    def send_half(source, target, half, first, send, receive):
        for k in range(first, 4):
            other = 4 * half + lax.rem(me_p + k, 4)
            pltpu.make_async_remote_copy(
                src_ref=source.at[other],
                dst_ref=target.at[me_p],
                send_sem=send,
                recv_sem=receive,
                device_id=(me_d, other),
                device_id_type=MESH,
            ).start()

    def all_of(view, send, receive):
        return pltpu.make_async_remote_copy(
            src_ref=view,
            dst_ref=view,
            send_sem=send,
            recv_sem=receive,
            device_id=(up, me_p),
            device_id_type=MESH,
        )

    own_group, in_group = me_d // 16, lax.rem(me_d, 16)
    side = 1 + 2 * lax.rem(me_d // RING_Y, 2)
    far_groups = [lax.rem(own_group + k, 4) for k in (2, side)]
    near_groups = [lax.rem(own_group + k, 4) for k in (4 - side, 0)]

    def send_groups(source, target, groups, send, receive):
        def one(other):
            pltpu.make_async_remote_copy(
                src_ref=source.at[other],
                dst_ref=target.at[me_d],
                send_sem=send,
                recv_sem=receive,
                device_id=(other, me_p),
                device_id_type=MESH,
            ).start()

        def body(step, carry):
            for j in range(4):
                one(16 * groups[0] + lax.rem(in_group + 4 * step + j, 16))
            return carry

        lax.fori_loop(0, 4, body, 0)
        if groups is near_groups:
            for k in range(1, 16):
                one(16 * own_group + lax.rem(in_group + k, 16))
        else:
            def last(step, carry):
                for j in range(4):
                    one(16 * groups[1] + lax.rem(in_group + 4 * step + j, 16))
                return carry

            lax.fori_loop(0, 4, last, 0)

    inputs[6].wait()
    for half in halves:
        columns_z = pl.ds(pl.multiple_of(128 * half, 128), 128)
        part = product(mesh, [h[i, :, :, columns_z].reshape(GRID, 128) for i in range(2)])
        pieces = [part[ROWS_Y * x : ROWS_Y * (x + 1)] for x in range(SX)]
        for g, piece in enumerate(swap_groups(pieces)):
            sp[4 * half + g] = piece
        if half is own_half:
            send_half(sp, rp, half, 1, p1_s, p1_near)
        else:
            send_half(sp, rp, half, 0, p1_s, p1_far)
    rp[me_p] = sp[me_p]

    for side in range(3):
        fill(side, slope, dz_hi, dz_lo)

    inputs[7].wait()
    all_of(rp.at[pl.ds(0, 3)], p1_s, p1_near).wait_recv()
    all_of(rp.at[pl.ds(0, 4)], p1_s, p1_far).wait_recv()
    received = split(rp[...].reshape(N_PME * ROWS_Y, 128))
    pl.semaphore_wait(column_s, RING_Y - 1)
    flat_sd = sd.reshape(GRID, 128)
    for groups in (far_groups, near_groups):
        rows_y = [jnp.concatenate([y[i, g] for g in groups], axis=0) for i in range(2)]
        lines = product(rows_y, received)
        pieces = [
            jnp.concatenate([lines[16 * k : 16 * k + 16], lines[64 + 16 * k : 80 + 16 * k]], axis=0)
            for k in range(4)
        ]
        for x, piece in enumerate(swap_groups(pieces)):
            for i, g in enumerate(groups):
                flat_sd[pl.ds(64 * g + x, 16, stride=4), :] = piece[16 * i : 16 * (i + 1)]
        send_groups(sd, rd, groups, d1_s, d1_r)
    rd[me_d] = sd[me_d]

    def folded(index):
        return jnp.where(index < GRID // 2, index, index - GRID).astype(f32) * (1.0 / GRID)

    freq_x = folded(lax.broadcasted_iota(jnp.int32, (GRID, 128), 0))
    freq_y = folded(me_d * 4 + lane_group((1, 128)))
    freq_z = folded(me_p * 32 + lane - 32 * lane_group((1, 128)))
    wave = freq_x * freq_x + (freq_y * freq_y + freq_z * freq_z)
    safe = jnp.where(wave > 0.0, wave, 1.0)
    lam[...] = jnp.where(
        wave > 0.0, (recip_scale / GRID**3) * jnp.exp(-(math.pi**2) * safe) / safe, 0.0
    )

    table = (h[0].reshape(GRID, GRID), h[1].reshape(GRID, GRID))
    for high_ref, low_ref in ((wz_hi, wz_lo), (dz_hi, dz_lo)):
        high, low = split(product(table, (high_ref[...], low_ref[...])))
        high_ref[...] = high
        low_ref[...] = low

    all_of(rd.at[pl.ds(0, N_DOM - 1)], d1_s, d1_r).wait_recv()
    spectrum = split(product(table, split(rd.reshape(GRID, 128)[...])) * lam[...])
    flat_sd2 = sd2.reshape(GRID, 128)
    for groups in (far_groups, near_groups):
        rows_x = [jnp.concatenate([h[i, g] for g in groups], axis=0) for i in range(2)]
        lines = product(rows_x, spectrum)
        for i, g in enumerate(groups):
            flat_sd2[pl.ds(pl.multiple_of(64 * g, 64), 64), :] = lines[64 * i : 64 * (i + 1)]
        send_groups(sd2, rd2, groups, d2_s, d2_r)
    rd2[me_d] = sd2[me_d]

    padded = jnp.concatenate([at[1, 0], at[1, 1], jnp.zeros((112, 128), f32)], axis=0)
    columns = padded.T
    inputs[4].wait()
    inputs[5].wait()
    rows = lax.broadcasted_iota(jnp.int32, (1, 48), 1)
    sublane = lax.broadcasted_iota(jnp.int32, (128, 128), 1)
    on_own = jnp.zeros((128, 128), f32)
    on_above = [[0.0] * 3, [0.0] * 3]
    for a in range(2):
        left = [columns[:, 8 * a + r : 8 * a + r + 1] for r in range(6)]
        on_left = [0.0] * 3
        for c in range(2):
            right = [at[2, c, r : r + 1, :] for r in range(6)]
            hit = (rows < listed[0]) & (pairs[0:1, :] == a) & (pairs[1:2, :] == c)
            times = jnp.sum(hit.astype(f32), axis=1, keepdims=True)
            dz = left[2] - right[2]
            if a < c:
                dz = jnp.where(dz < -128.0, dz + 256.0, dz)
            if a > c:
                dz = jnp.where(dz >= 128.0, dz - 256.0, dz)
            parts = [left[0] - (right[0] - wrap[2]), left[1] - right[1], dz]
            scalar = pair_scalar(parts, left, right) * times
            for v in range(3):
                force = scalar * parts[v]
                on_left[v] = on_left[v] + force
                on_above[c][v] = on_above[c][v] - jnp.sum(force, axis=0, keepdims=True)
        for v in range(3):
            on_own = jnp.where(
                sublane == 3 * a + v, jnp.sum(on_left[v], axis=1, keepdims=True), on_own
            )
    short[0] = on_own.T[0:8]
    short[1] = jnp.concatenate(on_above[0] + on_above[1] + [jnp.zeros((2, 128), f32)], axis=0)

    inputs[8].wait()

    all_of(rd2.at[pl.ds(0, N_DOM - 1)], d2_s, d2_r).wait_recv()
    flat_rd2 = rd2.reshape(GRID, 128)
    lines = jnp.concatenate(
        swap_groups([flat_rd2[pl.ds(x, 64, stride=4), :] for x in range(4)]), axis=0
    )
    lines = split(lines)
    for half in halves:
        part = product((yt[0, half], yt[1, half]), lines)
        for g in range(4):
            sq[4 * half + g] = part[ROWS_Y * g : ROWS_Y * (g + 1)]
        if half is own_half:
            send_half(sq, rq, half, 1, p2_s, p2_near)
        else:
            send_half(sq, rq, half, 0, p2_s, p2_far)
    rq[me_p] = sq[me_p]

    weights_x, slopes_x, weights_y, slopes_y = [], [], [], []
    for side in range(3):
        delta_x, delta_y = deltas(side)
        weights_x.append(weight(delta_x))
        slopes_x.append(slope(delta_x))
        weights_y.append(weight(delta_y))
        slopes_y.append(slope(delta_y))
    all_of(rq.at[pl.ds(0, 3)], p2_s, p2_near).wait_recv()
    near = swap_groups([rq[4 * own_half + g] for g in range(4)])
    all_of(rq.at[pl.ds(0, 4)], p2_s, p2_far).wait_recv()
    far = swap_groups([rq[4 * (1 - own_half) + g] for g in range(4)])
    lines = split(
        jnp.concatenate(
            [jnp.concatenate([near[x], far[x]], axis=1) for x in range(SX)], axis=0
        )
    )

    def arrived(ref, span):
        return jnp.concatenate(
            [ref[pl.ds(pl.multiple_of(128 * half, 128), 128), span] for half in halves[::-1]], axis=0
        )

    def force_rows(side):
        span = slice(LANES[side], LANES[side] + 256)
        base = 32 if side == 2 else 0
        spectrum = [part[base : base + (FLAT if side == 1 else 128)] for part in lines]
        along = product(spectrum, (arrived(wz_hi, span), arrived(wz_lo, span)))
        along_slope = product(spectrum, (arrived(dz_hi, span), arrived(dz_lo, span)))
        wx, dx, wy, dy = weights_x[side], slopes_x[side], weights_y[side], slopes_y[side]
        field = [0.0] * 3
        for x in ((0, 1, 2), (0, 1, 2, 3), (1, 2, 3))[side]:
            here = along[ROWS_Y * x - base : ROWS_Y * (x + 1) - base]
            there = along_slope[ROWS_Y * x - base : ROWS_Y * (x + 1) - base]
            field[0] = field[0] - dx[x : x + 1] * jnp.sum(wy * here, axis=0, keepdims=True)
            field[1] = field[1] - wx[x : x + 1] * jnp.sum(dy * here, axis=0, keepdims=True)
            field[2] = field[2] - wx[x : x + 1] * jnp.sum(wy * there, axis=0, keepdims=True)
        return jnp.concatenate(
            [field[v][:, 128 * b : 128 * (b + 1)] for b in range(2) for v in range(3)]
            + [jnp.zeros((2, 128), f32)],
            axis=0,
        )

    send_down = pltpu.make_async_remote_copy(
        src_ref=fs.at[0],
        dst_ref=fr.at[0],
        send_sem=f_s.at[0],
        recv_sem=f_r.at[0],
        device_id=(down, me_p),
        device_id_type=MESH,
    )
    send_up = pltpu.make_async_remote_copy(
        src_ref=fs.at[1],
        dst_ref=fr.at[1],
        send_sem=f_s.at[1],
        recv_sem=f_r.at[1],
        device_id=(up, me_p),
        device_id_type=MESH,
    )
    fs[0] = force_rows(0)
    send_down.start()
    fs[1] = force_rows(2) + short[1]
    send_up.start()
    total = force_rows(1) + short[0]

    to_up.wait_send()
    to_down.wait_send()
    all_of(sp.at[pl.ds(0, N_PME - 1)], p1_s, p1_near).wait_send()
    all_of(sd.at[pl.ds(0, N_DOM - 1)], d1_s, d1_r).wait_send()
    all_of(sd2.at[pl.ds(0, N_DOM - 1)], d2_s, d2_r).wait_send()
    all_of(sq.at[pl.ds(0, N_PME - 1)], p2_s, p2_near).wait_send()
    send_down.wait_recv()
    send_up.wait_recv()
    total = total + fr[0] + fr[1]
    for v in range(3):
        for b in range(2):
            out[v, b : b + 1, :] = total[3 * b + v : 3 * b + v + 1]
    send_down.wait_send()
    send_up.wait_send()


def two_parts(table):
    high = table.astype(ml_dtypes.bfloat16)
    low = (table - high.astype(np.float64)).astype(ml_dtypes.bfloat16)
    return np.stack([high, low])


def cas(first, second):
    angle = 2.0 * np.pi / GRID * (np.outer(first, second) % GRID)
    return np.cos(angle) + np.sin(angle)


def tables():
    index = np.arange(GRID)
    square = cas(index, index)
    freq = (64 * np.arange(4)[:, None, None] + np.arange(4)[:, None] + 4 * np.arange(16)).reshape(-1)
    cell = np.arange(ROWS_Y) - 3
    cells = (SY * np.arange(N_PME)[:, None] + cell[None, :]).reshape(-1)
    real = np.tile(np.arange(ROWS_Y) < SY + 6, N_PME)
    lines = cas(freq, cells % GRID) * real[None, :]
    turned = lines.reshape(4, 4, 16, -1).transpose(1, 0, 2, 3).reshape(GRID, -1).T
    return [
        two_parts(square).reshape(2, 4, 64, GRID),
        two_parts(lines).reshape(2, 4, 64, -1),
        two_parts(turned).reshape(2, 2, 4 * ROWS_Y, GRID),
    ]


def per_device(positions, charges, counts, mol_ids, pair_blocks, pair_count):
    one = pltpu.SemaphoreType.DMA
    two = pltpu.SemaphoreType.DMA((2,))
    constants = [jnp.asarray(t) for t in tables()]
    forces = pl.pallas_call(
        kernel,
        out_shape=pltpu.VMEM((3, 2, 128), f32),
        in_specs=[pl.BlockSpec(memory_space=pltpu.HBM)] * 9,
        out_specs=pl.BlockSpec(memory_space=pltpu.VMEM),
        scratch_shapes=[
            pltpu.VMEM((3, 2, 128), f32),
            pltpu.VMEM((2, 128), f32),
            pltpu.SMEM((2,), jnp.int32),
            pltpu.VMEM((2, 128), jnp.int32),
            pltpu.VMEM((2, 48), jnp.int32),
            pltpu.SMEM((1,), jnp.int32),
            pltpu.VMEM((2, 4, 64, GRID), bf16),
            pltpu.VMEM((2, 4, 64, N_PME * ROWS_Y), bf16),
            pltpu.VMEM((2, 2, 4 * ROWS_Y, GRID), bf16),
            pltpu.SemaphoreType.DMA((9,)),
            pltpu.VMEM((3, 2, 8, 128), f32),
            pltpu.VMEM((GRID, ATOMS), bf16),
            pltpu.VMEM((GRID, ATOMS), bf16),
            pltpu.VMEM((GRID, ATOMS), bf16),
            pltpu.VMEM((GRID, ATOMS), bf16),
            pltpu.VMEM((N_PME, ROWS_Y, 128), f32),
            pltpu.VMEM((N_PME, ROWS_Y, 128), f32),
            pltpu.VMEM((N_DOM, 4, 128), f32),
            pltpu.VMEM((N_DOM, 4, 128), f32),
            pltpu.VMEM((N_DOM, 4, 128), f32),
            pltpu.VMEM((N_DOM, 4, 128), f32),
            pltpu.VMEM((N_PME, ROWS_Y, 128), f32),
            pltpu.VMEM((N_PME, ROWS_Y, 128), f32),
            pltpu.VMEM((2, 8, 128), f32),
            pltpu.VMEM((2, 8, 128), f32),
            pltpu.VMEM((GRID, 128), f32),
            pltpu.VMEM((2, 8, 128), f32),
            pltpu.SemaphoreType.REGULAR,
            two,
            two,
            one,
            one,
            one,
            one,
            one,
            one,
            one,
            one,
            one,
            one,
            two,
            two,
        ],
        compiler_params=pltpu.CompilerParams(
            collective_id=0, has_side_effects=True, vmem_limit_bytes=48 * 1024 * 1024
        ),
    )(
        *(
            value if value is pair_count else pltpu.with_memory_space_constraint(value, pltpu.HBM)
            for value in (
                positions.transpose(1, 0, 2),
                charges,
                counts,
                mol_ids,
                pair_blocks.T,
                pair_count,
                *constants,
            )
        )
    )
    return forces.transpose(1, 0, 2)


def solution(mesh):
    in_specs = (
        P(("dom", "pme"), None, None),
        P(("dom", "pme"), None),
        P(("dom", "pme")),
        P(("dom", "pme"), None),
        P(("dom", "pme"), None),
        P(("dom", "pme")),
    )
    out_specs = P(("dom", "pme"), None, None)
    return jax.shard_map(
        per_device, mesh=mesh, in_specs=in_specs, out_specs=out_specs, check_vma=False
    )
```

```python
import functools
import math

import jax
import jax.numpy as jnp
import ml_dtypes
import numpy as np
from jax import lax
from jax.experimental import pallas as pl
from jax.experimental.pallas import tpu as pltpu
from jax.sharding import PartitionSpec as P

GRID = 256
N_DOM = 64
RING_Y = 4
RING_Z = 16
N_PME = 8
SX = 4
SY = 32
ROWS_Y = 40
FLAT = SX * ROWS_Y
ATOMS = 768
MESH = pl.DeviceIdType.MESH

coulomb = 8.0
sigma_six = 2.5**6
well_depth = 0.5
core_alpha = 0.5
recip_scale = 6.0
f32 = jnp.float32
bf16 = jnp.bfloat16

SPANS = (((0, 144, 0), (240, 256, -256)), ((112, 256, 0), (0, 16, 256)))

LANES = (256, 0, 512)

NN = (((1,), (0,)), ((), ()))
NT = (((1,), (1,)), ((), ()))


def split(value):
    high = value.astype(bf16)
    return high, (value - high.astype(f32)).astype(bf16)


def product(left, right, dims=NN):
    def one(a, b):
        return lax.dot_general(a, b, dims, preferred_element_type=f32)

    return one(left[0], right[0]) + (one(left[0], right[1]) + one(left[1], right[0]))


def lane_group(shape):
    return lax.shift_right_logical(lax.broadcasted_iota(jnp.int32, shape, 1), 5)


def swap_groups(pieces):
    group = lane_group((1, 128))
    out = []
    for j in range(4):
        total = pieces[j]
        for i in range(4):
            if i != j:
                total = jnp.where(group == i, pltpu.roll(pieces[i], 32 * ((i - j) % 4), 1), total)
        out.append(total)
    return out


def bumps(delta):
    away = jnp.abs(delta)
    return [jnp.maximum(top - away, 0.0) for top in (3.0, 2.0, 1.0)]


def weight(delta):
    total = 0.0
    for part, factor in zip(bumps(delta), (1.0, -6.0, 15.0)):
        square = part * part
        total = total + (factor / 120.0) * (square * square * part)
    return total


def slope(delta):
    total = 0.0
    for part, factor in zip(bumps(delta), (1.0, -6.0, 15.0)):
        square = part * part
        total = total + (factor / 24.0) * (square * square)
    return jnp.where(delta > 0.0, -total, total)


def scaled_erfc(z):
    t = 1.0 / (1.0 + 0.5 * z)
    poly = 0.17087277
    for c in (
        -0.82215223,
        1.48851587,
        -1.13520398,
        0.27886807,
        -0.18628806,
        0.09678418,
        0.37409196,
        1.00002368,
        -1.26551223,
    ):
        poly = poly * t + c
    return t * jnp.exp(poly)


def pair_scalar(parts, left, right):
    dist_sq = parts[0] * parts[0] + parts[1] * parts[1] + parts[2] * parts[2]
    soft_sq = dist_sq + 1.0
    inv = lax.rsqrt(soft_sq)
    inv_sq = inv * inv
    gauss = jnp.exp(-soft_sq)
    charge = coulomb * left[3] * right[3]
    whole = (
        charge * gauss * (scaled_erfc(soft_sq * inv) * inv + 2.0 / math.sqrt(math.pi)) * inv_sq
    )
    inv_hard = 1.0 / (core_alpha * sigma_six + dist_sq * dist_sq * dist_sq)
    ratio = sigma_six * inv_hard
    dispersion = 24.0 * well_depth * dist_sq * dist_sq * (2.0 * ratio - 1.0) * ratio * inv_hard
    other = jnp.where(left[4] == right[4], -charge * inv * inv_sq, dispersion)
    return left[5] * right[5] * (whole + other)


def kernel(
    pos_in,
    charges_in,
    counts_in,
    mols_in,
    pairs_in,
    listed_in,
    h_in,
    y_in,
    yt_in,
    out,
    pos,
    charges,
    counts,
    mols,
    pairs,
    listed,
    h,
    y,
    yt,
    in_s,
    at,
    wz_hi,
    wz_lo,
    dz_hi,
    dz_lo,
    sp,
    rp,
    sd,
    rd,
    sd2,
    rd2,
    sq,
    rq,
    fs,
    fr,
    lam,
    short,
    column_s,
    halo_s,
    halo_r,
    p1_s,
    p1_near,
    p1_far,
    d1_s,
    d1_r,
    d2_s,
    d2_r,
    p2_s,
    p2_near,
    p2_far,
    f_s,
    f_r,
):
    me_d = lax.axis_index("dom")
    me_p = lax.axis_index("pme")
    up = lax.rem(me_d + 1, N_DOM)
    down = lax.rem(me_d + N_DOM - 1, N_DOM)

    inputs = [
        pltpu.make_async_copy(source, target, in_s.at[i])
        for i, (source, target) in enumerate(
            (
                (pos_in, pos),
                (charges_in, charges),
                (counts_in, counts),
                (mols_in, mols),
                (pairs_in, pairs),
                (listed_in, listed),
                (h_in, h),
                (y_in, y),
                (yt_in, yt),
            )
        )
    ]
    barrier = pltpu.get_barrier_semaphore()
    for other in (up, down):
        pl.semaphore_signal(barrier, inc=1, device_id=(other, me_p), device_id_type=MESH)
    for copy in inputs[:4]:
        copy.start()

    def pme_at(k):
        there = me_p + k
        return jnp.where(there >= N_PME, there - N_PME, there)

    def dom_at(k):
        there = me_d + k
        return jnp.where(there >= N_DOM, there - N_DOM, there)

    def y_mate(k):
        own_y = lax.rem(me_d, RING_Y)
        return me_d - own_y + lax.rem(own_y + k, RING_Y)

    for k in range(1, N_PME):
        pl.semaphore_signal(barrier, inc=1, device_id=(me_d, pme_at(k)), device_id_type=MESH)

    for k in range(1, RING_Y):
        pl.semaphore_signal(barrier, inc=1, device_id=(y_mate(k), me_p), device_id_type=MESH)
    for k in range(1, RING_Z):
        pl.semaphore_signal(
            barrier, inc=1, device_id=(dom_at(RING_Y * k), me_p), device_id_type=MESH
        )

    for copy in inputs[4:]:
        copy.start()
    for copy in inputs[:4]:
        copy.wait()
    lane = lax.broadcasted_iota(jnp.int32, (1, 128), 1)
    for b in range(2):
        live = (lane < counts[b]).astype(f32)
        for v in range(3):
            at[1, b, v : v + 1, :] = pos[v, b : b + 1, :]
        at[1, b, 3:4, :] = charges[b : b + 1, :] * live
        at[1, b, 4:5, :] = mols[b : b + 1, :].astype(f32)
        at[1, b, 5:6, :] = live
        at[1, b, 6:8, :] = jnp.zeros((2, 128), f32)

    pl.semaphore_wait(barrier, 2 + N_PME - 1 + RING_Y - 1 + RING_Z - 1)

    to_up = pltpu.make_async_remote_copy(
        src_ref=at.at[1],
        dst_ref=at.at[0],
        send_sem=halo_s.at[0],
        recv_sem=halo_r.at[0],
        device_id=(up, me_p),
        device_id_type=MESH,
    )
    to_down = pltpu.make_async_remote_copy(
        src_ref=at.at[1],
        dst_ref=at.at[2],
        send_sem=halo_s.at[1],
        recv_sem=halo_r.at[1],
        device_id=(down, me_p),
        device_id_type=MESH,
    )
    to_up.start()
    to_down.start()
    for k in range(1, RING_Y):
        pl.semaphore_signal(column_s, inc=1, device_id=(y_mate(k), me_p), device_id_type=MESH)

    def fill(side, function, high_ref, low_ref):
        for b in range(2):
            first = LANES[side] + 128 * b
            coord = at[side, b, 2:3, :]
            charge = at[side, b, 3:4, :]
            for start, stop, wrap_z in SPANS[b]:
                cells = lax.broadcasted_iota(jnp.int32, (stop - start, 128), 0)
                delta = coord - (cells + (start + wrap_z)).astype(f32)
                high, low = split(function(delta) * charge)
                high_ref[start:stop, first : first + 128] = high
                low_ref[start:stop, first : first + 128] = low

    for refs in (wz_hi, wz_lo, dz_hi, dz_lo):
        for side in range(3):
            for b in range(2):
                first = LANES[side] + 128 * b
                refs[128 - 112 * b : 240 - 112 * b, first : first + 128] = jnp.zeros((112, 128), bf16)
    fill(1, weight, wz_hi, wz_lo)
    corner_x = (me_d * SX).astype(f32)
    corner_y = (me_p * SY).astype(f32)
    wrap = (
        jnp.where(me_d == 0, 256.0, 0.0).astype(f32),
        f32(0.0),
        jnp.where(me_d == N_DOM - 1, -256.0, 0.0).astype(f32),
    )
    cells_x = lax.broadcasted_iota(jnp.int32, (8, 256), 0).astype(f32)
    cells_y = lax.broadcasted_iota(jnp.int32, (ROWS_Y, 256), 0).astype(f32) - 3.0

    def deltas(side):
        flat_x = jnp.concatenate(
            [at[side, b, 0:1, :] - (wrap[side] + corner_x) for b in range(2)], axis=1
        )
        flat_y = jnp.concatenate([at[side, b, 1:2, :] - corner_y for b in range(2)], axis=1)
        return flat_x - cells_x, flat_y - cells_y

    def spread(sides):
        planes = []
        for side in sides:
            delta_x, delta_y = deltas(side)
            wx, wy = weight(delta_x), weight(delta_y)
            planes.append(jnp.concatenate([wx[x : x + 1] * wy for x in range(SX)], axis=0))
        span = slice(LANES[sides[0]], LANES[sides[-1]] + 256)
        loaded = (wz_hi[:, span], wz_lo[:, span])
        return product(split(jnp.concatenate(planes, axis=1)), loaded, NT)

    mesh = spread((1,))
    to_up.wait_recv()
    to_down.wait_recv()
    fill(0, weight, wz_hi, wz_lo)
    fill(2, weight, wz_hi, wz_lo)
    mesh = mesh + spread((0, 2))
    mesh = split(mesh)
    own_half = me_p // 4
    halves = (1 - own_half, own_half)

    def send_half(source, target, half, first, send, receive):
        for k in range(first, 4):
            other = 4 * half + lax.rem(me_p + k, 4)
            pltpu.make_async_remote_copy(
                src_ref=source.at[other],
                dst_ref=target.at[me_p],
                send_sem=send,
                recv_sem=receive,
                device_id=(me_d, other),
                device_id_type=MESH,
            ).start()

    def all_of(view, send, receive):
        return pltpu.make_async_remote_copy(
            src_ref=view,
            dst_ref=view,
            send_sem=send,
            recv_sem=receive,
            device_id=(up, me_p),
            device_id_type=MESH,
        )

    own_group, in_group = me_d // 16, lax.rem(me_d, 16)
    far_groups = [lax.rem(own_group + k, 4) for k in (2, 1)]
    near_groups = [lax.rem(own_group + k, 4) for k in (3, 0)]

    def send_groups(source, target, groups, send, receive):
        def one(other):
            pltpu.make_async_remote_copy(
                src_ref=source.at[other],
                dst_ref=target.at[me_d],
                send_sem=send,
                recv_sem=receive,
                device_id=(other, me_p),
                device_id_type=MESH,
            ).start()

        def body(step, carry):
            for j in range(4):
                one(16 * groups[0] + lax.rem(in_group + 4 * step + j, 16))
            return carry

        lax.fori_loop(0, 4, body, 0)
        if groups is near_groups:
            for k in range(1, 16):
                one(16 * own_group + lax.rem(in_group + k, 16))
        else:
            def last(step, carry):
                for j in range(4):
                    one(16 * groups[1] + lax.rem(in_group + 4 * step + j, 16))
                return carry

            lax.fori_loop(0, 4, last, 0)

    inputs[6].wait()
    for half in halves:
        columns_z = pl.ds(pl.multiple_of(128 * half, 128), 128)
        part = product(mesh, [h[i, :, :, columns_z].reshape(GRID, 128) for i in range(2)])
        pieces = [part[ROWS_Y * x : ROWS_Y * (x + 1)] for x in range(SX)]
        for g, piece in enumerate(swap_groups(pieces)):
            sp[4 * half + g] = piece
        if half is own_half:
            send_half(sp, rp, half, 1, p1_s, p1_near)
        else:
            send_half(sp, rp, half, 0, p1_s, p1_far)
    rp[me_p] = sp[me_p]

    for side in range(3):
        fill(side, slope, dz_hi, dz_lo)

    inputs[7].wait()
    all_of(rp.at[pl.ds(0, 3)], p1_s, p1_near).wait_recv()
    all_of(rp.at[pl.ds(0, 4)], p1_s, p1_far).wait_recv()
    received = split(rp[...].reshape(N_PME * ROWS_Y, 128))
    pl.semaphore_wait(column_s, RING_Y - 1)
    flat_sd = sd.reshape(GRID, 128)
    for groups in (far_groups, near_groups):
        rows_y = [jnp.concatenate([y[i, g] for g in groups], axis=0) for i in range(2)]
        lines = product(rows_y, received)
        pieces = [
            jnp.concatenate([lines[16 * k : 16 * k + 16], lines[64 + 16 * k : 80 + 16 * k]], axis=0)
            for k in range(4)
        ]
        for x, piece in enumerate(swap_groups(pieces)):
            for i, g in enumerate(groups):
                flat_sd[pl.ds(64 * g + x, 16, stride=4), :] = piece[16 * i : 16 * (i + 1)]
        send_groups(sd, rd, groups, d1_s, d1_r)
    rd[me_d] = sd[me_d]

    def folded(index):
        return jnp.where(index < GRID // 2, index, index - GRID).astype(f32) * (1.0 / GRID)

    freq_x = folded(lax.broadcasted_iota(jnp.int32, (GRID, 128), 0))
    freq_y = folded(me_d * 4 + lane_group((1, 128)))
    freq_z = folded(me_p * 32 + lane - 32 * lane_group((1, 128)))
    wave = freq_x * freq_x + (freq_y * freq_y + freq_z * freq_z)
    safe = jnp.where(wave > 0.0, wave, 1.0)
    lam[...] = jnp.where(
        wave > 0.0, (recip_scale / GRID**3) * jnp.exp(-(math.pi**2) * safe) / safe, 0.0
    )

    table = (h[0].reshape(GRID, GRID), h[1].reshape(GRID, GRID))

    def transform(high_ref, low_ref):
        high, low = split(product(table, (high_ref[...], low_ref[...])))
        high_ref[...] = high
        low_ref[...] = low

    transform(wz_hi, wz_lo)

    all_of(rd.at[pl.ds(0, N_DOM - 1)], d1_s, d1_r).wait_recv()
    spectrum = split(product(table, split(rd.reshape(GRID, 128)[...])) * lam[...])
    flat_sd2 = sd2.reshape(GRID, 128)
    for groups in (far_groups, near_groups):
        rows_x = [jnp.concatenate([h[i, g] for g in groups], axis=0) for i in range(2)]
        lines = product(rows_x, spectrum)
        for i, g in enumerate(groups):
            flat_sd2[pl.ds(pl.multiple_of(64 * g, 64), 64), :] = lines[64 * i : 64 * (i + 1)]
        send_groups(sd2, rd2, groups, d2_s, d2_r)
    rd2[me_d] = sd2[me_d]

    padded = jnp.concatenate([at[1, 0], at[1, 1], jnp.zeros((112, 128), f32)], axis=0)
    columns = padded.T
    inputs[4].wait()
    inputs[5].wait()
    rows = lax.broadcasted_iota(jnp.int32, (1, 48), 1)
    sublane = lax.broadcasted_iota(jnp.int32, (128, 128), 1)
    on_own = jnp.zeros((128, 128), f32)
    on_above = [[0.0] * 3, [0.0] * 3]
    for a in range(2):
        left = [columns[:, 8 * a + r : 8 * a + r + 1] for r in range(6)]
        on_left = [0.0] * 3
        for c in range(2):
            right = [at[2, c, r : r + 1, :] for r in range(6)]
            hit = (rows < listed[0]) & (pairs[0:1, :] == a) & (pairs[1:2, :] == c)
            times = jnp.sum(hit.astype(f32), axis=1, keepdims=True)
            dz = left[2] - right[2]
            if a < c:
                dz = jnp.where(dz < -128.0, dz + 256.0, dz)
            if a > c:
                dz = jnp.where(dz >= 128.0, dz - 256.0, dz)
            parts = [left[0] - (right[0] - wrap[2]), left[1] - right[1], dz]
            scalar = pair_scalar(parts, left, right) * times
            for v in range(3):
                force = scalar * parts[v]
                on_left[v] = on_left[v] + force
                on_above[c][v] = on_above[c][v] - jnp.sum(force, axis=0, keepdims=True)
        for v in range(3):
            on_own = jnp.where(
                sublane == 3 * a + v, jnp.sum(on_left[v], axis=1, keepdims=True), on_own
            )
    short[0] = on_own.T[0:8]
    short[1] = jnp.concatenate(on_above[0] + on_above[1] + [jnp.zeros((2, 128), f32)], axis=0)

    transform(dz_hi, dz_lo)
    inputs[8].wait()

    all_of(rd2.at[pl.ds(0, N_DOM - 1)], d2_s, d2_r).wait_recv()
    flat_rd2 = rd2.reshape(GRID, 128)
    lines = jnp.concatenate(
        swap_groups([flat_rd2[pl.ds(x, 64, stride=4), :] for x in range(4)]), axis=0
    )
    lines = split(lines)
    for half in halves:
        part = product((yt[0, half], yt[1, half]), lines)
        for g in range(4):
            sq[4 * half + g] = part[ROWS_Y * g : ROWS_Y * (g + 1)]
        if half is own_half:
            send_half(sq, rq, half, 1, p2_s, p2_near)
        else:
            send_half(sq, rq, half, 0, p2_s, p2_far)
    rq[me_p] = sq[me_p]

    weights_x, slopes_x, weights_y, slopes_y = [], [], [], []
    for side in range(3):
        delta_x, delta_y = deltas(side)
        weights_x.append(weight(delta_x))
        slopes_x.append(slope(delta_x))
        weights_y.append(weight(delta_y))
        slopes_y.append(slope(delta_y))
    all_of(rq.at[pl.ds(0, 3)], p2_s, p2_near).wait_recv()
    near = swap_groups([rq[4 * own_half + g] for g in range(4)])
    all_of(rq.at[pl.ds(0, 4)], p2_s, p2_far).wait_recv()
    far = swap_groups([rq[4 * (1 - own_half) + g] for g in range(4)])
    lines = split(
        jnp.concatenate(
            [jnp.concatenate([near[x], far[x]], axis=1) for x in range(SX)], axis=0
        )
    )

    def arrived(ref, span):
        return jnp.concatenate(
            [ref[pl.ds(pl.multiple_of(128 * half, 128), 128), span] for half in halves[::-1]], axis=0
        )

    def force_rows(side):
        span = slice(LANES[side], LANES[side] + 256)
        base = 32 if side == 2 else 0
        spectrum = [part[base : base + (FLAT if side == 1 else 128)] for part in lines]
        along = product(spectrum, (arrived(wz_hi, span), arrived(wz_lo, span)))
        along_slope = product(spectrum, (arrived(dz_hi, span), arrived(dz_lo, span)))
        wx, dx, wy, dy = weights_x[side], slopes_x[side], weights_y[side], slopes_y[side]
        field = [0.0] * 3
        for x in ((0, 1, 2), (0, 1, 2, 3), (1, 2, 3))[side]:
            here = along[ROWS_Y * x - base : ROWS_Y * (x + 1) - base]
            there = along_slope[ROWS_Y * x - base : ROWS_Y * (x + 1) - base]
            field[0] = field[0] - dx[x : x + 1] * jnp.sum(wy * here, axis=0, keepdims=True)
            field[1] = field[1] - wx[x : x + 1] * jnp.sum(dy * here, axis=0, keepdims=True)
            field[2] = field[2] - wx[x : x + 1] * jnp.sum(wy * there, axis=0, keepdims=True)
        return jnp.concatenate(
            [field[v][:, 128 * b : 128 * (b + 1)] for b in range(2) for v in range(3)]
            + [jnp.zeros((2, 128), f32)],
            axis=0,
        )

    send_down = pltpu.make_async_remote_copy(
        src_ref=fs.at[0],
        dst_ref=fr.at[0],
        send_sem=f_s.at[0],
        recv_sem=f_r.at[0],
        device_id=(down, me_p),
        device_id_type=MESH,
    )
    send_up = pltpu.make_async_remote_copy(
        src_ref=fs.at[1],
        dst_ref=fr.at[1],
        send_sem=f_s.at[1],
        recv_sem=f_r.at[1],
        device_id=(up, me_p),
        device_id_type=MESH,
    )
    fs[0] = force_rows(0)
    send_down.start()
    fs[1] = force_rows(2) + short[1]
    send_up.start()
    total = force_rows(1) + short[0]

    to_up.wait_send()
    to_down.wait_send()
    all_of(sp.at[pl.ds(0, N_PME - 1)], p1_s, p1_near).wait_send()
    all_of(sd.at[pl.ds(0, N_DOM - 1)], d1_s, d1_r).wait_send()
    all_of(sd2.at[pl.ds(0, N_DOM - 1)], d2_s, d2_r).wait_send()
    all_of(sq.at[pl.ds(0, N_PME - 1)], p2_s, p2_near).wait_send()
    send_down.wait_recv()
    send_up.wait_recv()
    total = total + fr[0] + fr[1]
    for v in range(3):
        for b in range(2):
            out[v, b : b + 1, :] = total[3 * b + v : 3 * b + v + 1]
    send_down.wait_send()
    send_up.wait_send()


def two_parts(table):
    high = table.astype(ml_dtypes.bfloat16)
    low = (table - high.astype(np.float64)).astype(ml_dtypes.bfloat16)
    return np.stack([high, low])


def cas(first, second):
    angle = 2.0 * np.pi / GRID * (np.outer(first, second) % GRID)
    return np.cos(angle) + np.sin(angle)


def tables():
    index = np.arange(GRID)
    square = cas(index, index)
    freq = (64 * np.arange(4)[:, None, None] + np.arange(4)[:, None] + 4 * np.arange(16)).reshape(-1)
    cell = np.arange(ROWS_Y) - 3
    cells = (SY * np.arange(N_PME)[:, None] + cell[None, :]).reshape(-1)
    real = np.tile(np.arange(ROWS_Y) < SY + 6, N_PME)
    lines = cas(freq, cells % GRID) * real[None, :]
    turned = lines.reshape(4, 4, 16, -1).transpose(1, 0, 2, 3).reshape(GRID, -1).T
    return [
        two_parts(square).reshape(2, 4, 64, GRID),
        two_parts(lines).reshape(2, 4, 64, -1),
        two_parts(turned).reshape(2, 2, 4 * ROWS_Y, GRID),
    ]


def per_device(positions, charges, counts, mol_ids, pair_blocks, pair_count):
    one = pltpu.SemaphoreType.DMA
    two = pltpu.SemaphoreType.DMA((2,))
    constants = [jnp.asarray(t) for t in tables()]
    forces = pl.pallas_call(
        kernel,
        out_shape=pltpu.VMEM((3, 2, 128), f32),
        in_specs=[pl.BlockSpec(memory_space=pltpu.HBM)] * 9,
        out_specs=pl.BlockSpec(memory_space=pltpu.VMEM),
        scratch_shapes=[
            pltpu.VMEM((3, 2, 128), f32),
            pltpu.VMEM((2, 128), f32),
            pltpu.SMEM((2,), jnp.int32),
            pltpu.VMEM((2, 128), jnp.int32),
            pltpu.VMEM((2, 48), jnp.int32),
            pltpu.SMEM((1,), jnp.int32),
            pltpu.VMEM((2, 4, 64, GRID), bf16),
            pltpu.VMEM((2, 4, 64, N_PME * ROWS_Y), bf16),
            pltpu.VMEM((2, 2, 4 * ROWS_Y, GRID), bf16),
            pltpu.SemaphoreType.DMA((9,)),
            pltpu.VMEM((3, 2, 8, 128), f32),
            pltpu.VMEM((GRID, ATOMS), bf16),
            pltpu.VMEM((GRID, ATOMS), bf16),
            pltpu.VMEM((GRID, ATOMS), bf16),
            pltpu.VMEM((GRID, ATOMS), bf16),
            pltpu.VMEM((N_PME, ROWS_Y, 128), f32),
            pltpu.VMEM((N_PME, ROWS_Y, 128), f32),
            pltpu.VMEM((N_DOM, 4, 128), f32),
            pltpu.VMEM((N_DOM, 4, 128), f32),
            pltpu.VMEM((N_DOM, 4, 128), f32),
            pltpu.VMEM((N_DOM, 4, 128), f32),
            pltpu.VMEM((N_PME, ROWS_Y, 128), f32),
            pltpu.VMEM((N_PME, ROWS_Y, 128), f32),
            pltpu.VMEM((2, 8, 128), f32),
            pltpu.VMEM((2, 8, 128), f32),
            pltpu.VMEM((GRID, 128), f32),
            pltpu.VMEM((2, 8, 128), f32),
            pltpu.SemaphoreType.REGULAR,
            two,
            two,
            one,
            one,
            one,
            one,
            one,
            one,
            one,
            one,
            one,
            one,
            two,
            two,
        ],
        compiler_params=pltpu.CompilerParams(
            collective_id=0, has_side_effects=True, vmem_limit_bytes=48 * 1024 * 1024
        ),
    )(
        *(
            value if value is pair_count else pltpu.with_memory_space_constraint(value, pltpu.HBM)
            for value in (
                positions.transpose(1, 0, 2),
                charges,
                counts,
                mol_ids,
                pair_blocks.T,
                pair_count,
                *constants,
            )
        )
    )
    return forces.transpose(1, 0, 2)


def solution(mesh):
    in_specs = (
        P(("dom", "pme"), None, None),
        P(("dom", "pme"), None),
        P(("dom", "pme")),
        P(("dom", "pme"), None),
        P(("dom", "pme"), None),
        P(("dom", "pme")),
    )
    out_specs = P(("dom", "pme"), None, None)
    return jax.shard_map(
        per_device, mesh=mesh, in_specs=in_specs, out_specs=out_specs, check_vma=False
    )
```
